256 devices in a mesh: dp: 16 (over y, z_lo, core), space: 4 (over x), tensor: 4 (over z_hi).
Axes of the slice: x: 4, y: 4, z: 8 (z_hi: 4, z_lo: 2; z = z_hi * 2 + z_lo), core: 2. Of those that a mesh axis runs over, the one named last changes fastest.
Arguments:
- tokens: bfloat16 [16, 1024, 4096], P('dp', 'space'), may hold values from -4 to 4
- weights: bfloat16 [4096, 3, 2048], P('dp', None, 'tensor'), may hold values from -0.0625 to 0.0625
- cotangent: bfloat16 [16, 1024, 2048], P('dp', 'space', 'tensor'), may hold values from -6 to 6
Outputs:
- attended: bfloat16 [16, 1024, 2048], P('dp', 'space', 'tensor')
- token_grad: bfloat16 [16, 1024, 4096], P('dp', 'space', 'tensor')
- weight_grad: float32 [4096, 3, 2048], P('dp', None, 'tensor')
The draws below stay inside these ranges and needn't reach their ends.
All inputs are finite; a program needn't handle non-finite values.
Results may differ from the reference program's by a relative error of at most 0.039.
Values may be sent and summed in bfloat16 or wider, within the bound.
No kernel may reach another device: no remote copies, remote signals or barrier semaphores. Data moves between devices by JAX's collectives and lax.ppermute only.
A program may use at most 128 MiB of HBM per device.

```python
import math
import jax
import jax.numpy as jnp
from jax import lax

D = 4096
HEADS = 16
HS = 128
PATCHES = 1024
FRAMES_DEV = 1
FRAMES = 16
HD = 2048
N_DP = 16
N_SPACE = 4
N_TENSOR = 4


def draw_tokens(key, part):
    key = jax.random.fold_in(key, 11)
    key_main = jax.random.fold_in(key, 0)
    array_shape = (FRAMES, PATCHES, D)
    values = jax.random.normal(key_main, array_shape, jnp.float32)
    return jnp.clip(values, -4.0, 4.0).astype(jnp.bfloat16)


def draw_weights(key, part):
    key = jax.random.fold_in(key, 23)
    key_main = jax.random.fold_in(key, 0)
    clip_limit = 4.0 / math.sqrt(D)
    base_part = jax.random.normal(key_main, (D, 3, HD), jnp.float32) / math.sqrt(D)
    values = base_part
    return jnp.clip(values, -clip_limit, clip_limit).astype(jnp.bfloat16)


def block_levels(rng, shape, cuts, low, largest):
    level = 1.0
    for axis_at, shards_of in cuts:
        draws = jax.random.uniform(jax.random.fold_in(jax.random.fold_in(rng, 6), axis_at), (shards_of,), jnp.float32, low / len(cuts), largest / len(cuts))
        level = level * jnp.repeat(jnp.exp(draws), shape[axis_at] // shards_of).reshape((-1,) + (1,) * (len(shape) - 1 - axis_at))
    return level


def scatter_about(own_key, shape, scale, bound, shards=(), dtype=jnp.bfloat16):
    values = scale * jax.random.normal(own_key, shape, jnp.float32)
    if shards:
        values = values * block_levels(own_key, shape, shards, -0.22, 0.18)
    return jnp.clip(values, -bound, bound).astype(dtype)


def setup_inputs(seed: int = 0) -> dict:
    seeds = jax.random.split(jax.random.key(seed), 4)
    return {
        "tokens": draw_tokens(jax.random.fold_in(seeds[3], 71), 0),
        "weights": draw_weights(jax.random.fold_in(seeds[3], 71), 0),
        "cotangent": scatter_about(seeds[2], (FRAMES, PATCHES, HD), 1.0, 6.0, ((0, 16), (1, 4), (2, 4))),
    }


def round_bf(value):
    return lax.optimization_barrier(value.astype(jnp.bfloat16)).astype(jnp.float32)

def reference(tokens, weights, cotangent):
    score_scale = 1.0 / math.sqrt(HS)
    block_rows = PATCHES // N_SPACE
    col_block = HD // N_TENSOR
    flat_w = weights.reshape(D, 3 * HD)
    wide_w = weights.astype(jnp.float32).reshape(D, 3, N_TENSOR, col_block)

    def one_frame(pair):
        tok, cot = pair
        tok_f = tok.astype(jnp.float32)
        root_ms = jnp.sqrt(lax.optimization_barrier(jnp.mean(tok_f * tok_f, -1, keepdims=True)) + 1e-05)
        unit_rows = tok_f / root_ms
        normed = unit_rows.astype(jnp.bfloat16)
        proj = jnp.dot(normed, flat_w, preferred_element_type=jnp.float32).astype(jnp.bfloat16)
        proj = proj.reshape(PATCHES, 3, HEADS, HS).astype(jnp.float32)
        query_f, key_f, value_f = (proj[:, 0], proj[:, 1], proj[:, 2])
        scores = jnp.einsum('qhc,khc->hqk', query_f, key_f) * score_scale
        attn_prob = jax.nn.softmax(scores, axis=-1)
        prob_bf = round_bf(attn_prob)
        attended = jnp.einsum('hqk,khc->qhc', prob_bf, value_f).astype(jnp.bfloat16)
        dout = cot.astype(jnp.float32).reshape(PATCHES, HEADS, HS)
        dprob = jnp.einsum('qhc,khc->hqk', dout, value_f)
        row_dot = lax.optimization_barrier(jnp.sum(dout * attended.astype(jnp.float32), -1)).T
        dscore = round_bf(attn_prob * (dprob - row_dot[:, :, None]))
        dquery = (jnp.einsum('hqk,khc->qhc', dscore, key_f) * score_scale).astype(jnp.bfloat16)
        score_split = dscore.reshape(HEADS, N_SPACE, block_rows, PATCHES)
        prob_split = prob_bf.reshape(HEADS, N_SPACE, block_rows, PATCHES)
        query_split = query_f.reshape(N_SPACE, block_rows, HEADS, HS)
        dout_split = dout.reshape(N_SPACE, block_rows, HEADS, HS)
        dkey_parts = round_bf(jnp.einsum('hsqk,sqhc->skhc', score_split, query_split) * score_scale)
        dval_parts = round_bf(jnp.einsum('hsqk,sqhc->skhc', prob_split, dout_split))
        dkey = lax.optimization_barrier(jnp.sum(dkey_parts, 0)).astype(jnp.bfloat16)
        dvalue = lax.optimization_barrier(jnp.sum(dval_parts, 0)).astype(jnp.bfloat16)
        grads = jnp.stack([dquery, dkey, dvalue], axis=1).reshape(PATCHES, 3, HD)
        grads_split = grads.astype(jnp.float32).reshape(PATCHES, 3, N_TENSOR, col_block)
        norm_parts = round_bf(jnp.einsum('pjtc,djtc->tpd', grads_split, wide_w))
        norm_grad = lax.optimization_barrier(jnp.sum(norm_parts, 0))
        row_stat = lax.optimization_barrier(jnp.mean(norm_grad * unit_rows, -1, keepdims=True))
        token_grad = ((norm_grad - unit_rows * row_stat) / root_ms).astype(jnp.bfloat16)
        return (attended.reshape(PATCHES, HD), token_grad, normed, grads.reshape(PATCHES, 3 * HD))
    attended, token_grad, normed, grads = lax.map(one_frame, (tokens, cotangent))
    groups = N_DP * N_SPACE
    normed_groups = normed.reshape(N_DP, FRAMES_DEV, N_SPACE, block_rows, D).transpose(0, 2, 1, 3, 4).reshape(groups, FRAMES_DEV * block_rows, D)
    grad_groups = grads.reshape(N_DP, FRAMES_DEV, N_SPACE, block_rows, 3 * HD).transpose(0, 2, 1, 3, 4).reshape(groups, FRAMES_DEV * block_rows, 3 * HD)

    def add_group(total, pair):
        normed_rows, grad_rows = pair
        term = lax.dot_general(normed_rows, grad_rows, (((0,), (0,)), ((), ())), preferred_element_type=jnp.float32)
        return (total + round_bf(term), None)
    weight_grad, unused = lax.scan(add_group, jnp.zeros((D, 3 * HD), jnp.float32), (normed_groups, grad_groups))
    return (attended, token_grad, weight_grad.reshape(D, 3, HD))
```

```python
import functools
import math

import jax
import jax.numpy as jnp
from jax import lax
from jax.experimental import pallas as pl
from jax.experimental.pallas import tpu as pltpu
from jax.sharding import Mesh
from jax.sharding import PartitionSpec as P

HS = 128
BF = jnp.bfloat16
F32 = jnp.float32
VMEM_LIMIT = 48 * 1024 * 1024


def dot(a, b, ca, cb):
    return lax.dot_general(a, b, (((ca,), (cb,)), ((), ())), preferred_element_type=F32)


def attention_kernel(q_rows, qkv_ref, dout_ref, att_ref, grad_ref, dk_ref, dv_ref):
    scale = 1.0 / math.sqrt(HS)
    key = qkv_ref[:, HS : 2 * HS]
    value = qkv_ref[:, 2 * HS : 3 * HS]
    key_t = key.T
    value_t = value.T
    for i in range(qkv_ref.shape[0] // q_rows):
        rows = pl.ds(i * q_rows, q_rows)
        query = qkv_ref[rows, 0:HS]
        dout = dout_ref[rows, :]
        scores = dot(key, query, 1, 1) * (scale * math.log2(math.e))
        top = jnp.max(scores, axis=0, keepdims=True)
        expo = jnp.exp2(scores - top)
        prob = expo * (1.0 / jnp.sum(expo, axis=0, keepdims=True))
        prob_bf = prob.astype(BF)
        att = dot(value_t, prob_bf, 1, 0).T.astype(BF)
        att_ref[rows, :] = att
        row_dot = jnp.sum(
            dout.astype(F32).T * att.astype(F32).T, axis=0, keepdims=True
        )
        dprob = dot(value, dout, 1, 1)
        dscore = (prob * (dprob - row_dot)).astype(BF)
        grad_ref[rows, 0:HS] = (dot(key_t, dscore, 1, 0) * scale).T.astype(BF)
        dv = dot(prob_bf, dout, 1, 0)
        dk = dot(dscore, query, 1, 0)
        if i == 0:
            dv_ref[...] = dv
            dk_ref[...] = dk
        else:
            dv_ref[...] += dv
            dk_ref[...] += dk
    grad_ref[:, HS : 2 * HS] = (dk_ref[...] * scale).astype(BF)
    grad_ref[:, 2 * HS : 3 * HS] = dv_ref[...].astype(BF)


def attention(qkv, dout):
    n = qkv.shape[0]
    return pl.pallas_call(
        functools.partial(attention_kernel, min(256, n)),
        out_shape=(
            jax.ShapeDtypeStruct((n, HS), BF),
            jax.ShapeDtypeStruct((n, 3 * HS), BF),
        ),
        in_specs=[pl.BlockSpec(memory_space=pltpu.VMEM)] * 2,
        out_specs=(pl.BlockSpec(memory_space=pltpu.VMEM),) * 2,
        scratch_shapes=[pltpu.VMEM((n, HS), F32), pltpu.VMEM((n, HS), F32)],
        compiler_params=pltpu.CompilerParams(vmem_limit_bytes=VMEM_LIMIT),
        cost_estimate=pl.CostEstimate(
            flops=14 * n * n * HS, bytes_accessed=16 * n * HS, transcendentals=n * n
        ),
    )(qkv, dout)


def project_kernel(a_ref, w_ref, flat_ref, heads_ref, acc_ref):
    step = pl.program_id(0)
    part = jnp.dot(a_ref[...], w_ref[...], preferred_element_type=F32)

    @pl.when(step == 0)
    def _():
        acc_ref[...] = part

    @pl.when(step > 0)
    def _():
        acc_ref[...] += part

    @pl.when(step == pl.num_programs(0) - 1)
    def _():
        heads = heads_ref.shape[0]
        out = acc_ref[...].astype(BF)
        flat_ref[...] = out
        for j in range(3):
            for h in range(heads):
                at = (j * heads + h) * HS
                heads_ref[h, :, j * HS : (j + 1) * HS] = out[:, at : at + HS]


def project(normed, flat_w, heads):
    rows, depth = normed.shape
    cols = flat_w.shape[1]
    tile = 512
    return pl.pallas_call(
        project_kernel,
        grid=(depth // tile,),
        in_specs=[
            pl.BlockSpec((rows, tile), lambda i: (0, i)),
            pl.BlockSpec((tile, cols), lambda i: (i, 0)),
        ],
        out_specs=(
            pl.BlockSpec((rows, cols), lambda i: (0, 0)),
            pl.BlockSpec((heads, rows, 3 * HS), lambda i: (0, 0, 0)),
        ),
        out_shape=(
            jax.ShapeDtypeStruct((rows, cols), BF),
            jax.ShapeDtypeStruct((heads, rows, 3 * HS), BF),
        ),
        scratch_shapes=[pltpu.VMEM((rows, cols), F32)],
        compiler_params=pltpu.CompilerParams(vmem_limit_bytes=VMEM_LIMIT),
        cost_estimate=pl.CostEstimate(
            flops=2 * rows * depth * cols,
            bytes_accessed=2 * (depth * cols + rows * depth),
            transcendentals=0,
        ),
    )(normed, flat_w)


def norm_kernel(at_ref, g_ref, w_ref, out_ref):
    out_ref[...] = dot(g_ref[...], w_ref[...], 1, 1).astype(BF)


def norm_quarter(grads, flat_w, quarter, share):
    rows, cols = grads.shape
    tile = 256
    tiles = share // tile
    return pl.pallas_call(
        norm_kernel,
        grid_spec=pltpu.PrefetchScalarGridSpec(
            num_scalar_prefetch=1,
            grid=(tiles,),
            in_specs=[
                pl.BlockSpec((rows, cols), lambda i, at: (0, 0)),
                pl.BlockSpec((tile, cols), lambda i, at: (at[0] * tiles + i, 0)),
            ],
            out_specs=pl.BlockSpec((rows, tile), lambda i, at: (0, i)),
        ),
        out_shape=jax.ShapeDtypeStruct((rows, share), BF),
        compiler_params=pltpu.CompilerParams(vmem_limit_bytes=VMEM_LIMIT),
        cost_estimate=pl.CostEstimate(
            flops=2 * rows * share * cols,
            bytes_accessed=2 * (share * cols + rows * (share + cols)),
            transcendentals=0,
        ),
    )(quarter.reshape(1), grads, flat_w)


def shift(x, axis, by):
    n = lax.axis_size(axis)
    return lax.ppermute(x, axis, [(i, (i + by) % n) for i in range(n)])


def per_device(tokens, weights, cotangent):
    _, rows, width = tokens.shape
    w_rows, _, cols = weights.shape
    heads = cols // HS
    n_x = lax.axis_size("x")
    n_t = lax.axis_size("zh")
    at_core, at_x, at_t = (lax.axis_index(a) for a in ("core", "x", "zh"))
    share = width // n_t

    full_w = lax.all_gather(weights.reshape(w_rows, 3 * cols), ("y", "zl", "core"), axis=0, tiled=True)

    tokens_f = tokens[0].astype(F32)
    root_ms = jnp.sqrt(jnp.mean(tokens_f * tokens_f, -1, keepdims=True) + 1e-05)
    normed = (tokens_f / root_ms).astype(BF)

    dout = cotangent.reshape(rows, heads, HS).transpose(1, 0, 2)
    dout = lax.all_to_all(dout, "x", 0, 0, tiled=True).reshape(n_x * rows, HS)

    halves = normed.reshape(rows, width // (2 * w_rows), 2, w_rows)
    mine = lax.dynamic_index_in_dim(halves, at_core, 2, False).reshape(rows, width // 2)
    given = lax.dynamic_index_in_dim(halves, 1 - at_core, 2, False).reshape(rows, width // 2)
    theirs = shift(given, "core", 1)
    left_m, left_t = shift(mine, "x", 1), shift(theirs, "x", 1)
    right_m, right_t = shift(mine, "x", -1), shift(theirs, "x", -1)
    far_m, far_t = shift(left_m, "x", 1), shift(right_t, "x", -1)
    all_rows = jnp.concatenate([mine, left_m, right_m, far_m, theirs, left_t, right_t, far_t], 0)

    proj, by_head = project(normed, full_w, heads)
    qkv = lax.all_to_all(by_head, "x", 0, 0, tiled=True).reshape(n_x * rows, 3 * HS)
    att, head_grads = attention(qkv, dout)

    by_block = head_grads.reshape(n_x, rows, 3 * HS)
    grads = lax.all_to_all(by_block, "x", 0, 0, tiled=True)
    grads = grads.reshape(heads, rows, 3, HS).transpose(1, 2, 0, 3).reshape(rows, 3 * cols)

    stat = jnp.sum(grads.astype(F32) * proj.astype(F32), -1, keepdims=True) * (1.0 / width)
    stat = lax.psum(stat, "zh")

    far = norm_quarter(grads, full_w, (at_t + 2) % n_t, share)
    half = share // 2
    up = shift(far[:, :half], "zh", 1)
    down = shift(far[:, half:], "zh", -1)
    to_up = norm_quarter(grads, full_w, (at_t + 1) % n_t, share)
    to_down = norm_quarter(grads, full_w, (at_t + n_t - 1) % n_t, share)
    own = norm_quarter(grads, full_w, at_t, share)
    to_up = jnp.concatenate(
        [(to_up[:, :half].astype(F32) + up.astype(F32)).astype(BF), to_up[:, half:]], 1
    )
    to_down = jnp.concatenate(
        [to_down[:, :half], (to_down[:, half:].astype(F32) + down.astype(F32)).astype(BF)], 1
    )
    norm_grad = (
        own.astype(F32) + shift(to_up, "zh", 1).astype(F32) + shift(to_down, "zh", -1).astype(F32)
    )
    unit = lax.dynamic_slice_in_dim(tokens[0], at_t * share, share, 1).astype(F32) / root_ms
    token_grad = ((norm_grad - unit * stat) / root_ms).astype(BF)

    other_grads = shift(by_block, "core", 1)
    order = [at_x, (at_x + n_x - 1) % n_x, (at_x + 1) % n_x, (at_x + 2) % n_x]
    blocks = [lax.dynamic_index_in_dim(g, o, 0, False) for g in (by_block, other_grads) for o in order]
    part = dot(all_rows, jnp.concatenate(blocks, 0), 0, 0).astype(BF)
    part = lax.all_to_all(part, ("y", "zl"), 0, 0, tiled=True)
    part = jnp.sum(part.reshape(-1, w_rows, 3 * HS).astype(F32), 0).astype(BF)
    part = lax.all_to_all(jnp.broadcast_to(part, (n_x,) + part.shape), "x", 0, 0, tiled=True)
    weight_grad = part.reshape(heads, w_rows, 3, HS).transpose(1, 2, 0, 3).reshape(weights.shape)

    attended = lax.all_to_all(att.reshape(n_x, rows, HS), "x", 0, 0, tiled=True)
    attended = attended.transpose(1, 0, 2).reshape(1, rows, cols)
    return attended, token_grad[None], weight_grad.astype(F32)


def solution(mesh):
    fine = Mesh(mesh.devices.reshape(4, 2, 2, 4, 4), ("y", "zl", "core", "x", "zh"))
    dp = ("y", "zl", "core")
    return jax.shard_map(
        per_device,
        mesh=fine,
        in_specs=(P(dp, "x", None), P(dp, None, "zh"), P(dp, "x", "zh")),
        out_specs=(P(dp, "x", "zh"), P(dp, "x", "zh"), P(dp, None, "zh")),
        check_vma=False,
    )
```

```python
import functools
import math

import jax
import jax.numpy as jnp
from jax import lax
from jax.experimental import pallas as pl
from jax.experimental.pallas import tpu as pltpu
from jax.sharding import Mesh
from jax.sharding import PartitionSpec as P

HS = 128
BF = jnp.bfloat16
F32 = jnp.float32
PARAMS = pltpu.CompilerParams(vmem_limit_bytes=48 * 1024 * 1024)


def dot(a, b, ca, cb):
    return lax.dot_general(a, b, (((ca,), (cb,)), ((), ())), preferred_element_type=F32)


def cost(flops, nbytes, exps=0):
    return pl.CostEstimate(flops=flops, bytes_accessed=nbytes, transcendentals=exps)


def shape(*dims, dtype=BF):
    return jax.ShapeDtypeStruct(dims, dtype)


def unit_kernel(at_ref, tok_ref, normed_ref, root_ref, mine_ref, given_ref, *, band):
    tok = tok_ref[...].astype(F32)
    root = jnp.sqrt(jnp.mean(tok * tok, -1, keepdims=True) + 1e-05)
    normed_ref[...] = (tok / root).astype(BF)
    root_ref[...] = root
    core = at_ref[0]
    for i in range(mine_ref.shape[0] // band):
        for ref, which in ((mine_ref, core), (given_ref, 1 - core)):
            at = pl.multiple_of((2 * i + which) * band, band)
            ref[i * band : (i + 1) * band, :] = normed_ref[:, pl.ds(at, band)].T


def unit_rows(tokens, core, band):
    rows, width = tokens.shape
    tile = 128
    return pl.pallas_call(
        functools.partial(unit_kernel, band=band),
        grid_spec=pltpu.PrefetchScalarGridSpec(
            num_scalar_prefetch=1,
            grid=(rows // tile,),
            in_specs=[pl.BlockSpec((tile, width), lambda i, at: (i, 0))],
            out_specs=(
                pl.BlockSpec((tile, width), lambda i, at: (i, 0)),
                pl.BlockSpec((tile, 1), lambda i, at: (i, 0)),
                pl.BlockSpec((width // 2, tile), lambda i, at: (0, i)),
                pl.BlockSpec((width // 2, tile), lambda i, at: (0, i)),
            ),
        ),
        out_shape=(
            shape(rows, width),
            shape(rows, 1, dtype=F32),
            shape(width // 2, rows),
            shape(width // 2, rows),
        ),
        compiler_params=PARAMS,
        cost_estimate=cost(6 * rows * width, 6 * rows * width),
    )(core.reshape(1), tokens)


def project_kernel(a_ref, w_ref, heads_ref, acc_ref):
    step = pl.program_id(0)
    part = jnp.dot(a_ref[...], w_ref[...], preferred_element_type=F32)

    @pl.when(step == 0)
    def _():
        acc_ref[...] = part

    @pl.when(step > 0)
    def _():
        acc_ref[...] += part

    @pl.when(step == pl.num_programs(0) - 1)
    def _():
        heads = heads_ref.shape[0]
        for j in range(3):
            for h in range(heads):
                at = (j * heads + h) * HS
                heads_ref[h, :, j * HS : (j + 1) * HS] = acc_ref[:, at : at + HS].astype(BF)


def project(normed, flat_w, heads):
    rows, depth = normed.shape
    cols = flat_w.shape[1]
    tile = 512
    return pl.pallas_call(
        project_kernel,
        grid=(depth // tile,),
        in_specs=[
            pl.BlockSpec((rows, tile), lambda i: (0, i)),
            pl.BlockSpec((tile, cols), lambda i: (i, 0)),
        ],
        out_specs=pl.BlockSpec((heads, rows, 3 * HS), lambda i: (0, 0, 0)),
        out_shape=shape(heads, rows, 3 * HS),
        scratch_shapes=[pltpu.VMEM((rows, cols), F32)],
        compiler_params=PARAMS,
        cost_estimate=cost(2 * rows * depth * cols, 2 * (depth * cols + rows * depth)),
    )(normed, flat_w)


def attention_kernel(q_rows, qkv_ref, dout_ref, att_ref, grad_ref, dk_ref, dv_ref):
    scale = 1.0 / math.sqrt(HS)
    key = qkv_ref[:, HS : 2 * HS]
    value = qkv_ref[:, 2 * HS : 3 * HS]
    key_t = key.T
    value_t = value.T
    for i in range(qkv_ref.shape[0] // q_rows):
        rows = pl.ds(i * q_rows, q_rows)
        query = qkv_ref[rows, 0:HS]
        dout = dout_ref[rows, :]
        scores = dot(key, query, 1, 1) * (scale * math.log2(math.e))
        top = jnp.max(scores, axis=0, keepdims=True)
        expo = jnp.exp2(scores - top)
        prob = expo * (1.0 / jnp.sum(expo, axis=0, keepdims=True))
        prob_bf = prob.astype(BF)
        att = dot(value_t, prob_bf, 1, 0).T.astype(BF)
        att_ref[rows, :] = att
        row_dot = jnp.sum(
            dout.astype(F32).T * att.astype(F32).T, axis=0, keepdims=True
        )
        dprob = dot(value, dout, 1, 1)
        dscore = (prob * (dprob - row_dot)).astype(BF)
        grad_ref[rows, 0:HS] = (dot(key_t, dscore, 1, 0) * scale).T.astype(BF)
        dv = dot(prob_bf, dout, 1, 0)
        dk = dot(dscore, query, 1, 0)
        if i == 0:
            dv_ref[...] = dv
            dk_ref[...] = dk
        else:
            dv_ref[...] += dv
            dk_ref[...] += dk
    grad_ref[:, HS : 2 * HS] = (dk_ref[...] * scale).astype(BF)
    grad_ref[:, 2 * HS : 3 * HS] = dv_ref[...].astype(BF)


def attention(qkv, dout):
    n = qkv.shape[0]
    return pl.pallas_call(
        functools.partial(attention_kernel, min(256, n)),
        out_shape=(shape(n, HS), shape(n, 3 * HS)),
        in_specs=[pl.BlockSpec(memory_space=pltpu.VMEM)] * 2,
        out_specs=(pl.BlockSpec(memory_space=pltpu.VMEM),) * 2,
        scratch_shapes=[pltpu.VMEM((n, HS), F32), pltpu.VMEM((n, HS), F32)],
        compiler_params=PARAMS,
        cost_estimate=cost(14 * n * n * HS, 16 * n * HS, n * n),
    )(qkv, dout)


def norm_kernel(at_ref, g_ref, w_ref, out_ref, flat_ref):
    @pl.when(pl.program_id(0) == 0)
    def _():
        heads = g_ref.shape[0]
        for j in range(3):
            for h in range(heads):
                at = (j * heads + h) * HS
                flat_ref[:, at : at + HS] = g_ref[h, :, j * HS : (j + 1) * HS]

    out_ref[...] = dot(w_ref[...], flat_ref[...], 1, 1).astype(BF)


def norm_quarter(grads, flat_w, quarter, share):
    heads, rows, _ = grads.shape
    cols = flat_w.shape[1]
    tile = 512
    tiles = share // tile
    return pl.pallas_call(
        norm_kernel,
        grid_spec=pltpu.PrefetchScalarGridSpec(
            num_scalar_prefetch=1,
            grid=(tiles,),
            in_specs=[
                pl.BlockSpec(grads.shape, lambda i, at: (0, 0, 0)),
                pl.BlockSpec((tile, cols), lambda i, at: (at[0] * tiles + i, 0)),
            ],
            out_specs=pl.BlockSpec((tile, rows), lambda i, at: (i, 0)),
            scratch_shapes=[pltpu.VMEM((rows, cols), BF)],
        ),
        out_shape=shape(share, rows),
        compiler_params=PARAMS,
        cost_estimate=cost(2 * rows * share * cols, 2 * (share * cols + rows * (share + cols))),
    )(quarter.reshape(1), grads, flat_w)


def finish_kernel(at_ref, own_ref, a0_ref, a1_ref, b0_ref, b1_ref, tok_ref, root_ref, stat_ref, out_ref):
    half = a0_ref.shape[0]
    for i, refs in enumerate(((a0_ref, b0_ref), (a1_ref, b1_ref))):
        span = slice(i * half, (i + 1) * half)
        total = own_ref[span, :].astype(F32)
        for ref in refs:
            total += ref[...].astype(F32)
        unit = tok_ref[:, span].astype(F32) / root_ref[...]
        out_ref[:, span] = ((total.T - unit * stat_ref[...]) / root_ref[...]).astype(BF)


def finish(quarter, own, parts, tokens, root, stat):
    share, rows = own.shape
    whole = lambda a: pl.BlockSpec(a.shape, lambda i, at: (0, 0))
    return pl.pallas_call(
        finish_kernel,
        grid_spec=pltpu.PrefetchScalarGridSpec(
            num_scalar_prefetch=1,
            grid=(1,),
            in_specs=[whole(own)]
            + [whole(p) for p in parts]
            + [pl.BlockSpec((rows, share), lambda i, at: (0, at[0]))]
            + [whole(root), whole(stat)],
            out_specs=pl.BlockSpec((rows, share), lambda i, at: (0, 0)),
        ),
        out_shape=shape(rows, share),
        compiler_params=PARAMS,
        cost_estimate=cost(8 * rows * share, 10 * rows * share),
    )(quarter.reshape(1), own, *parts, tokens, root, stat)


def outer_kernel(at_ref, *refs):
    *blocks, mine_ref, other_ref, out_ref = refs
    n = mine_ref.shape[0]
    total = None
    for i, block in enumerate(blocks):
        g_ref = mine_ref if i < n else other_ref
        part = jnp.dot(block[...], g_ref[at_ref[i % n]], preferred_element_type=F32)
        total = part if total is None else total + part
    out_ref[...] = total.astype(BF)


def outer(blocks, order, mine, other):
    depth, rows = blocks[0].shape
    cols = mine.shape[2]
    tile = 256
    return pl.pallas_call(
        outer_kernel,
        grid_spec=pltpu.PrefetchScalarGridSpec(
            num_scalar_prefetch=1,
            grid=(depth // tile,),
            in_specs=[pl.BlockSpec((tile, rows), lambda i, at: (i, 0))] * len(blocks)
            + [pl.BlockSpec(mine.shape, lambda i, at: (0, 0, 0))] * 2,
            out_specs=pl.BlockSpec((tile, cols), lambda i, at: (i, 0)),
        ),
        out_shape=shape(depth, cols),
        compiler_params=PARAMS,
        cost_estimate=cost(
            2 * len(blocks) * depth * rows * cols, 2 * len(blocks) * depth * rows
        ),
    )(order, *blocks, mine, other)


def shift(x, axis, by):
    n = lax.axis_size(axis)
    return lax.ppermute(x, axis, [(i, (i + by) % n) for i in range(n)])


def per_device(tokens, weights, cotangent):
    _, rows, width = tokens.shape
    w_rows, _, cols = weights.shape
    heads = cols // HS
    n_x = lax.axis_size("x")
    n_t = lax.axis_size("zh")
    at_core, at_x, at_t = (lax.axis_index(a) for a in ("core", "x", "zh"))
    share = width // n_t
    tokens = tokens.reshape(rows, width)

    full_w = lax.all_gather(
        weights.reshape(w_rows, 3 * cols), ("y", "zl", "core"), axis=0, tiled=True
    )

    normed, root, mine, given = unit_rows(tokens, at_core, w_rows)
    theirs = shift(given, "core", 1)
    left_m, right_m = shift(mine, "x", 1), shift(mine, "x", -1)
    left_t, right_t = shift(theirs, "x", 1), shift(theirs, "x", -1)
    far_m, far_t = shift(left_m, "x", 1), shift(right_t, "x", -1)
    blocks = (mine, left_m, right_m, far_m, theirs, left_t, right_t, far_t)
    order = jnp.stack([(at_x + by) % n_x for by in (0, n_x - 1, 1, 2)])

    dout = cotangent.reshape(rows, heads, HS).transpose(1, 0, 2)
    dout = lax.all_to_all(dout, "x", 0, 0, tiled=True).reshape(n_x * rows, HS)

    proj = project(normed, full_w, heads)
    qkv = lax.all_to_all(proj, "x", 0, 0, tiled=True).reshape(n_x * rows, 3 * HS)
    att, head_grads = attention(qkv, dout)

    head_grads = head_grads.reshape(n_x, rows, 3 * HS)
    grads = lax.all_to_all(head_grads, "x", 0, 0, tiled=True)

    half = share // 2
    far = norm_quarter(grads, full_w, (at_t + 2) % n_t, share)
    up = shift(far[:half], "zh", 1)
    down = shift(far[half:], "zh", -1)
    to_up = norm_quarter(grads, full_w, (at_t + 1) % n_t, share)
    up_1 = shift(to_up[half:], "zh", 1)
    to_down = norm_quarter(grads, full_w, (at_t + n_t - 1) % n_t, share)
    down_0 = shift(to_down[:half], "zh", -1)
    own = norm_quarter(grads, full_w, at_t, share)
    stat = jnp.sum(grads.astype(F32) * proj.astype(F32), (0, 2)) * (1.0 / width)
    stat = stat + sum(shift(stat, "zh", by) for by in range(1, n_t))
    up_0 = shift((to_up[:half].astype(F32) + up.astype(F32)).astype(BF), "zh", 1)
    down_1 = shift((to_down[half:].astype(F32) + down.astype(F32)).astype(BF), "zh", -1)
    token_grad = finish(
        at_t, own, (up_0, up_1, down_0, down_1), tokens, root, stat.reshape(rows, 1)
    )

    other_grads = shift(head_grads, "core", 1)
    part = outer(blocks, order, head_grads, other_grads)
    part = lax.all_to_all(part, ("y", "zl"), 0, 0, tiled=True)
    part = jnp.sum(part.reshape(-1, w_rows, 3 * HS).astype(F32), 0).astype(BF)
    part = jnp.broadcast_to(part, (n_x,) + part.shape)
    last = jnp.concatenate([part, att.reshape(n_x, rows, HS)], 2)
    last = lax.all_to_all(last, "x", 0, 0, tiled=True)
    weight_grad = last[:, :, : 3 * HS].reshape(heads, w_rows, 3, HS).transpose(1, 2, 0, 3)
    attended = last[:, :, 3 * HS :].transpose(1, 0, 2).reshape(1, rows, cols)
    return attended, token_grad[None], weight_grad.reshape(weights.shape).astype(F32)


def solution(mesh):
    fine = Mesh(mesh.devices.reshape(4, 2, 2, 4, 4), ("y", "zl", "core", "x", "zh"))
    dp = ("y", "zl", "core")
    return jax.shard_map(
        per_device,
        mesh=fine,
        in_specs=(P(dp, "x", None), P(dp, None, "zh"), P(dp, "x", "zh")),
        out_specs=(P(dp, "x", "zh"), P(dp, "x", "zh"), P(dp, None, "zh")),
        check_vma=False,
    )
```

```python
import functools
import math

import jax
import jax.numpy as jnp
from jax import lax
from jax.experimental import pallas as pl
from jax.experimental.pallas import tpu as pltpu
from jax.sharding import Mesh
from jax.sharding import PartitionSpec as P

HS = 128
BF = jnp.bfloat16
F32 = jnp.float32
PARAMS = pltpu.CompilerParams(vmem_limit_bytes=48 * 1024 * 1024)


def dot(a, b, ca, cb):
    return lax.dot_general(a, b, (((ca,), (cb,)), ((), ())), preferred_element_type=F32)


def cost(flops, nbytes, exps=0):
    return pl.CostEstimate(flops=flops, bytes_accessed=nbytes, transcendentals=exps)


def shape(*dims, dtype=BF):
    return jax.ShapeDtypeStruct(dims, dtype)


def unit_kernel(at_ref, tok_ref, normed_ref, root_ref, mine_ref, given_ref, *, band):
    tok = tok_ref[...].astype(F32)
    root = jnp.sqrt(jnp.mean(tok * tok, -1, keepdims=True) + 1e-05)
    normed_ref[...] = (tok / root).astype(BF)
    root_ref[...] = root
    core = at_ref[0]
    for i in range(mine_ref.shape[0] // band):
        for ref, which in ((mine_ref, core), (given_ref, 1 - core)):
            at = pl.multiple_of((2 * i + which) * band, band)
            ref[i * band : (i + 1) * band, :] = normed_ref[:, pl.ds(at, band)].T


def unit_rows(tokens, core, band):
    rows, width = tokens.shape
    tile = 128
    return pl.pallas_call(
        functools.partial(unit_kernel, band=band),
        grid_spec=pltpu.PrefetchScalarGridSpec(
            num_scalar_prefetch=1,
            grid=(rows // tile,),
            in_specs=[pl.BlockSpec((tile, width), lambda i, at: (i, 0))],
            out_specs=(
                pl.BlockSpec((tile, width), lambda i, at: (i, 0)),
                pl.BlockSpec((tile, 1), lambda i, at: (i, 0)),
                pl.BlockSpec((width // 2, tile), lambda i, at: (0, i)),
                pl.BlockSpec((width // 2, tile), lambda i, at: (0, i)),
            ),
        ),
        out_shape=(
            shape(rows, width),
            shape(rows, 1, dtype=F32),
            shape(width // 2, rows),
            shape(width // 2, rows),
        ),
        compiler_params=PARAMS,
        cost_estimate=cost(6 * rows * width, 6 * rows * width),
    )(core.reshape(1), tokens)


def project_kernel(before, a_ref, w_ref, *refs):
    *_, heads_ref, acc_ref = refs
    step = pl.program_id(0)
    tiles, kinds, depth, cols = w_ref.shape
    for j in range(kinds):
        span = slice(j * cols, (j + 1) * cols)
        part = sum(
            jnp.dot(
                a_ref[:, i * depth : (i + 1) * depth],
                w_ref[i, j],
                preferred_element_type=F32,
            )
            for i in range(tiles)
        )

        @pl.when(step == 0)
        def _(span=span, part=part):
            acc_ref[:, span] = part

        @pl.when(step > 0)
        def _(span=span, part=part):
            acc_ref[:, span] += part

    @pl.when(step == pl.num_programs(0) - 1)
    def _():
        heads = heads_ref.shape[0]
        if before:
            heads_ref[:, :, :before] = refs[0][...]
        for j in range(kinds):
            for h in range(heads):
                at = (j * heads + h) * HS
                to = before + j * HS
                heads_ref[h, :, to : to + HS] = acc_ref[:, at : at + HS].astype(BF)


def project(normed, w, heads, earlier=None, after=()):
    rows, depth = normed.shape
    n, kinds, band, cols = w.shape
    tiles = 2
    before = 0 if earlier is None else earlier.shape[2]
    out = (heads, rows, before + kinds * HS)
    more = () if earlier is None else (earlier,)
    return pl.pallas_call(
        functools.partial(project_kernel, before),
        grid=(n // tiles,),
        in_specs=[
            pl.BlockSpec((rows, tiles * band), lambda i: (0, i)),
            pl.BlockSpec((tiles, kinds, band, cols), lambda i: (i, 0, 0, 0)),
        ]
        + [pl.BlockSpec(m.shape, lambda i: (0, 0, 0)) for m in more]
        + [pl.BlockSpec(memory_space=pl.ANY)] * len(after),
        out_specs=pl.BlockSpec(out, lambda i: (0, 0, 0)),
        out_shape=shape(*out),
        scratch_shapes=[pltpu.VMEM((rows, kinds * cols), F32)],
        compiler_params=PARAMS,
        cost_estimate=cost(2 * rows * w.size, 2 * (w.size + rows * depth)),
    )(normed, w, *more, *after)


def attention_kernel(q_rows, qkv_ref, dout_ref, att_ref, grad_ref, dk_ref, dv_ref):
    scale = 1.0 / math.sqrt(HS)
    key = qkv_ref[:, HS : 2 * HS]
    value = qkv_ref[:, 2 * HS : 3 * HS]
    key_t = key.T
    value_t = value.T
    for i in range(qkv_ref.shape[0] // q_rows):
        rows = pl.ds(i * q_rows, q_rows)
        query = qkv_ref[rows, 0:HS]
        dout = dout_ref[rows, :]
        scores = dot(key, query, 1, 1) * (scale * math.log2(math.e))
        top = jnp.max(scores, axis=0, keepdims=True)
        expo = jnp.exp2(scores - top)
        prob = expo * (1.0 / jnp.sum(expo, axis=0, keepdims=True))
        prob_bf = prob.astype(BF)
        att = dot(value_t, prob_bf, 1, 0).T.astype(BF)
        att_ref[rows, :] = att
        row_dot = jnp.sum(
            dout.astype(F32).T * att.astype(F32).T, axis=0, keepdims=True
        )
        dprob = dot(value, dout, 1, 1)
        dscore = (prob * (dprob - row_dot)).astype(BF)
        grad_ref[rows, 0:HS] = (dot(key_t, dscore, 1, 0) * scale).T.astype(BF)
        dv = dot(prob_bf, dout, 1, 0)
        dk = dot(dscore, query, 1, 0)
        if i == 0:
            dv_ref[...] = dv
            dk_ref[...] = dk
        else:
            dv_ref[...] += dv
            dk_ref[...] += dk
    grad_ref[:, HS : 2 * HS] = (dk_ref[...] * scale).astype(BF)
    grad_ref[:, 2 * HS : 3 * HS] = dv_ref[...].astype(BF)


def attention(qkv, dout):
    n = qkv.shape[0]
    return pl.pallas_call(
        functools.partial(attention_kernel, min(256, n)),
        out_shape=(shape(n, HS), shape(n, 3 * HS)),
        in_specs=[pl.BlockSpec(memory_space=pltpu.VMEM)] * 2,
        out_specs=(pl.BlockSpec(memory_space=pltpu.VMEM),) * 2,
        scratch_shapes=[pltpu.VMEM((n, HS), F32), pltpu.VMEM((n, HS), F32)],
        compiler_params=PARAMS,
        cost_estimate=cost(14 * n * n * HS, 16 * n * HS, n * n),
    )(qkv, dout)


def write_stat(ref, at, stat):
    ref[at:, :] = jnp.zeros((ref.shape[0] - at, ref.shape[1]), BF)
    rest = stat
    for i in range(3):
        top = rest.astype(BF)
        ref[at + i : at + i + 1, :] = top
        rest = rest - top.astype(F32)


def read_stat(ref, at):
    return sum(ref[at + i : at + i + 1, :].astype(F32) for i in range(3))


def norm_kernel(width, spots, carried, at_ref, g_ref, p_ref, qk_w, v_w, *refs):
    refs = refs[carried:]
    n_out = max(spot[0] for spot in spots) + 1
    outs, stat_ref, flat_ref = refs[:n_out], refs[n_out], refs[-1]
    step = pl.program_id(0)

    @pl.when(step == 0)
    def _():
        heads, _, _ = g_ref.shape
        for h in range(heads):
            for j in range(3):
                at = (j * heads + h) * HS
                flat_ref[:, at : at + HS] = g_ref[h, :, j * HS : (j + 1) * HS]
        total = sum(
            g_ref[h, :, j * HS : (j + 1) * HS].astype(F32)
            * p_ref[h, :, j * HS : (j + 1) * HS].astype(F32)
            for h in range(heads)
            for j in range(3)
        )
        stat = jnp.sum(total.T, axis=0, keepdims=True) * (1.0 / width)
        stat_ref[...] = stat
        for ref in outs:
            if ref.shape[0] % 128:
                write_stat(ref, ref.shape[0] - 16, stat)

    tiles, _, band, cols = qk_w.shape
    pieces = [(qk_w, 0), (qk_w, 1), (v_w, 0)]
    for i in range(tiles):
        total = sum(
            dot(ref[i, j], flat_ref[:, n * cols : (n + 1) * cols], 1, 1)
            for n, (ref, j) in enumerate(pieces)
        ).astype(BF)
        for at_step, (which, at) in enumerate(spots):

            @pl.when(step == at_step)
            def _(ref=outs[which], at=at + i * band, total=total):
                ref[at : at + band, :] = total


def norm_halves(grads, proj, w_qk, w_v, halves, spots, sizes, width, carry=()):
    heads, rows, _ = grads.shape
    n = len(spots)
    _, _, band, cols = w_qk.shape
    tiles = 2
    whole = pl.BlockSpec(grads.shape, lambda i, at: (0, 0, 0))
    w_spec = lambda w: pl.BlockSpec(
        (tiles, w.shape[1], band, cols), lambda i, at: (at[i], 0, 0, 0)
    )
    sizes = (*sizes, 1)
    return pl.pallas_call(
        functools.partial(norm_kernel, width, spots, len(carry)),
        grid_spec=pltpu.PrefetchScalarGridSpec(
            num_scalar_prefetch=1,
            grid=(n,),
            in_specs=[whole, whole, w_spec(w_qk), w_spec(w_v)]
            + [pl.BlockSpec(memory_space=pl.ANY)] * len(carry),
            out_specs=tuple(pl.BlockSpec((s, rows), lambda i, at: (0, 0)) for s in sizes)
            + (pl.BlockSpec(memory_space=pl.ANY),) * len(carry),
            scratch_shapes=[pltpu.VMEM((rows, 3 * cols), BF)],
        ),
        out_shape=tuple(shape(s, rows) for s in sizes[:-1])
        + (shape(1, rows, dtype=F32),)
        + tuple(shape(*c.shape) for c in carry),
        input_output_aliases={5 + i: len(sizes) + i for i in range(len(carry))},
        compiler_params=PARAMS,
        cost_estimate=cost(1, 1),
    )(halves, grads, proj, w_qk, w_v, *carry)


def add_kernel(up_part, up_in, down_part, down_in, stat_ref, after_ref, up_out, down_out):
    half = up_part.shape[0]
    for part, came, out in ((up_part, up_in, up_out), (down_part, down_in, down_out)):
        out[:half, :] = (part[...].astype(F32) + came[:half, :].astype(F32)).astype(BF)
    at = up_in.shape[0] - 16
    write_stat(up_out, half, stat_ref[...] + read_stat(up_in, at))
    write_stat(down_out, half, stat_ref[...])


def add_messages(up_part, up_in, down_part, down_in, stat, after):
    half, rows = up_part.shape
    vmem = pl.BlockSpec(memory_space=pltpu.VMEM)
    return pl.pallas_call(
        add_kernel,
        out_shape=(shape(half + 16, rows),) * 2,
        in_specs=[vmem] * 5 + [pl.BlockSpec(memory_space=pl.ANY)],
        out_specs=(vmem, vmem),
        compiler_params=PARAMS,
        cost_estimate=cost(2 * half * rows, 12 * half * rows),
    )(up_part, up_in, down_part, down_in, stat, after)


def finish_kernel(at_ref, own0, own1, up0, up1, down0, down1, tok_ref, root_ref, stat_ref, out_ref):
    half = own0.shape[0]
    stat = stat_ref[...] + read_stat(up0, half) + read_stat(down1, half)
    stat = jnp.broadcast_to(stat, (HS, stat.shape[1])).T[:, 0:1]
    root = root_ref[...]
    parts = (
        (own0[...], up0[:half, :], down0[half : 2 * half, :]),
        (own1[...], up1[half : 2 * half, :], down1[:half, :]),
    )
    for i, part in enumerate(parts):
        span = slice(i * half, (i + 1) * half)
        total = sum(p.astype(F32) for p in part)
        unit = tok_ref[:, span].astype(F32) / root
        out_ref[:, span] = ((total.T - unit * stat) / root).astype(BF)


def finish(quarter, parts, tokens, root, stat):
    half, rows = parts[0].shape
    share = 2 * half
    whole = lambda a: pl.BlockSpec(a.shape, lambda i, at: (0, 0))
    return pl.pallas_call(
        finish_kernel,
        grid_spec=pltpu.PrefetchScalarGridSpec(
            num_scalar_prefetch=1,
            grid=(1,),
            in_specs=[whole(p) for p in parts]
            + [pl.BlockSpec((rows, share), lambda i, at: (0, at[0]))]
            + [whole(root), whole(stat)],
            out_specs=pl.BlockSpec((rows, share), lambda i, at: (0, 0)),
        ),
        out_shape=shape(rows, share),
        compiler_params=PARAMS,
        cost_estimate=cost(8 * rows * share, 10 * rows * share),
    )(quarter.reshape(1), *parts, tokens, root, stat)


def outer_kernel(at_ref, *refs):
    *blocks, mine_ref, other_ref, out_ref = refs
    n = mine_ref.shape[0]
    total = None
    for i, block in enumerate(blocks):
        g_ref = mine_ref if i < n else other_ref
        part = jnp.dot(block[...], g_ref[at_ref[i % n]], preferred_element_type=F32)
        total = part if total is None else total + part
    out_ref[...] = total.astype(BF)


def outer(blocks, order, mine, other):
    depth, rows = blocks[0].shape
    cols = mine.shape[2]
    tile = 1024
    return pl.pallas_call(
        outer_kernel,
        grid_spec=pltpu.PrefetchScalarGridSpec(
            num_scalar_prefetch=1,
            grid=(depth // tile,),
            in_specs=[pl.BlockSpec((tile, rows), lambda i, at: (i, 0))] * len(blocks)
            + [pl.BlockSpec(mine.shape, lambda i, at: (0, 0, 0))] * 2,
            out_specs=pl.BlockSpec((tile, cols), lambda i, at: (i, 0)),
        ),
        out_shape=shape(depth, cols),
        compiler_params=PARAMS,
        cost_estimate=cost(1, 1),
    )(order, *blocks, mine, other)


def merge_kernel(part_ref, att_ref, after_ref, out_ref):
    total = sum(part_ref[i].astype(F32) for i in range(part_ref.shape[0])).astype(BF)
    cols = total.shape[1]
    for i in range(out_ref.shape[0]):
        out_ref[i, :, :cols] = total
        out_ref[i, :, cols:] = att_ref[i]


def merge(part, att, after):
    _, rows, cols = part.shape
    n, _, more = att.shape
    vmem = pl.BlockSpec(memory_space=pltpu.VMEM)
    return pl.pallas_call(
        merge_kernel,
        out_shape=shape(n, rows, cols + more),
        in_specs=[vmem, vmem, pl.BlockSpec(memory_space=pl.ANY)],
        out_specs=vmem,
        compiler_params=PARAMS,
        cost_estimate=cost(1, 1),
    )(part, att, after)


def unpack_kernel(in_ref, w_ref, att_ref):
    for h in range(in_ref.shape[0]):
        span = slice(h * HS, (h + 1) * HS)
        for j in range(3):
            w_ref[j, :, span] = in_ref[h, :, j * HS : (j + 1) * HS].astype(F32)
        att_ref[:, span] = in_ref[h, :, 3 * HS :]


def unpack(last):
    heads, rows, _ = last.shape
    return pl.pallas_call(
        unpack_kernel,
        out_shape=(shape(3, rows, heads * HS, dtype=F32), shape(rows, heads * HS)),
        compiler_params=PARAMS,
        cost_estimate=cost(last.size, 6 * last.size),
    )(last)


def shift(x, axis, by):
    n = lax.axis_size(axis)
    return lax.ppermute(x, axis, [(i, (i + by) % n) for i in range(n)])


def per_device(tokens, weights, cotangent):
    _, rows, width = tokens.shape
    w_rows, _, cols = weights.shape
    heads = cols // HS
    n_x = lax.axis_size("x")
    n_t = lax.axis_size("zh")
    at_core, at_x, at_t = (lax.axis_index(a) for a in ("core", "x", "zh"))
    share = width // n_t
    tokens = tokens.reshape(rows, width)

    w_kinds = weights.transpose(1, 0, 2)[None]
    gather = lambda w: lax.all_gather(w, ("y", "zl", "core"), axis=0, tiled=True)
    w_qk = gather(w_kinds[:, :2])
    w_v = gather(w_kinds[:, 2:])

    normed, root, mine, given = unit_rows(tokens, at_core, w_rows)
    theirs = shift(given, "core", 1)
    left_m, right_m = shift(mine, "x", 1), shift(mine, "x", -1)
    left_t, right_t = shift(theirs, "x", 1), shift(theirs, "x", -1)
    far_m, far_t = shift(left_m, "x", 1), shift(right_t, "x", -1)
    blocks = (mine, left_m, right_m, far_m, theirs, left_t, right_t, far_t)
    order = jnp.stack([(at_x + by) % n_x for by in (0, n_x - 1, 1, 2)])

    dout = cotangent.reshape(rows, heads, HS).transpose(1, 0, 2)
    dout = lax.all_to_all(dout, "x", 0, 0, tiled=True).reshape(n_x * rows, HS)

    proj = project(normed, w_qk, heads)
    proj = project(normed, w_v, heads, proj, blocks)
    qkv = lax.all_to_all(proj, "x", 0, 0, tiled=True).reshape(n_x * rows, 3 * HS)
    att, head_grads = attention(qkv, dout)

    head_grads = head_grads.reshape(n_x, rows, 3 * HS)
    grads = lax.all_to_all(head_grads, "x", 0, 0, tiled=True)

    half = share // 2
    norm = lambda at, spots, sizes, carry=(): norm_halves(
        grads, proj, w_qk, w_v, jnp.stack(at), spots, sizes, width, carry
    )
    here, above, far, below = (2 * ((at_t + by) % n_t) for by in range(n_t))
    part = outer(blocks, order, head_grads, shift(head_grads, "core", 1))
    up, down, stat, part = norm(
        [far, above + 1, far + 1, below],
        ((0, 0), (0, half), (1, 0), (1, half)),
        (share + 16, share),
        (part,),
    )
    up, down = shift(up, "zh", 1), shift(down, "zh", -1)
    part = lax.all_to_all(part, ("y", "zl"), 0, 0, tiled=True)
    up_part, down_part, own0, own1, _ = norm(
        [above, below + 1, here, here + 1], ((0, 0), (1, 0), (2, 0), (3, 0)), (half,) * 4
    )
    last = merge(part.reshape(-1, w_rows, 3 * HS), att.reshape(n_x, rows, HS), own0)
    up_2, down_2 = add_messages(up_part, up, down_part, down, stat, last)
    up_2, down_2 = shift(up_2, "zh", 1), shift(down_2, "zh", -1)
    last = lax.all_to_all(last, "x", 0, 0, tiled=True)
    token_grad = finish(at_t, (own0, own1, up_2, up, down, down_2), tokens, root, stat)
    weight_grad, attended = unpack(last)
    return attended[None], token_grad[None], weight_grad.transpose(1, 0, 2)


def solution(mesh):
    fine = Mesh(mesh.devices.reshape(4, 2, 2, 4, 4), ("y", "zl", "core", "x", "zh"))
    dp = ("y", "zl", "core")
    return jax.shard_map(
        per_device,
        mesh=fine,
        in_specs=(P(dp, "x", None), P(dp, None, "zh"), P(dp, "x", "zh")),
        out_specs=(P(dp, "x", "zh"), P(dp, "x", "zh"), P(dp, None, "zh")),
        check_vma=False,
    )
```

```python
import functools
import math

import jax
import jax.numpy as jnp
from jax import lax
from jax.experimental import pallas as pl
from jax.experimental.pallas import tpu as pltpu
from jax.sharding import Mesh
from jax.sharding import PartitionSpec as P

HS = 128
BF = jnp.bfloat16
F32 = jnp.float32
PARAMS = pltpu.CompilerParams(vmem_limit_bytes=62 * 1024 * 1024)


def dot(a, b, ca, cb):
    return lax.dot_general(a, b, (((ca,), (cb,)), ((), ())), preferred_element_type=F32)


def cost(flops, nbytes, exps=0):
    return pl.CostEstimate(flops=flops, bytes_accessed=nbytes, transcendentals=exps)


def shape(*dims, dtype=BF):
    return jax.ShapeDtypeStruct(dims, dtype)


def unit_kernel(at_ref, tok_ref, normed_ref, root_ref, mine_ref, given_ref, *, band):
    tok = tok_ref[...].astype(F32)
    root = jnp.sqrt(jnp.mean(tok * tok, -1, keepdims=True) + 1e-05)
    normed_ref[...] = (tok / root).astype(BF)
    root_ref[...] = root
    core = at_ref[0]
    for i in range(mine_ref.shape[0] // band):
        for ref, which in ((mine_ref, core), (given_ref, 1 - core)):
            at = pl.multiple_of((2 * i + which) * band, band)
            ref[i * band : (i + 1) * band, :] = normed_ref[:, pl.ds(at, band)].T


def unit_rows(tokens, core, band):
    rows, width = tokens.shape
    tile = 128
    return pl.pallas_call(
        functools.partial(unit_kernel, band=band),
        grid_spec=pltpu.PrefetchScalarGridSpec(
            num_scalar_prefetch=1,
            grid=(rows // tile,),
            in_specs=[pl.BlockSpec((tile, width), lambda i, at: (i, 0))],
            out_specs=(
                pl.BlockSpec((tile, width), lambda i, at: (i, 0)),
                pl.BlockSpec((tile, 1), lambda i, at: (i, 0)),
                pl.BlockSpec((width // 2, tile), lambda i, at: (0, i)),
                pl.BlockSpec((width // 2, tile), lambda i, at: (0, i)),
            ),
        ),
        out_shape=(
            shape(rows, width),
            shape(rows, 1, dtype=F32),
            shape(width // 2, rows),
            shape(width // 2, rows),
        ),
        compiler_params=PARAMS,
        cost_estimate=cost(6 * rows * width, 6 * rows * width),
    )(core.reshape(1), tokens)


def project_kernel(spots, first, last, at_ref, a_ref, *refs):
    out_ref = refs[-1] if not last else refs[-2]
    acc_ref = refs[-1]
    shards = refs[0 if first else 1 :]
    for j in range(3):
        total = None
        for n, pieces in enumerate(spots):
            which, at = pieces[j]
            depth, cols = shards[which].shape[-2:]
            band = a_ref[:, pl.ds(pl.multiple_of(at_ref[n] * depth, depth), depth)]
            part = jnp.dot(band, shards[which][at], preferred_element_type=F32)
            total = part if total is None else total + part
        span = slice(j * cols, (j + 1) * cols)
        if not first:
            total += refs[0][:, span]
        if not last:
            acc_ref[:, span] = total
        else:
            for h in range(out_ref.shape[0]):
                out_ref[h, :, j * HS : (j + 1) * HS] = total[:, h * HS : (h + 1) * HS].astype(BF)


def project(normed, bands, shards, spots, earlier=None, heads=None, after=()):
    rows, depth = normed.shape
    cols = 3 * shards[0].shape[-1]
    first, last = earlier is None, heads is not None
    more = () if first else (earlier,)
    vmem = pl.BlockSpec(memory_space=pltpu.VMEM)

    def kernel(at_ref, a_ref, *refs):
        n = len(more) + len(shards)
        refs = refs[:n] + refs[n + len(after) :]
        project_kernel(spots, first, last, at_ref, a_ref, *refs, *refs[-1:] * last)

    return pl.pallas_call(
        kernel,
        in_specs=[pl.BlockSpec(memory_space=pltpu.SMEM)]
        + [vmem] * (1 + len(more) + len(shards))
        + [pl.BlockSpec(memory_space=pl.ANY)] * len(after),
        out_specs=vmem,
        out_shape=shape(heads, rows, cols // heads) if last else shape(rows, cols, dtype=F32),
        compiler_params=PARAMS,
        cost_estimate=cost(
            2 * rows * sum(w.size for w in shards), 2 * sum(w.size for w in shards)
        ),
    )(jnp.stack(bands), normed, *more, *shards, *after)


def attention_kernel(q_rows, qkv_ref, dout_ref, *refs):
    att_ref, grad_ref, dk_ref, dv_ref = refs[-4:]
    scale = 1.0 / math.sqrt(HS)
    key = qkv_ref[:, HS : 2 * HS]
    value = qkv_ref[:, 2 * HS : 3 * HS]
    key_t = key.T
    value_t = value.T
    for i in range(qkv_ref.shape[0] // q_rows):
        rows = pl.ds(i * q_rows, q_rows)
        query = qkv_ref[rows, 0:HS]
        dout = dout_ref[rows, :]
        scores = dot(key, query, 1, 1) * (scale * math.log2(math.e))
        top = jnp.max(scores, axis=0, keepdims=True)
        expo = jnp.exp2(scores - top)
        prob = expo * (1.0 / jnp.sum(expo, axis=0, keepdims=True))
        prob_bf = prob.astype(BF)
        att = dot(value_t, prob_bf, 1, 0).T.astype(BF)
        att_ref[rows, :] = att
        row_dot = jnp.sum(
            dout.astype(F32).T * att.astype(F32).T, axis=0, keepdims=True
        )
        dprob = dot(value, dout, 1, 1)
        dscore = (prob * (dprob - row_dot)).astype(BF)
        grad_ref[rows, 0:HS] = (dot(key_t, dscore, 1, 0) * scale).T.astype(BF)
        dv = dot(prob_bf, dout, 1, 0)
        dk = dot(dscore, query, 1, 0)
        if i == 0:
            dv_ref[...] = dv
            dk_ref[...] = dk
        else:
            dv_ref[...] += dv
            dk_ref[...] += dk
    grad_ref[:, HS : 2 * HS] = (dk_ref[...] * scale).astype(BF)
    grad_ref[:, 2 * HS : 3 * HS] = dv_ref[...].astype(BF)


def attention(qkv, dout, after):
    n = qkv.shape[0]
    return pl.pallas_call(
        functools.partial(attention_kernel, min(256, n)),
        out_shape=(shape(n, HS), shape(n, 3 * HS)),
        in_specs=[pl.BlockSpec(memory_space=pltpu.VMEM)] * 2
        + [pl.BlockSpec(memory_space=pl.ANY)] * len(after),
        out_specs=(pl.BlockSpec(memory_space=pltpu.VMEM),) * 2,
        scratch_shapes=[pltpu.VMEM((n, HS), F32), pltpu.VMEM((n, HS), F32)],
        compiler_params=PARAMS,
        cost_estimate=cost(1, 1),
    )(qkv, dout, *after)


def write_stat(ref, at, stat):
    ref[at:, :] = jnp.zeros((ref.shape[0] - at, ref.shape[1]), BF)
    rest = stat
    for i in range(3):
        top = rest.astype(BF)
        ref[at + i : at + i + 1, :] = top
        rest = rest - top.astype(F32)


def read_stat(ref, at):
    return sum(ref[at + i : at + i + 1, :].astype(F32) for i in range(3))


def norm_kernel(width, spots, places, n_in, carried, at_ref, core_ref, g_ref, p_ref, *refs):
    shards, refs = refs[:n_in], refs[n_in + carried :]
    n_out = max(spot[0] for spot in spots) + 1
    outs, stat_ref = refs[:n_out], refs[n_out]
    w_ref, flat_ref, sems = refs[-3:]
    _, _, depth, cols = w_ref.shape
    band = depth // 2

    def copy(step, core, j, source):
        to = jnp.where(core == 0, core_ref[0], 1 - core_ref[0])
        at = pl.ds(pl.multiple_of(to * band, band), band)
        return pltpu.make_async_copy(source, w_ref.at[step, j, at], sems.at[step, core, j])

    for step in range(len(spots)):
        for place, cores in enumerate(places):

            @pl.when(at_ref[step] == place)
            def _(step=step, cores=cores):
                for core, pieces in enumerate(cores):
                    for j, (which, at) in enumerate(pieces):
                        copy(step, core, j, shards[which].at[at]).start()

    heads, _, _ = g_ref.shape
    for h in range(heads):
        for j in range(3):
            at = (j * heads + h) * HS
            flat_ref[:, at : at + HS] = g_ref[h, :, j * HS : (j + 1) * HS]
    total = sum(
        g_ref[h, :, j * HS : (j + 1) * HS].astype(F32)
        * p_ref[h, :, j * HS : (j + 1) * HS].astype(F32)
        for h in range(heads)
        for j in range(3)
    )
    stat = jnp.sum(total.T, axis=0, keepdims=True) * (1.0 / width)
    stat_ref[...] = stat
    for ref in outs:
        if ref.shape[0] % 128:
            write_stat(ref, ref.shape[0] - 16, stat)

    for step, (which, at) in enumerate(spots):
        for core in range(2):
            for j in range(3):
                copy(step, core, j, shards[0].at[0]).wait()
        total = sum(
            dot(w_ref[step, j], flat_ref[:, j * cols : (j + 1) * cols], 1, 1) for j in range(3)
        )
        outs[which][at : at + depth, :] = total.astype(BF)


def norm_halves(grads, proj, shards, places, halves, core, spots, sizes, width, carry=()):
    heads, rows, _ = grads.shape
    band, cols = shards[0].shape[-2:]
    n = len(spots)
    sizes = (*sizes, 1)
    vmem = pl.BlockSpec(memory_space=pltpu.VMEM)
    smem = pl.BlockSpec(memory_space=pltpu.SMEM)
    free = pl.BlockSpec(memory_space=pl.ANY)
    return pl.pallas_call(
        functools.partial(norm_kernel, width, spots, places, len(shards), len(carry)),
        in_specs=[smem, smem, vmem, vmem] + [free] * (len(shards) + len(carry)),
        out_specs=(vmem,) * len(sizes) + (free,) * len(carry),
        out_shape=tuple(shape(s, rows) for s in sizes[:-1])
        + (shape(1, rows, dtype=F32),)
        + tuple(shape(*c.shape) for c in carry),
        scratch_shapes=[
            pltpu.VMEM((n, 3, 2 * band, cols), BF),
            pltpu.VMEM((rows, 3 * cols), BF),
            pltpu.SemaphoreType.DMA((n, 2, 3)),
        ],
        input_output_aliases={4 + len(shards) + i: len(sizes) + i for i in range(len(carry))},
        compiler_params=PARAMS,
        cost_estimate=cost(1, 1),
    )(jnp.stack(halves), core.reshape(1), grads, proj, *shards, *carry)


def add_kernel(up_part, up_in, down_part, down_in, stat_ref, after_ref, up_out, down_out):
    half = up_part.shape[0]
    for part, came, out in ((up_part, up_in, up_out), (down_part, down_in, down_out)):
        out[:half, :] = (part[...].astype(F32) + came[:half, :].astype(F32)).astype(BF)
    at = up_in.shape[0] - 16
    write_stat(up_out, half, stat_ref[...] + read_stat(up_in, at))
    write_stat(down_out, half, stat_ref[...])


def add_messages(up_part, up_in, down_part, down_in, stat, after):
    half, rows = up_part.shape
    vmem = pl.BlockSpec(memory_space=pltpu.VMEM)
    return pl.pallas_call(
        add_kernel,
        out_shape=(shape(half + 16, rows),) * 2,
        in_specs=[vmem] * 5 + [pl.BlockSpec(memory_space=pl.ANY)],
        out_specs=(vmem, vmem),
        compiler_params=PARAMS,
        cost_estimate=cost(2 * half * rows, 12 * half * rows),
    )(up_part, up_in, down_part, down_in, stat, after)


def finish_kernel(at_ref, own0, own1, up0, up1, down0, down1, tok_ref, root_ref, stat_ref, out_ref):
    half = own0.shape[0]
    stat = stat_ref[...] + read_stat(up0, half) + read_stat(down1, half)
    stat = jnp.broadcast_to(stat, (HS, stat.shape[1])).T[:, 0:1]
    root = root_ref[...]
    parts = (
        (own0[...], up0[:half, :], down0[half : 2 * half, :]),
        (own1[...], up1[half : 2 * half, :], down1[:half, :]),
    )
    for i, part in enumerate(parts):
        span = slice(i * half, (i + 1) * half)
        total = sum(p.astype(F32) for p in part)
        unit = tok_ref[:, span].astype(F32) / root
        out_ref[:, span] = ((total.T - unit * stat) / root).astype(BF)


def finish(quarter, parts, tokens, root, stat):
    half, rows = parts[0].shape
    share = 2 * half
    whole = lambda a: pl.BlockSpec(a.shape, lambda i, at: (0, 0))
    return pl.pallas_call(
        finish_kernel,
        grid_spec=pltpu.PrefetchScalarGridSpec(
            num_scalar_prefetch=1,
            grid=(1,),
            in_specs=[whole(p) for p in parts]
            + [pl.BlockSpec((rows, share), lambda i, at: (0, at[0]))]
            + [whole(root), whole(stat)],
            out_specs=pl.BlockSpec((rows, share), lambda i, at: (0, 0)),
        ),
        out_shape=shape(rows, share),
        compiler_params=PARAMS,
        cost_estimate=cost(8 * rows * share, 10 * rows * share),
    )(quarter.reshape(1), *parts, tokens, root, stat)


def outer_kernel(at_ref, *refs):
    *blocks, mine_ref, other_ref, out_ref = refs
    n = mine_ref.shape[0]
    total = None
    for i, block in enumerate(blocks):
        g_ref = mine_ref if i < n else other_ref
        part = jnp.dot(block[...], g_ref[at_ref[i % n]], preferred_element_type=F32)
        total = part if total is None else total + part
    out_ref[...] = total.astype(BF)


def outer(blocks, order, mine, other):
    depth, rows = blocks[0].shape
    cols = mine.shape[2]
    tile = 512
    return pl.pallas_call(
        outer_kernel,
        grid_spec=pltpu.PrefetchScalarGridSpec(
            num_scalar_prefetch=1,
            grid=(depth // tile,),
            in_specs=[pl.BlockSpec((tile, rows), lambda i, at: (i, 0))] * len(blocks)
            + [pl.BlockSpec(mine.shape, lambda i, at: (0, 0, 0))] * 2,
            out_specs=pl.BlockSpec((tile, cols), lambda i, at: (i, 0)),
        ),
        out_shape=shape(depth, cols),
        compiler_params=PARAMS,
        cost_estimate=cost(1, 1),
    )(order, *blocks, mine, other)


def split_kernel(at_ref, part_ref, keep_ref, give_ref):
    n, _, rows, _ = part_ref.shape
    for ref, which in ((keep_ref, at_ref[0]), (give_ref, 1 - at_ref[0])):
        ref[...] = sum(part_ref[i, which].astype(F32) for i in range(n)).astype(ref.dtype)


def split(part, at):
    _, _, rows, cols = part.shape
    vmem = pl.BlockSpec(memory_space=pltpu.VMEM)
    return pl.pallas_call(
        split_kernel,
        in_specs=[pl.BlockSpec(memory_space=pltpu.SMEM), vmem],
        out_specs=(vmem, vmem),
        out_shape=(shape(rows, cols, dtype=F32), shape(rows, cols)),
        compiler_params=PARAMS,
        cost_estimate=cost(1, 1),
    )(at.reshape(1), part)


def merge_kernel(keep_ref, came_ref, att_ref, after_ref, out_ref):
    total = (keep_ref[...] + came_ref[...].astype(F32)).astype(BF)
    cols = total.shape[1]
    for i in range(out_ref.shape[0]):
        out_ref[i, :, :cols] = total
        out_ref[i, :, cols:] = att_ref[i]


def merge(keep, came, att, after):
    rows, cols = keep.shape
    n, _, more = att.shape
    vmem = pl.BlockSpec(memory_space=pltpu.VMEM)
    return pl.pallas_call(
        merge_kernel,
        out_shape=shape(n, rows, cols + more),
        in_specs=[vmem] * 3 + [pl.BlockSpec(memory_space=pl.ANY)],
        out_specs=vmem,
        compiler_params=PARAMS,
        cost_estimate=cost(1, 1),
    )(keep, came, att, after)


def unpack_kernel(in_ref, w_ref, att_ref):
    for h in range(in_ref.shape[0]):
        span = slice(h * HS, (h + 1) * HS)
        for j in range(3):
            w_ref[j, :, span] = in_ref[h, :, j * HS : (j + 1) * HS].astype(F32)
        att_ref[:, span] = in_ref[h, :, 3 * HS :]


def unpack(last):
    heads, rows, _ = last.shape
    return pl.pallas_call(
        unpack_kernel,
        out_shape=(shape(3, rows, heads * HS, dtype=F32), shape(rows, heads * HS)),
        compiler_params=PARAMS,
        cost_estimate=cost(last.size, 6 * last.size),
    )(last)


def gate(*arrays):
    free = pl.BlockSpec(memory_space=pl.ANY)
    return pl.pallas_call(
        lambda *refs: None,
        in_specs=[free] * len(arrays),
        out_specs=(free,) * len(arrays),
        out_shape=tuple(shape(*a.shape) for a in arrays),
        input_output_aliases={i: i for i in range(len(arrays))},
        compiler_params=PARAMS,
        cost_estimate=cost(1, 1),
    )(*arrays)


def shift(x, axis, by):
    n = lax.axis_size(axis)
    return lax.ppermute(x, axis, [(i, (i + by) % n) for i in range(n)])


def per_device(tokens, weights, cotangent):
    _, rows, width = tokens.shape
    w_rows, _, cols = weights.shape
    heads = cols // HS
    n_x, n_t, n_y = (lax.axis_size(a) for a in ("x", "zh", "y"))
    at_core, at_x, at_t, at_y, at_z = (lax.axis_index(a) for a in ("core", "x", "zh", "y", "zl"))
    share = width // n_t
    tokens = tokens.reshape(rows, width)

    def band(key):
        by, other_z, other_core = key
        return (((at_y + by) % n_y) * 2 + (at_z + other_z) % 2) * 2 + (at_core + other_core) % 2

    shards, place = [], {}

    def hold(by, z, core, *pieces):
        place[(by, z, core)] = [(len(shards) + j * (len(pieces) > 1), j * (len(pieces) == 1)) for j in range(3)]
        shards.extend(pieces)

    def projection(some, earlier, **more):
        used = sorted({which for k in some for which, _ in place[k]})
        spots = [[(used.index(which), at) for which, at in place[k]] for k in some]
        return project(
            normed, [band(k) for k in some], [shards[u] for u in used], spots, earlier, **more
        )

    swap = lambda w: shift(w, "core", 1)
    own = weights.transpose(1, 0, 2)
    normed, root, mine, given = unit_rows(tokens, at_core, w_rows)
    own_2, left, right, other, theirs, left_m, right_m = gate(
        swap(own),
        shift(own, "y", 1),
        shift(own, "y", -1),
        shift(own, "zl", 1),
        swap(given),
        shift(mine, "x", 1),
        shift(mine, "x", -1),
    )
    hold(0, 0, 0, own)
    hold(0, 0, 1, own_2)
    far, other_left, other_right, left_2, right_2, other_2, left_t, right_t = gate(
        shift(left, "y", 1),
        shift(left, "zl", 1),
        shift(other, "y", -1),
        swap(left),
        swap(right),
        swap(other),
        shift(theirs, "x", 1),
        shift(theirs, "x", -1),
    )
    for key, one, two in (((3, 0), left, left_2), ((1, 0), right, right_2), ((0, 1), other, other_2)):
        hold(*key, 0, one)
        hold(*key, 1, two)
    proj = projection(list(place), None)
    far_m, far_t = shift(left_m, "x", 1), shift(right_t, "x", -1)
    *last_pieces, far_2, other_left_2, other_right_2 = gate(
        shift(far[0:1], "zl", 1),
        shift(other_left[1:2], "y", 1),
        shift(other_right[2:3], "y", -1),
        swap(far),
        swap(other_left),
        swap(other_right),
    )
    start = len(place)
    for key, one, two in (
        ((2, 0), far, far_2),
        ((3, 1), other_left, other_left_2),
        ((1, 1), other_right, other_right_2),
    ):
        hold(*key, 0, one)
        hold(*key, 1, two)
    proj = projection(list(place)[start:], proj)
    start = len(place)
    hold(2, 1, 0, *last_pieces)
    hold(2, 1, 1, *(swap(p) for p in last_pieces))
    proj = projection(list(place)[start:], proj, heads=heads)

    dout = cotangent.reshape(rows, heads, HS).transpose(1, 0, 2)
    dout = lax.all_to_all(dout, "x", 0, 0, tiled=True).reshape(n_x * rows, HS)
    blocks = (mine, left_m, right_m, far_m, theirs, left_t, right_t, far_t)
    order = jnp.stack([(at_x + by) % n_x for by in (0, n_x - 1, 1, 2)])
    qkv = lax.all_to_all(proj, "x", 0, 0, tiled=True).reshape(n_x * rows, 3 * HS)
    att, head_grads = attention(qkv, dout, (far_m, far_t))

    head_grads = head_grads.reshape(n_x, rows, 3 * HS)
    grads = lax.all_to_all(head_grads, "x", 0, 0, tiled=True)
    part = outer(blocks, order, head_grads, shift(head_grads, "core", 1))

    half = share // 2
    spread = [[place[(by, z, core)] for core in range(2)] for by in range(n_y) for z in range(2)]

    def norm(at, spots, sizes, carry=()):
        where = [2 * ((quarter - at_y) % n_y) + (at_z + z) % 2 for quarter, z in at]
        return norm_halves(
            grads, proj, shards, spread, where, at_core, spots, sizes, width, carry
        )

    here, above, far, below = ((at_t + by) % n_t for by in range(n_t))
    up, down, stat, part = norm(
        [(far, 0), (above, 1), (far, 1), (below, 0)],
        ((0, 0), (0, half), (1, 0), (1, half)),
        (share + 16, share),
        (part,),
    )
    up, down = shift(up, "zh", 1), shift(down, "zh", -1)
    up_part, down_part, own0, own1, _ = norm(
        [(above, 0), (below, 1), (here, 0), (here, 1)],
        ((0, 0), (1, 0), (2, 0), (3, 0)),
        (half,) * 4,
    )
    part = lax.all_to_all(part, "y", 0, 0, tiled=True).reshape(n_y, 2, w_rows, 3 * HS)
    keep, give = split(part, at_z)
    came = shift(give, "zl", 1)
    up_2, down_2 = add_messages(up_part, up, down_part, down, stat, give)
    last = merge(keep, came, att.reshape(n_x, rows, HS), up_2)
    up_2, down_2 = shift(up_2, "zh", 1), shift(down_2, "zh", -1)
    last = lax.all_to_all(last, "x", 0, 0, tiled=True)
    token_grad = finish(at_t, (own0, own1, up_2, up, down, down_2), tokens, root, stat)
    weight_grad, attended = unpack(last)
    return attended[None], token_grad[None], weight_grad.transpose(1, 0, 2)


def solution(mesh):
    fine = Mesh(mesh.devices.reshape(4, 2, 2, 4, 4), ("y", "zl", "core", "x", "zh"))
    dp = ("y", "zl", "core")
    return jax.shard_map(
        per_device,
        mesh=fine,
        in_specs=(P(dp, "x", None), P(dp, None, "zh"), P(dp, "x", "zh")),
        out_specs=(P(dp, "x", "zh"), P(dp, "x", "zh"), P(dp, None, "zh")),
        check_vma=False,
    )
```

```python
import functools
import math

import jax
import jax.numpy as jnp
from jax import lax
from jax.experimental import pallas as pl
from jax.experimental.pallas import tpu as pltpu
from jax.sharding import Mesh
from jax.sharding import PartitionSpec as P

HS = 128
CORE, X, T, Y, Z = range(5)
BF = jnp.bfloat16
F32 = jnp.float32
PARAMS = pltpu.CompilerParams(vmem_limit_bytes=60 * 1024 * 1024)


def dot(a, b, ca, cb):
    return lax.dot_general(a, b, (((ca,), (cb,)), ((), ())), preferred_element_type=F32)


def cost(flops, nbytes, exps=0):
    return pl.CostEstimate(flops=flops, bytes_accessed=nbytes, transcendentals=exps)


def shape(*dims, dtype=BF):
    return jax.ShapeDtypeStruct(dims, dtype)


def unit_kernel(at_ref, tok_ref, normed_ref, root_ref, mine_ref, given_ref, *, band):
    tok = tok_ref[...].astype(F32)
    root = jnp.sqrt(jnp.mean(tok * tok, -1, keepdims=True) + 1e-05)
    normed_ref[...] = (tok / root).astype(BF)
    root_ref[...] = root
    core = at_ref[CORE]
    for i in range(mine_ref.shape[0] // band):
        for ref, which in ((mine_ref, core), (given_ref, 1 - core)):
            at = pl.multiple_of((2 * i + which) * band, band)
            ref[i * band : (i + 1) * band, :] = normed_ref[:, pl.ds(at, band)].T


def unit_rows(ids, tokens, band):
    rows, width = tokens.shape
    tile = 128
    return pl.pallas_call(
        functools.partial(unit_kernel, band=band),
        grid_spec=pltpu.PrefetchScalarGridSpec(
            num_scalar_prefetch=1,
            grid=(rows // tile,),
            in_specs=[pl.BlockSpec((tile, width), lambda i, at: (i, 0))],
            out_specs=(
                pl.BlockSpec((tile, width), lambda i, at: (i, 0)),
                pl.BlockSpec((tile, 1), lambda i, at: (i, 0)),
                pl.BlockSpec((width // 2, tile), lambda i, at: (0, i)),
                pl.BlockSpec((width // 2, tile), lambda i, at: (0, i)),
            ),
        ),
        out_shape=(
            shape(rows, width),
            shape(rows, 1, dtype=F32),
            shape(width // 2, rows),
            shape(width // 2, rows),
        ),
        compiler_params=PARAMS,
        cost_estimate=cost(6 * rows * width, 6 * rows * width),
    )(ids, tokens)


def project_kernel(chunks, a_any, w_any, *refs):
    heads_ref, a_ref, w_ref, acc_ref, a_sem, w_sem = refs[-6:]
    bands, kinds, depth, cols = w_ref.shape
    n = bands // chunks
    copies = []
    for c in range(chunks):
        span = pl.ds(c * n * depth, n * depth)
        some = pl.ds(c * n, n)
        copies.append(
            (
                pltpu.make_async_copy(a_any.at[:, span], a_ref.at[:, span], a_sem.at[c]),
                pltpu.make_async_copy(w_any.at[some], w_ref.at[some], w_sem.at[c]),
            )
        )
        for copy in copies[-1]:
            copy.start()
    for c in range(chunks):
        for copy in copies[c]:
            copy.wait()
        band = a_ref[:, c * n * depth : (c + 1) * n * depth]
        for j in range(kinds):
            w = w_ref[c * n : (c + 1) * n, j].reshape(n * depth, cols)
            part = jnp.dot(band, w, preferred_element_type=F32)
            span = slice(j * cols, (j + 1) * cols)
            if c:
                part += acc_ref[:, span]
            if c < chunks - 1:
                acc_ref[:, span] = part
            else:
                for h in range(heads_ref.shape[0]):
                    heads_ref[h, :, j * HS : (j + 1) * HS] = part[:, h * HS : (h + 1) * HS].astype(BF)


def project(normed, w, heads, after):
    rows, depth = normed.shape
    bands, kinds, _, cols = w.shape
    chunks = 4
    free = pl.BlockSpec(memory_space=pl.ANY)
    return pl.pallas_call(
        functools.partial(project_kernel, chunks),
        in_specs=[free] * (2 + len(after)),
        out_specs=pl.BlockSpec(memory_space=pltpu.VMEM),
        out_shape=shape(heads, rows, kinds * cols // heads),
        scratch_shapes=[
            pltpu.VMEM(normed.shape, BF),
            pltpu.VMEM(w.shape, BF),
            pltpu.VMEM((rows, kinds * cols), F32),
            pltpu.SemaphoreType.DMA((chunks,)),
            pltpu.SemaphoreType.DMA((chunks,)),
        ],
        compiler_params=PARAMS,
        cost_estimate=cost(1, 1),
    )(normed, w, *after)


def attention_kernel(q_rows, qkv_ref, dout_ref, *refs):
    att_ref, grad_ref, dk_ref, dv_ref = refs[-4:]
    scale = 1.0 / math.sqrt(HS)
    key = qkv_ref[:, HS : 2 * HS]
    value = qkv_ref[:, 2 * HS : 3 * HS]
    key_t = key.T
    value_t = value.T
    for i in range(qkv_ref.shape[0] // q_rows):
        rows = pl.ds(i * q_rows, q_rows)
        query = qkv_ref[rows, 0:HS]
        dout = dout_ref[rows, :]
        scores = dot(key, query, 1, 1) * (scale * math.log2(math.e))
        top = jnp.max(scores, axis=0, keepdims=True)
        expo = jnp.exp2(scores - top)
        prob = expo * (1.0 / jnp.sum(expo, axis=0, keepdims=True))
        prob_bf = prob.astype(BF)
        att = dot(value_t, prob_bf, 1, 0).T.astype(BF)
        att_ref[rows, :] = att
        row_dot = jnp.sum(
            dout.astype(F32).T * att.astype(F32).T, axis=0, keepdims=True
        )
        dprob = dot(value, dout, 1, 1)
        dscore = (prob * (dprob - row_dot)).astype(BF)
        grad_ref[rows, 0:HS] = (dot(key_t, dscore, 1, 0) * scale).T.astype(BF)
        dv = dot(prob_bf, dout, 1, 0)
        dk = dot(dscore, query, 1, 0)
        if i == 0:
            dv_ref[...] = dv
            dk_ref[...] = dk
        else:
            dv_ref[...] += dv
            dk_ref[...] += dk
    grad_ref[:, HS : 2 * HS] = (dk_ref[...] * scale).astype(BF)
    grad_ref[:, 2 * HS : 3 * HS] = dv_ref[...].astype(BF)


def attention(qkv, dout, after=()):
    n = qkv.shape[0]
    return pl.pallas_call(
        functools.partial(attention_kernel, min(256, n)),
        out_shape=(shape(n, HS), shape(n, 3 * HS)),
        in_specs=[pl.BlockSpec(memory_space=pltpu.VMEM)] * 2
        + [pl.BlockSpec(memory_space=pl.ANY)] * len(after),
        out_specs=(pl.BlockSpec(memory_space=pltpu.VMEM),) * 2,
        scratch_shapes=[pltpu.VMEM((n, HS), F32), pltpu.VMEM((n, HS), F32)],
        compiler_params=PARAMS,
        cost_estimate=cost(1, 1),
    )(qkv, dout, *after)


def write_stat(ref, at, stat):
    ref[at:, :] = jnp.zeros((ref.shape[0] - at, ref.shape[1]), BF)
    rest = stat
    for i in range(3):
        top = rest.astype(BF)
        ref[at + i : at + i + 1, :] = top
        rest = rest - top.astype(F32)


def read_stat(ref, at):
    return sum(ref[at + i : at + i + 1, :].astype(F32) for i in range(3))


def norm_kernel(width, halves, spots, at_ref, g_ref, p_ref, w_any, *refs):
    n_out = max(spot[0] for spot in spots) + 1
    outs, stat_ref = refs[-4 - n_out : -4], refs[-4]
    w_ref, flat_ref, sems = refs[-3:]
    n, bands, kinds, depth, cols = w_ref.shape
    quarters = w_any.shape[0] // (2 * bands)
    copies = []
    for step, (by, half) in enumerate(halves):
        at = (lax.rem(at_ref[T] + by, quarters) * 2 + half) * bands
        copy = pltpu.make_async_copy(w_any.at[pl.ds(at, bands)], w_ref.at[step], sems.at[step])
        copy.start()
        copies.append(copy)

    heads, _, _ = g_ref.shape
    for h in range(heads):
        for j in range(kinds):
            at = (j * heads + h) * HS
            flat_ref[at : at + HS, :] = g_ref[h, :, j * HS : (j + 1) * HS].T
    total = sum(
        g_ref[h, :, j * HS : (j + 1) * HS].astype(F32)
        * p_ref[h, :, j * HS : (j + 1) * HS].astype(F32)
        for h in range(heads)
        for j in range(kinds)
    )
    stat = jnp.sum(total.T, axis=0, keepdims=True) * (1.0 / width)
    stat_ref[...] = stat
    for ref in outs:
        if ref.shape[0] % 128:
            write_stat(ref, ref.shape[0] - 16, stat)

    for step, (which, at) in enumerate(spots):
        copies[step].wait()
        total = sum(
            dot(
                w_ref[step, :, j].reshape(bands * depth, cols),
                flat_ref[j * cols : (j + 1) * cols, :],
                1,
                0,
            )
            for j in range(kinds)
        )
        outs[which][at : at + bands * depth, :] = total.astype(BF)


def norm_halves(ids, grads, proj, w, halves, spots, sizes, width, after=()):
    heads, rows, _ = grads.shape
    bands, kinds, depth, cols = w.shape
    n = len(spots)
    sizes = (*sizes, 1)
    vmem = pl.BlockSpec(memory_space=pltpu.VMEM)
    free = pl.BlockSpec(memory_space=pl.ANY)
    return pl.pallas_call(
        functools.partial(norm_kernel, width, halves, spots),
        in_specs=[pl.BlockSpec(memory_space=pltpu.SMEM), vmem, vmem, free] + [free] * len(after),
        out_specs=(vmem,) * len(sizes),
        out_shape=tuple(shape(s, rows) for s in sizes[:-1]) + (shape(1, rows, dtype=F32),),
        scratch_shapes=[
            pltpu.VMEM((n, bands // 8, kinds, depth, cols), BF),
            pltpu.VMEM((kinds * cols, rows), BF),
            pltpu.SemaphoreType.DMA((n,)),
        ],
        compiler_params=PARAMS,
        cost_estimate=cost(1, 1),
    )(ids, grads, proj, w, *after)


def add_kernel(up_part, up_in, stat_in, down_part, down_in, stat_ref, *refs):
    up_out, down_out = refs[-2:]
    half = up_part.shape[0]
    for part, came, out in ((up_part, up_in, up_out), (down_part, down_in, down_out)):
        out[:half, :] = (part[...].astype(F32) + came[...].astype(F32)).astype(BF)
    write_stat(up_out, half, stat_ref[...] + read_stat(stat_in, 0))
    write_stat(down_out, half, stat_ref[...])


def add_messages(up_part, up_in, down_part, down_in, stat, after=()):
    half, rows = up_part.shape
    block = pl.BlockSpec((half, rows), lambda i: (0, 0))
    out = pl.BlockSpec((half + 16, rows), lambda i: (0, 0))
    end = pl.BlockSpec((16, rows), lambda i: (2 * half // 16, 0))
    return pl.pallas_call(
        add_kernel,
        grid=(1,),
        out_shape=(shape(half + 16, rows),) * 2,
        in_specs=[block, block, end, block, block, pl.BlockSpec((1, rows), lambda i: (0, 0))]
        + [pl.BlockSpec(memory_space=pl.ANY)] * len(after),
        out_specs=(out, out),
        compiler_params=PARAMS,
        cost_estimate=cost(1, 1),
    )(up_part, up_in, up_in, down_part, down_in, stat, *after)


def finish_kernel(at_ref, own0, own1, up0, up1, down0, down1, tok_ref, root_ref, stat_ref, out_ref):
    half = own0.shape[0]
    stat = stat_ref[...] + read_stat(up0, half) + read_stat(down1, half)
    stat = jnp.broadcast_to(stat, (HS, stat.shape[1])).T[:, 0:1]
    root = root_ref[...]
    parts = (
        (own0[...], up0[:half, :], down0[half : 2 * half, :]),
        (own1[...], up1[half : 2 * half, :], down1[:half, :]),
    )
    for i, part in enumerate(parts):
        span = slice(i * half, (i + 1) * half)
        total = sum(p.astype(F32) for p in part)
        unit = tok_ref[:, span].astype(F32) / root
        out_ref[:, span] = ((total.T - unit * stat) / root).astype(BF)


def finish(ids, parts, tokens, root, stat):
    half, rows = parts[0].shape
    share = 2 * half
    tile = HS
    some = lambda a: pl.BlockSpec((a.shape[0], tile), lambda i, at: (0, i))
    return pl.pallas_call(
        finish_kernel,
        grid_spec=pltpu.PrefetchScalarGridSpec(
            num_scalar_prefetch=1,
            grid=(rows // tile,),
            in_specs=[some(p) for p in parts]
            + [pl.BlockSpec((tile, share), lambda i, at: (i, at[T]))]
            + [pl.BlockSpec((tile, 1), lambda i, at: (i, 0)), some(stat)],
            out_specs=pl.BlockSpec((tile, share), lambda i, at: (i, 0)),
        ),
        out_shape=shape(rows, share),
        compiler_params=PARAMS,
        cost_estimate=cost(1, 1),
    )(ids, *parts, tokens, root, stat)


def outer_kernel(tile, at_ref, *refs):
    blocks, (mine_ref, other_ref, out_ref, a_ref, g_ref, sems) = refs[:-6], refs[-6:]
    n, rows, _ = mine_ref.shape
    depth = a_ref.shape[0]
    copies = []
    for step in range(depth // tile):
        span = pl.ds(step * tile, tile)
        some = []
        for i, block in enumerate(blocks):
            to = a_ref.at[span, pl.ds(i * rows, rows)]
            some.append(pltpu.make_async_copy(block.at[span], to, sems.at[step, i]))
            some[-1].start()
        copies.append(some)
    for i, by in enumerate((0, n - 1, 1, 2)):
        at = lax.rem(at_ref[X] + by, n)
        g_ref[i * rows : (i + 1) * rows, :] = mine_ref[at]
        g_ref[(n + i) * rows : (n + i + 1) * rows, :] = other_ref[at]
    for step, some in enumerate(copies):
        for copy in some:
            copy.wait()
        span = slice(step * tile, (step + 1) * tile)
        out_ref[span, :] = jnp.dot(
            a_ref[span, :], g_ref[...], preferred_element_type=F32
        ).astype(BF)


def outer(ids, blocks, mine, other):
    depth, rows = blocks[0].shape
    cols = mine.shape[2]
    tile = 512
    vmem = pl.BlockSpec(memory_space=pltpu.VMEM)
    return pl.pallas_call(
        functools.partial(outer_kernel, tile),
        in_specs=[pl.BlockSpec(memory_space=pltpu.SMEM)]
        + [pl.BlockSpec(memory_space=pl.ANY)] * len(blocks)
        + [vmem, vmem],
        out_specs=vmem,
        out_shape=shape(depth, cols),
        scratch_shapes=[
            pltpu.VMEM((depth, len(blocks) * rows), BF),
            pltpu.VMEM((len(blocks) * rows, cols), BF),
            pltpu.SemaphoreType.DMA((depth // tile, len(blocks))),
        ],
        compiler_params=PARAMS,
        cost_estimate=cost(1, 1),
    )(ids, *blocks, mine, other)


def split_kernel(at_ref, part_ref, *refs):
    keep_ref, give_ref = refs[-2:]
    n, _, rows, _ = part_ref.shape
    for ref, which in ((keep_ref, at_ref[Z]), (give_ref, 1 - at_ref[Z])):
        ref[...] = sum(part_ref[i, which].astype(F32) for i in range(n)).astype(ref.dtype)


def split(ids, part, after=()):
    _, _, rows, cols = part.shape
    vmem = pl.BlockSpec(memory_space=pltpu.VMEM)
    return pl.pallas_call(
        split_kernel,
        in_specs=[pl.BlockSpec(memory_space=pltpu.SMEM), vmem]
        + [pl.BlockSpec(memory_space=pl.ANY)] * len(after),
        out_specs=(vmem, vmem),
        out_shape=(shape(rows, cols, dtype=F32), shape(rows, cols)),
        compiler_params=PARAMS,
        cost_estimate=cost(1, 1),
    )(ids, part, *after)


def merge_kernel(keep_ref, came_ref, att_ref, *refs):
    out_ref = refs[-1]
    total = (keep_ref[...] + came_ref[...].astype(F32)).astype(BF)
    cols = total.shape[1]
    for i in range(out_ref.shape[0]):
        out_ref[i, :, :cols] = total
        out_ref[i, :, cols:] = att_ref[i]


def merge(keep, came, att, after=()):
    rows, cols = keep.shape
    n, _, more = att.shape
    vmem = pl.BlockSpec(memory_space=pltpu.VMEM)
    return pl.pallas_call(
        merge_kernel,
        out_shape=shape(n, rows, cols + more),
        in_specs=[vmem] * 3 + [pl.BlockSpec(memory_space=pl.ANY)] * len(after),
        out_specs=vmem,
        compiler_params=PARAMS,
        cost_estimate=cost(1, 1),
    )(keep, came, att, *after)


def unpack_kernel(in_ref, w_ref, att_ref):
    for h in range(in_ref.shape[0]):
        span = slice(h * HS, (h + 1) * HS)
        for j in range(3):
            w_ref[j, :, span] = in_ref[h, :, j * HS : (j + 1) * HS].astype(F32)
        att_ref[:, span] = in_ref[h, :, 3 * HS :]


def unpack(last):
    heads, rows, more = last.shape
    tile = rows // 4
    return pl.pallas_call(
        unpack_kernel,
        grid=(rows // tile,),
        in_specs=[pl.BlockSpec((heads, tile, more), lambda i: (0, i, 0))],
        out_specs=(
            pl.BlockSpec((3, tile, heads * HS), lambda i: (0, i, 0)),
            pl.BlockSpec((tile, heads * HS), lambda i: (i, 0)),
        ),
        out_shape=(shape(3, rows, heads * HS, dtype=F32), shape(rows, heads * HS)),
        compiler_params=PARAMS,
        cost_estimate=cost(1, 1),
    )(last)


def shift(x, axis, by):
    n = lax.axis_size(axis)
    return lax.ppermute(x, axis, [(i, (i + by) % n) for i in range(n)])


def per_device(tokens, weights, cotangent):
    _, rows, width = tokens.shape
    w_rows, _, cols = weights.shape
    heads = cols // HS
    n_x, n_y = (lax.axis_size(a) for a in ("x", "y"))
    ids = jnp.stack([lax.axis_index(a) for a in ("core", "x", "zh", "y", "zl")])
    tokens = tokens.reshape(rows, width)
    half = width // lax.axis_size("zh") // 2

    w = lax.all_gather(weights.transpose(1, 0, 2)[None], ("y", "zl", "core"), axis=0, tiled=True)

    normed, root, mine, given = unit_rows(ids, tokens, w_rows)
    theirs = shift(given, "core", 1)
    left_m, right_m = shift(mine, "x", 1), shift(mine, "x", -1)
    left_t, right_t = shift(theirs, "x", 1), shift(theirs, "x", -1)
    far_m, far_t = shift(left_m, "x", 1), shift(right_t, "x", -1)
    blocks = (mine, left_m, right_m, far_m, theirs, left_t, right_t, far_t)

    dout = cotangent.reshape(rows, heads, HS).transpose(1, 0, 2)
    dout = lax.all_to_all(dout, "x", 0, 0, tiled=True).reshape(n_x * rows, HS)

    proj = project(normed, w, heads, (*blocks, dout))
    qkv = lax.all_to_all(proj, "x", 0, 0, tiled=True).reshape(n_x * rows, 3 * HS)
    att, head_grads = attention(qkv, dout)

    head_grads = head_grads.reshape(n_x, rows, 3 * HS)
    grads = lax.all_to_all(head_grads, "x", 0, 0, tiled=True)
    part = outer(ids, blocks, head_grads, shift(head_grads, "core", 1))

    up, down, stat = norm_halves(
        ids, grads, proj, w,
        ((2, 0), (1, 1), (2, 1), (3, 0)),
        ((0, 0), (0, half), (1, 0), (1, half)),
        (2 * half + 16, 2 * half),
        width,
    )
    up, down = shift(up, "zh", 1), shift(down, "zh", -1)
    up_part, down_part, own0, own1, _ = norm_halves(
        ids, grads, proj, w,
        ((1, 0), (3, 1), (0, 0), (0, 1)),
        ((0, 0), (1, 0), (2, 0), (3, 0)),
        (half,) * 4,
        width,
        (stat,),
    )
    part = lax.all_to_all(part, "y", 0, 0, tiled=True).reshape(n_y, 2, w_rows, 3 * HS)
    keep, give = split(ids, part, (own0,))
    came = shift(give, "zl", 1)
    up_2, down_2 = add_messages(up_part, up, down_part, down, stat, (give,))
    last = merge(keep, came, att.reshape(n_x, rows, HS), (up_2,))
    up_2, down_2 = shift(up_2, "zh", 1), shift(down_2, "zh", -1)
    last = lax.all_to_all(last, "x", 0, 0, tiled=True)
    token_grad = finish(ids, (own0, own1, up_2, up, down, down_2), tokens, root, stat)
    weight_grad, attended = unpack(last)
    return attended[None], token_grad[None], weight_grad.transpose(1, 0, 2)


def solution(mesh):
    fine = Mesh(mesh.devices.reshape(4, 2, 2, 4, 4), ("y", "zl", "core", "x", "zh"))
    dp = ("y", "zl", "core")
    return jax.shard_map(
        per_device,
        mesh=fine,
        in_specs=(P(dp, "x", None), P(dp, None, "zh"), P(dp, "x", "zh")),
        out_specs=(P(dp, "x", "zh"), P(dp, "x", "zh"), P(dp, None, "zh")),
        check_vma=False,
    )
```

```python
import functools
import math

import jax
import jax.numpy as jnp
from jax import lax
from jax.experimental import pallas as pl
from jax.experimental.pallas import tpu as pltpu
from jax.sharding import Mesh
from jax.sharding import PartitionSpec as P

HS = 128
CORE, X, T, Y, Z = range(5)
BF = jnp.bfloat16
BUSY = 2 * 10**10
F32 = jnp.float32
PARAMS = pltpu.CompilerParams(vmem_limit_bytes=60 * 1024 * 1024)


def dot(a, b, ca, cb):
    return lax.dot_general(a, b, (((ca,), (cb,)), ((), ())), preferred_element_type=F32)


def cost(flops, nbytes, exps=0):
    return pl.CostEstimate(flops=flops, bytes_accessed=nbytes, transcendentals=exps)


def shape(*dims, dtype=BF):
    return jax.ShapeDtypeStruct(dims, dtype)


def unit_kernel(at_ref, tok_ref, other_ref, root_ref, mine_ref, given_ref, theirs_ref, both_ref, *, band):
    core = at_ref[CORE]
    for n, ref in enumerate((tok_ref, other_ref)):
        tok = ref[...].astype(F32)
        root = jnp.sqrt(jnp.mean(tok * tok, -1, keepdims=True) + 1e-05)
        outs = [(theirs_ref, core)]
        if n == 0:
            root_ref[...] = root
            outs = [(mine_ref, core), (given_ref, 1 - core)]
        for i in range(mine_ref.shape[1] // band):
            for k, (out, which) in enumerate(outs):
                at = pl.multiple_of((2 * i + which) * band, band)
                unit = (ref[:, pl.ds(at, band)].astype(F32) / root).astype(BF)
                out[:, i * band : (i + 1) * band] = unit
                if k == 0:
                    both_ref[n, i * band : (i + 1) * band, :] = unit.T


def unit_rows(ids, tokens, others, band):
    rows, width = tokens.shape
    tile = 128
    half = width // 2
    row = pl.BlockSpec((tile, width), lambda i, at: (i, 0))
    return pl.pallas_call(
        functools.partial(unit_kernel, band=band),
        grid_spec=pltpu.PrefetchScalarGridSpec(
            num_scalar_prefetch=1,
            grid=(rows // tile,),
            in_specs=[row, row],
            out_specs=(pl.BlockSpec((tile, 1), lambda i, at: (i, 0)),)
            + (pl.BlockSpec((tile, half), lambda i, at: (i, 0)),) * 3
            + (pl.BlockSpec((2, half, tile), lambda i, at: (0, 0, i)),),
        ),
        out_shape=(shape(rows, 1, dtype=F32),)
        + (shape(rows, half),) * 3
        + (shape(2, half, rows),),
        compiler_params=PARAMS,
        cost_estimate=cost(BUSY, 1),
    )(ids, tokens, others)


def project_kernel(offsets, first, at_ref, mine_ref, theirs_ref, *refs):
    keep_ref, give_ref, stack_ref, sems = refs[-4:]
    n = len(offsets)
    shards, sums = refs[:n], refs[n:-4]
    copies = [pltpu.make_async_copy(w, stack_ref.at[i], sems.at[i]) for i, w in enumerate(shards)]
    for copy in copies:
        copy.start()
    kinds, depth, cols = shards[0].shape
    bands = [
        pl.ds(pl.multiple_of(place_of(at_ref, *offset) * depth, depth), depth) for offset in offsets
    ]
    for i, (rows, out) in enumerate(((mine_ref, keep_ref), (theirs_ref, give_ref))):
        for j in range(kinds):
            span = slice(j * cols, (j + 1) * cols)
            total = None if first else sums[i][:, span]
            for band, shard in zip(bands, shards):
                part = jnp.dot(rows[:, band], shard[j], preferred_element_type=F32)
                total = part if total is None else total + part
            out[:, span] = total.astype(out.dtype)
    for copy in copies:
        copy.wait()


def place_of(at_ref, y, z):
    return lax.rem(at_ref[Y] + y, 4) * 2 + lax.rem(at_ref[Z] + z, 2)


def project(ids, mine, theirs, shards, offsets, sums=(), give=F32):
    rows, _ = mine.shape
    n = len(shards)
    vmem = pl.BlockSpec(memory_space=pltpu.VMEM)
    cols = 3 * shards[0].shape[-1]
    return pl.pallas_call(
        functools.partial(project_kernel, offsets, not sums),
        in_specs=[pl.BlockSpec(memory_space=pltpu.SMEM)] + [vmem] * (2 + n + len(sums)),
        out_specs=(vmem, vmem, pl.BlockSpec(memory_space=pl.ANY)),
        out_shape=(
            shape(rows, cols, dtype=F32),
            shape(rows, cols, dtype=give),
            shape(n, *shards[0].shape),
        ),
        scratch_shapes=[pltpu.SemaphoreType.DMA((n,))],
        compiler_params=PARAMS,
        cost_estimate=cost(BUSY, 1),
    )(ids, mine, theirs, *shards, *sums)


def project_last_kernel(offset, at_ref, mine_ref, given_ref, keep_ref, came_ref, *refs):
    shards, heads_ref = refs[:-1], refs[-1]
    depth, cols = shards[0].shape[-2:]
    band = pl.ds(pl.multiple_of(place_of(at_ref, *offset) * depth, depth), depth)
    for j in range(3):
        span = slice(j * cols, (j + 1) * cols)
        total = keep_ref[:, span] + came_ref[:, span].astype(F32)
        total += jnp.dot(mine_ref[:, band], shards[j][0], preferred_element_type=F32)
        total += jnp.dot(given_ref[:, band], shards[3 + j][0], preferred_element_type=F32)
        for h in range(heads_ref.shape[0]):
            heads_ref[h, :, j * HS : (j + 1) * HS] = total[:, h * HS : (h + 1) * HS].astype(BF)


def project_last(ids, mine, given, keep, came, pieces, offset, heads):
    rows, cols = keep.shape
    vmem = pl.BlockSpec(memory_space=pltpu.VMEM)
    return pl.pallas_call(
        functools.partial(project_last_kernel, offset),
        in_specs=[pl.BlockSpec(memory_space=pltpu.SMEM)] + [vmem] * (4 + len(pieces)),
        out_specs=vmem,
        out_shape=shape(heads, rows, cols // heads),
        compiler_params=PARAMS,
        cost_estimate=cost(1, 1),
    )(ids, mine, given, keep, came, *pieces)


def attention_kernel(q_rows, qkv_ref, dout_ref, *refs):
    att_ref, grad_ref, dk_ref, dv_ref = refs[-4:]
    scale = 1.0 / math.sqrt(HS)
    key = qkv_ref[:, HS : 2 * HS]
    value = qkv_ref[:, 2 * HS : 3 * HS]
    key_t = key.T
    value_t = value.T
    for i in range(qkv_ref.shape[0] // q_rows):
        rows = pl.ds(i * q_rows, q_rows)
        query = qkv_ref[rows, 0:HS]
        dout = dout_ref[rows, :]
        scores = dot(key, query, 1, 1) * (scale * math.log2(math.e))
        top = jnp.max(scores, axis=0, keepdims=True)
        expo = jnp.exp2(scores - top)
        prob = expo * (1.0 / jnp.sum(expo, axis=0, keepdims=True))
        prob_bf = prob.astype(BF)
        att = dot(value_t, prob_bf, 1, 0).T.astype(BF)
        att_ref[rows, :] = att
        row_dot = jnp.sum(
            dout.astype(F32).T * att.astype(F32).T, axis=0, keepdims=True
        )
        dprob = dot(value, dout, 1, 1)
        dscore = (prob * (dprob - row_dot)).astype(BF)
        grad_ref[rows, 0:HS] = (dot(key_t, dscore, 1, 0) * scale).T.astype(BF)
        dv = dot(prob_bf, dout, 1, 0)
        dk = dot(dscore, query, 1, 0)
        if i == 0:
            dv_ref[...] = dv
            dk_ref[...] = dk
        else:
            dv_ref[...] += dv
            dk_ref[...] += dk
    grad_ref[:, HS : 2 * HS] = (dk_ref[...] * scale).astype(BF)
    grad_ref[:, 2 * HS : 3 * HS] = dv_ref[...].astype(BF)


def attention(qkv, dout, after=()):
    n = qkv.shape[0]
    return pl.pallas_call(
        functools.partial(attention_kernel, min(256, n)),
        out_shape=(shape(n, HS), shape(n, 3 * HS)),
        in_specs=[pl.BlockSpec(memory_space=pltpu.VMEM)] * 2
        + [pl.BlockSpec(memory_space=pl.ANY)] * len(after),
        out_specs=(pl.BlockSpec(memory_space=pltpu.VMEM),) * 2,
        scratch_shapes=[pltpu.VMEM((n, HS), F32), pltpu.VMEM((n, HS), F32)],
        compiler_params=PARAMS,
        cost_estimate=cost(1, 1),
    )(qkv, dout, *after)


def write_stat(ref, at, stat):
    ref[at:, :] = jnp.zeros((ref.shape[0] - at, ref.shape[1]), BF)
    rest = stat
    for i in range(3):
        top = rest.astype(BF)
        ref[at + i : at + i + 1, :] = top
        rest = rest - top.astype(F32)


def read_stat(ref, at):
    return sum(ref[at + i : at + i + 1, :].astype(F32) for i in range(3))


def norm_kernel(width, halves, spots, places, n_in, at_ref, g_ref, p_ref, *refs):
    shards = refs[:n_in]
    n_out = max(spot[0] for spot in spots) + 1
    outs, stat_ref = refs[-4 - n_out : -4], refs[-4]
    w_ref, flat_ref, sems = refs[-3:]
    _, kinds, depth, cols = w_ref.shape
    band = depth // 2
    quarters = len(places) // 2

    def copy(step, core, j, source):
        to = lax.rem(at_ref[CORE] + core, 2)
        at = pl.ds(pl.multiple_of(to * band, band), band)
        return pltpu.make_async_copy(source, w_ref.at[step, j, at], sems.at[step, core, j])

    for step, (by, half) in enumerate(halves):
        y_off = lax.rem(at_ref[T] + (by + quarters) - at_ref[Y], quarters)
        where = y_off * 2 + lax.rem(at_ref[Z] + half, 2)
        for place, cores in enumerate(places):

            @pl.when(where == place)
            def _(step=step, cores=cores):
                for core, pieces in enumerate(cores):
                    for j, (which, at) in enumerate(pieces):
                        copy(step, core, j, shards[which].at[*at]).start()

    heads, _, _ = g_ref.shape
    for h in range(heads):
        for j in range(kinds):
            at = (j * heads + h) * HS
            flat_ref[at : at + HS, :] = g_ref[h, :, j * HS : (j + 1) * HS].T
    total = sum(
        g_ref[h, :, j * HS : (j + 1) * HS].astype(F32)
        * p_ref[h, :, j * HS : (j + 1) * HS].astype(F32)
        for h in range(heads)
        for j in range(kinds)
    )
    stat = jnp.sum(total.T, axis=0, keepdims=True) * (1.0 / width)
    stat_ref[...] = stat
    for ref in outs:
        if ref.shape[0] % 128:
            write_stat(ref, ref.shape[0] - 16, stat)

    for step, (which, at) in enumerate(spots):
        for core in range(2):
            for j in range(kinds):
                copy(step, core, j, shards[0].at[0]).wait()
        total = sum(
            dot(w_ref[step, j], flat_ref[j * cols : (j + 1) * cols, :], 1, 0)
            for j in range(kinds)
        )
        outs[which][at : at + depth, :] = total.astype(BF)


def norm_halves(ids, grads, proj, shards, places, halves, spots, sizes, width, after=()):
    heads, rows, _ = grads.shape
    kinds = 3
    band, cols = shards[0].shape[-2:]
    n = len(spots)
    sizes = (*sizes, 1)
    vmem = pl.BlockSpec(memory_space=pltpu.VMEM)
    free = pl.BlockSpec(memory_space=pl.ANY)
    return pl.pallas_call(
        functools.partial(norm_kernel, width, halves, spots, places, len(shards)),
        in_specs=[pl.BlockSpec(memory_space=pltpu.SMEM), vmem, vmem]
        + [free] * (len(shards) + len(after)),
        out_specs=(vmem,) * len(sizes),
        out_shape=tuple(shape(s, rows) for s in sizes[:-1]) + (shape(1, rows, dtype=F32),),
        scratch_shapes=[
            pltpu.VMEM((n, kinds, 2 * band, cols), BF),
            pltpu.VMEM((kinds * cols, rows), BF),
            pltpu.SemaphoreType.DMA((n, 2, kinds)),
        ],
        compiler_params=PARAMS,
        cost_estimate=cost(1, 1),
    )(ids, grads, proj, *shards, *after)


def add_kernel(up_part, up_in, stat_in, down_part, down_in, stat_ref, *refs):
    up_out, down_out = refs[-2:]
    half = up_part.shape[0]
    for part, came, out in ((up_part, up_in, up_out), (down_part, down_in, down_out)):
        out[:half, :] = (part[...].astype(F32) + came[...].astype(F32)).astype(BF)
    write_stat(up_out, half, stat_ref[...] + read_stat(stat_in, 0))
    write_stat(down_out, half, stat_ref[...])


def add_messages(up_part, up_in, down_part, down_in, stat, after=()):
    half, rows = up_part.shape
    block = pl.BlockSpec((half, rows), lambda i: (0, 0))
    out = pl.BlockSpec((half + 16, rows), lambda i: (0, 0))
    end = pl.BlockSpec((16, rows), lambda i: (2 * half // 16, 0))
    return pl.pallas_call(
        add_kernel,
        grid=(1,),
        out_shape=(shape(half + 16, rows),) * 2,
        in_specs=[block, block, end, block, block, pl.BlockSpec((1, rows), lambda i: (0, 0))]
        + [pl.BlockSpec(memory_space=pl.ANY)] * len(after),
        out_specs=(out, out),
        compiler_params=PARAMS,
        cost_estimate=cost(1, 1),
    )(up_part, up_in, up_in, down_part, down_in, stat, *after)


def finish_kernel(at_ref, own0, own1, up0, up1, down0, down1, tok_ref, root_ref, stat_ref, out_ref):
    half = own0.shape[0]
    stat = stat_ref[...] + read_stat(up0, half) + read_stat(down1, half)
    stat = jnp.broadcast_to(stat, (HS, stat.shape[1])).T[:, 0:1]
    root = root_ref[...]
    parts = (
        (own0[...], up0[:half, :], down0[half : 2 * half, :]),
        (own1[...], up1[half : 2 * half, :], down1[:half, :]),
    )
    for i, part in enumerate(parts):
        span = slice(i * half, (i + 1) * half)
        total = sum(p.astype(F32) for p in part)
        unit = tok_ref[:, span].astype(F32) / root
        out_ref[:, span] = ((total.T - unit * stat) / root).astype(BF)


def finish(ids, parts, tokens, root, stat):
    half, rows = parts[0].shape
    share = 2 * half
    tile = HS
    some = lambda a: pl.BlockSpec((a.shape[0], tile), lambda i, at: (0, i))
    return pl.pallas_call(
        finish_kernel,
        grid_spec=pltpu.PrefetchScalarGridSpec(
            num_scalar_prefetch=1,
            grid=(rows // tile,),
            in_specs=[some(p) for p in parts]
            + [pl.BlockSpec((tile, share), lambda i, at: (i, at[T]))]
            + [pl.BlockSpec((tile, 1), lambda i, at: (i, 0)), some(stat)],
            out_specs=pl.BlockSpec((tile, share), lambda i, at: (i, 0)),
        ),
        out_shape=shape(rows, share),
        compiler_params=PARAMS,
        cost_estimate=cost(1, 1),
    )(ids, *parts, tokens, root, stat)


def outer_kernel(tile, blocks_any, mine_ref, other_ref, out_ref, a_ref, g_ref, sems):
    n, rows, _ = mine_ref.shape
    depth = a_ref.shape[0]
    copies = []
    for step in range(depth // tile):
        span = pl.ds(step * tile, tile)
        some = []
        for i in range(2 * n):
            to = a_ref.at[span, pl.ds(i * rows, rows)]
            some.append(pltpu.make_async_copy(blocks_any.at[i, span], to, sems.at[step, i]))
            some[-1].start()
        copies.append(some)
    for i in range(n):
        g_ref[2 * i * rows : (2 * i + 1) * rows, :] = mine_ref[i]
        g_ref[(2 * i + 1) * rows : (2 * i + 2) * rows, :] = other_ref[i]
    for step, some in enumerate(copies):
        for copy in some:
            copy.wait()
        span = slice(step * tile, (step + 1) * tile)
        out_ref[span, :] = jnp.dot(
            a_ref[span, :], g_ref[...], preferred_element_type=F32
        ).astype(BF)


def outer(blocks, mine, other):
    n, depth, rows = blocks.shape
    cols = mine.shape[2]
    tile = 512
    vmem = pl.BlockSpec(memory_space=pltpu.VMEM)
    return pl.pallas_call(
        functools.partial(outer_kernel, tile),
        in_specs=[pl.BlockSpec(memory_space=pl.ANY), vmem, vmem],
        out_specs=vmem,
        out_shape=shape(depth, cols),
        scratch_shapes=[
            pltpu.VMEM((depth, n * rows), BF),
            pltpu.VMEM((n * rows, cols), BF),
            pltpu.SemaphoreType.DMA((depth // tile, n)),
        ],
        compiler_params=PARAMS,
        cost_estimate=cost(1, 1),
    )(blocks, mine, other)


def split_kernel(at_ref, part_ref, *refs):
    keep_ref, give_ref = refs[-2:]
    n, _, rows, _ = part_ref.shape
    for ref, which in ((keep_ref, at_ref[Z]), (give_ref, 1 - at_ref[Z])):
        ref[...] = sum(part_ref[i, which].astype(F32) for i in range(n)).astype(ref.dtype)


def split(ids, part, after=()):
    _, _, rows, cols = part.shape
    vmem = pl.BlockSpec(memory_space=pltpu.VMEM)
    return pl.pallas_call(
        split_kernel,
        in_specs=[pl.BlockSpec(memory_space=pltpu.SMEM), vmem]
        + [pl.BlockSpec(memory_space=pl.ANY)] * len(after),
        out_specs=(vmem, vmem),
        out_shape=(shape(rows, cols, dtype=F32), shape(rows, cols)),
        compiler_params=PARAMS,
        cost_estimate=cost(1, 1),
    )(ids, part, *after)


def merge_kernel(keep_ref, came_ref, att_ref, *refs):
    out_ref = refs[-1]
    total = (keep_ref[...] + came_ref[...].astype(F32)).astype(BF)
    cols = total.shape[1]
    for i in range(out_ref.shape[0]):
        out_ref[i, :, :cols] = total
        out_ref[i, :, cols:] = att_ref[i]


def merge(keep, came, att, after=()):
    rows, cols = keep.shape
    n, _, more = att.shape
    vmem = pl.BlockSpec(memory_space=pltpu.VMEM)
    return pl.pallas_call(
        merge_kernel,
        out_shape=shape(n, rows, cols + more),
        in_specs=[vmem] * 3 + [pl.BlockSpec(memory_space=pl.ANY)] * len(after),
        out_specs=vmem,
        compiler_params=PARAMS,
        cost_estimate=cost(1, 1),
    )(keep, came, att, *after)


def unpack_kernel(in_ref, w_ref, att_ref):
    for h in range(in_ref.shape[0]):
        span = slice(h * HS, (h + 1) * HS)
        for j in range(3):
            w_ref[j, :, span] = in_ref[h, :, j * HS : (j + 1) * HS].astype(F32)
        att_ref[:, span] = in_ref[h, :, 3 * HS :]


def unpack(last):
    heads, rows, more = last.shape
    tile = rows // 4
    return pl.pallas_call(
        unpack_kernel,
        grid=(rows // tile,),
        in_specs=[pl.BlockSpec((heads, tile, more), lambda i: (0, i, 0))],
        out_specs=(
            pl.BlockSpec((3, tile, heads * HS), lambda i: (0, i, 0)),
            pl.BlockSpec((tile, heads * HS), lambda i: (i, 0)),
        ),
        out_shape=(shape(3, rows, heads * HS, dtype=F32), shape(rows, heads * HS)),
        compiler_params=PARAMS,
        cost_estimate=cost(1, 1),
    )(last)


def gate(arrays, after=(), pieces=()):
    n, m = len(arrays), len(arrays) + len(after)
    free = pl.BlockSpec(memory_space=pl.ANY)

    def kernel(*refs):
        outs, sems = refs[m + n : -1], refs[-1]
        copies = [
            pltpu.make_async_copy(refs[which].at[pl.ds(at, 1)], out, sems.at[i])
            for i, ((which, at), out) in enumerate(zip(pieces, outs))
        ]
        for copy in copies:
            copy.start()
        for copy in copies:
            copy.wait()

    return pl.pallas_call(
        kernel,
        in_specs=[free] * m,
        out_specs=(free,) * (n + len(pieces)),
        out_shape=tuple(shape(*a.shape) for a in arrays)
        + tuple(shape(1, *arrays[which].shape[1:]) for which, _ in pieces),
        scratch_shapes=[pltpu.SemaphoreType.DMA((max(len(pieces), 1),))],
        input_output_aliases={i: i for i in range(n)},
        compiler_params=PARAMS,
        cost_estimate=cost(1, 1),
    )(*arrays, *after)


def shift(x, axis, by):
    n = lax.axis_size(axis)
    return lax.ppermute(x, axis, [(i, (i + by) % n) for i in range(n)])


def per_device(tokens, weights, cotangent):
    _, rows, width = tokens.shape
    w_rows, _, cols = weights.shape
    heads = cols // HS
    n_x, n_y = (lax.axis_size(a) for a in ("x", "y"))
    ids = jnp.stack([lax.axis_index(a) for a in ("core", "x", "zh", "y", "zl")])
    tokens = tokens.reshape(rows, width)
    half = width // lax.axis_size("zh") // 2

    swap = lambda a: shift(a, "core", 1)
    own = weights.transpose(1, 0, 2)
    left, right, other = shift(own, "y", 1), shift(own, "y", -1), shift(own, "zl", 1)
    root, mine, given, theirs, pair = unit_rows(ids, tokens, swap(tokens), w_rows)
    left, right, other = gate((left, right, other), (pair,))

    blocks = lax.all_gather(pair, "x", axis=0, tiled=True)

    dout = cotangent.reshape(rows, heads, HS).transpose(1, 0, 2)
    dout = lax.all_to_all(dout, "x", 0, 0, tiled=True).reshape(n_x * rows, HS)
    near = ((0, 0), (3, 0), (1, 0), (0, 1))
    *sums, stack_0 = project(ids, mine, theirs, (own, left, right, other), near)
    far, other_left, other_right, *pieces = gate(
        (shift(left, "y", 1), shift(left, "zl", 1), shift(other, "y", -1)),
        (dout, *sums),
        ((0, 0), (1, 1), (2, 2)),
    )
    then = ((2, 0), (3, 1), (1, 1))
    keep, give, stack_1 = project(
        ids, mine, theirs, (far, other_left, other_right), then, sums, BF
    )
    *pieces, give = gate(
        (shift(pieces[0], "zl", 1), shift(pieces[1], "y", 1), shift(pieces[2], "y", -1), give)
    )
    pieces = (*pieces, *(swap(p) for p in pieces))
    proj = project_last(ids, mine, given, keep, swap(give), pieces, (2, 1), heads)

    shards = (*pieces, stack_0, swap(stack_0), stack_1, swap(stack_1))
    places = {(2, 1): [[(3 * core + j, (0,)) for j in range(3)] for core in range(2)]}
    for first, keys in ((6, near), (8, then)):
        for i, key in enumerate(keys):
            places[key] = [[(first + core, (i, j)) for j in range(3)] for core in range(2)]
    places = [places[(by, z)] for by in range(n_y) for z in range(2)]
    qkv = lax.all_to_all(proj, "x", 0, 0, tiled=True).reshape(n_x * rows, 3 * HS)
    att, head_grads = attention(qkv, dout)

    head_grads = head_grads.reshape(n_x, rows, 3 * HS)
    grads = lax.all_to_all(head_grads, "x", 0, 0, tiled=True)
    part = outer(blocks, head_grads, swap(head_grads))

    up, down, stat = norm_halves(
        ids, grads, proj, shards, places,
        ((2, 0), (1, 1), (2, 1), (3, 0)),
        ((0, 0), (0, half), (1, 0), (1, half)),
        (2 * half + 16, 2 * half),
        width,
    )
    up, down = shift(up, "zh", 1), shift(down, "zh", -1)
    up_part, down_part, own0, own1, _ = norm_halves(
        ids, grads, proj, shards, places,
        ((1, 0), (3, 1), (0, 0), (0, 1)),
        ((0, 0), (1, 0), (2, 0), (3, 0)),
        (half,) * 4,
        width,
        (stat,),
    )
    part = lax.all_to_all(part, "y", 0, 0, tiled=True).reshape(n_y, 2, w_rows, 3 * HS)
    keep, give = split(ids, part, (own0,))
    came = shift(give, "zl", 1)
    up_2, down_2 = add_messages(up_part, up, down_part, down, stat, (give,))
    last = merge(keep, came, att.reshape(n_x, rows, HS), (up_2,))
    up_2, down_2 = shift(up_2, "zh", 1), shift(down_2, "zh", -1)
    last = lax.all_to_all(last, "x", 0, 0, tiled=True)
    token_grad = finish(ids, (own0, own1, up_2, up, down, down_2), tokens, root, stat)
    weight_grad, attended = unpack(last)
    return attended[None], token_grad[None], weight_grad.transpose(1, 0, 2)


def solution(mesh):
    fine = Mesh(mesh.devices.reshape(4, 2, 2, 4, 4), ("y", "zl", "core", "x", "zh"))
    dp = ("y", "zl", "core")
    return jax.shard_map(
        per_device,
        mesh=fine,
        in_specs=(P(dp, "x", None), P(dp, None, "zh"), P(dp, "x", "zh")),
        out_specs=(P(dp, "x", "zh"), P(dp, "x", "zh"), P(dp, None, "zh")),
        check_vma=False,
    )
```

```python
import functools
import math

import jax
import jax.numpy as jnp
from jax import lax
from jax.experimental import pallas as pl
from jax.experimental.pallas import tpu as pltpu
from jax.sharding import Mesh
from jax.sharding import PartitionSpec as P

HS = 128
CORE, X, T, Y, Z = range(5)
BF = jnp.bfloat16
BUSY = 2 * 10**10
F32 = jnp.float32
PARAMS = pltpu.CompilerParams(vmem_limit_bytes=60 * 1024 * 1024)


def dot(a, b, ca, cb):
    return lax.dot_general(a, b, (((ca,), (cb,)), ((), ())), preferred_element_type=F32)


def cost(flops, nbytes, exps=0):
    return pl.CostEstimate(flops=flops, bytes_accessed=nbytes, transcendentals=exps)


def shape(*dims, dtype=BF):
    return jax.ShapeDtypeStruct(dims, dtype)


def unit_kernel(at_ref, tok_ref, other_ref, root_ref, mine_ref, given_ref, theirs_ref, both_ref, *, band):
    core = at_ref[CORE]
    for n, ref in enumerate((tok_ref, other_ref)):
        tok = ref[...].astype(F32)
        root = jnp.sqrt(jnp.mean(tok * tok, -1, keepdims=True) + 1e-05)
        outs = [(theirs_ref, core)]
        if n == 0:
            root_ref[...] = root
            outs = [(mine_ref, core), (given_ref, 1 - core)]
        for i in range(mine_ref.shape[1] // band):
            for k, (out, which) in enumerate(outs):
                at = pl.multiple_of((2 * i + which) * band, band)
                unit = (ref[:, pl.ds(at, band)].astype(F32) / root).astype(BF)
                out[:, i * band : (i + 1) * band] = unit
                if k == 0:
                    both_ref[n, i * band : (i + 1) * band, :] = unit.T


def unit_rows(ids, tokens, others, band):
    rows, width = tokens.shape
    tile = 128
    half = width // 2
    row = pl.BlockSpec((tile, width), lambda i, at: (i, 0))
    return pl.pallas_call(
        functools.partial(unit_kernel, band=band),
        grid_spec=pltpu.PrefetchScalarGridSpec(
            num_scalar_prefetch=1,
            grid=(rows // tile,),
            in_specs=[row, row],
            out_specs=(pl.BlockSpec((tile, 1), lambda i, at: (i, 0)),)
            + (pl.BlockSpec((tile, half), lambda i, at: (i, 0)),) * 3
            + (pl.BlockSpec((2, half, tile), lambda i, at: (0, 0, i)),),
        ),
        out_shape=(shape(rows, 1, dtype=F32),)
        + (shape(rows, half),) * 3
        + (shape(2, half, rows),),
        compiler_params=PARAMS,
        cost_estimate=cost(BUSY, 1),
    )(ids, tokens, others)


def project_kernel(offsets, first, at_ref, mine_ref, theirs_ref, *refs):
    keep_ref, give_ref, stack_ref, sems = refs[-4:]
    n = len(offsets)
    shards, sums = refs[:n], refs[n:-4]
    copies = [pltpu.make_async_copy(w, stack_ref.at[i], sems.at[i]) for i, w in enumerate(shards)]
    for copy in copies:
        copy.start()
    kinds, depth, cols = shards[0].shape
    bands = [
        pl.ds(pl.multiple_of(place_of(at_ref, *offset) * depth, depth), depth) for offset in offsets
    ]
    for i, (rows, out) in enumerate(((mine_ref, keep_ref), (theirs_ref, give_ref))):
        for j in range(kinds):
            span = slice(j * cols, (j + 1) * cols)
            total = None if first else sums[i][:, span]
            for band, shard in zip(bands, shards):
                part = jnp.dot(rows[:, band], shard[j], preferred_element_type=F32)
                total = part if total is None else total + part
            out[:, span] = total.astype(out.dtype)
    for copy in copies:
        copy.wait()


def place_of(at_ref, y, z):
    return lax.rem(at_ref[Y] + y, 4) * 2 + lax.rem(at_ref[Z] + z, 2)


def project(ids, mine, theirs, shards, offsets, sums=(), give=F32):
    rows, _ = mine.shape
    n = len(shards)
    vmem = pl.BlockSpec(memory_space=pltpu.VMEM)
    cols = 3 * shards[0].shape[-1]
    return pl.pallas_call(
        functools.partial(project_kernel, offsets, not sums),
        in_specs=[pl.BlockSpec(memory_space=pltpu.SMEM)] + [vmem] * (2 + n + len(sums)),
        out_specs=(vmem, vmem, pl.BlockSpec(memory_space=pl.ANY)),
        out_shape=(
            shape(rows, cols, dtype=F32),
            shape(rows, cols, dtype=give),
            shape(n, *shards[0].shape),
        ),
        scratch_shapes=[pltpu.SemaphoreType.DMA((n,))],
        compiler_params=PARAMS,
        cost_estimate=cost(1, 1),
    )(ids, mine, theirs, *shards, *sums)


def project_last_kernel(offset, at_ref, mine_ref, given_ref, keep_ref, came_ref, *refs):
    shards, heads_ref = refs[:-1], refs[-1]
    depth, cols = shards[0].shape[-2:]
    band = pl.ds(pl.multiple_of(place_of(at_ref, *offset) * depth, depth), depth)
    for j in range(3):
        span = slice(j * cols, (j + 1) * cols)
        total = keep_ref[:, span] + came_ref[:, span].astype(F32)
        total += jnp.dot(mine_ref[:, band], shards[j][0], preferred_element_type=F32)
        total += jnp.dot(given_ref[:, band], shards[3 + j][0], preferred_element_type=F32)
        for h in range(heads_ref.shape[0]):
            heads_ref[h, :, j * HS : (j + 1) * HS] = total[:, h * HS : (h + 1) * HS].astype(BF)


def project_last(ids, mine, given, keep, came, pieces, offset, heads):
    rows, cols = keep.shape
    vmem = pl.BlockSpec(memory_space=pltpu.VMEM)
    return pl.pallas_call(
        functools.partial(project_last_kernel, offset),
        in_specs=[pl.BlockSpec(memory_space=pltpu.SMEM)] + [vmem] * (4 + len(pieces)),
        out_specs=vmem,
        out_shape=shape(heads, rows, cols // heads),
        compiler_params=PARAMS,
        cost_estimate=cost(1, 1),
    )(ids, mine, given, keep, came, *pieces)


def attention_kernel(q_rows, carried, qkv_ref, dout_ref, *refs):
    att_ref, grad_ref = refs[-4 - carried : -2 - carried]
    dk_ref, dv_ref = refs[-2:]
    scale = 1.0 / math.sqrt(HS)
    key = qkv_ref[:, HS : 2 * HS]
    value = qkv_ref[:, 2 * HS : 3 * HS]
    key_t = key.T
    value_t = value.T
    for i in range(qkv_ref.shape[0] // q_rows):
        rows = pl.ds(i * q_rows, q_rows)
        query = qkv_ref[rows, 0:HS]
        dout = dout_ref[rows, :]
        scores = dot(key, query, 1, 1) * (scale * math.log2(math.e))
        top = jnp.max(scores, axis=0, keepdims=True)
        expo = jnp.exp2(scores - top)
        prob = expo * (1.0 / jnp.sum(expo, axis=0, keepdims=True))
        prob_bf = prob.astype(BF)
        att = dot(value_t, prob_bf, 1, 0).T.astype(BF)
        att_ref[rows, :] = att
        row_dot = jnp.sum(
            dout.astype(F32).T * att.astype(F32).T, axis=0, keepdims=True
        )
        dprob = dot(value, dout, 1, 1)
        dscore = (prob * (dprob - row_dot)).astype(BF)
        grad_ref[rows, 0:HS] = (dot(key_t, dscore, 1, 0) * scale).T.astype(BF)
        dv = dot(prob_bf, dout, 1, 0)
        dk = dot(dscore, query, 1, 0)
        if i == 0:
            dv_ref[...] = dv
            dk_ref[...] = dk
        else:
            dv_ref[...] += dv
            dk_ref[...] += dk
    grad_ref[:, HS : 2 * HS] = (dk_ref[...] * scale).astype(BF)
    grad_ref[:, 2 * HS : 3 * HS] = dv_ref[...].astype(BF)


def attention(qkv, dout, carry, after):
    n = qkv.shape[0]
    vmem = pl.BlockSpec(memory_space=pltpu.VMEM)
    free = pl.BlockSpec(memory_space=pl.ANY)
    return pl.pallas_call(
        functools.partial(attention_kernel, min(256, n), len(carry)),
        out_shape=(shape(n, HS), shape(n, 3 * HS)) + tuple(shape(*c.shape) for c in carry),
        in_specs=[vmem] * 2 + [free] * (len(carry) + len(after)),
        out_specs=(vmem,) * 2 + (free,) * len(carry),
        scratch_shapes=[pltpu.VMEM((n, HS), F32), pltpu.VMEM((n, HS), F32)],
        input_output_aliases={2 + i: 2 + i for i in range(len(carry))},
        compiler_params=PARAMS,
        cost_estimate=cost(BUSY, 1),
    )(qkv, dout, *carry, *after)


def write_stat(ref, at, stat):
    ref[at:, :] = jnp.zeros((ref.shape[0] - at, ref.shape[1]), BF)
    rest = stat
    for i in range(3):
        top = rest.astype(BF)
        ref[at + i : at + i + 1, :] = top
        rest = rest - top.astype(F32)


def read_stat(ref, at):
    return sum(ref[at + i : at + i + 1, :].astype(F32) for i in range(3))


def norm_kernel(width, halves, spots, places, n_in, at_ref, g_ref, p_ref, *refs):
    shards = refs[:n_in]
    n_out = max(spot[0] for spot in spots) + 1
    outs, stat_ref = refs[-4 - n_out : -4], refs[-4]
    w_ref, flat_ref, sems = refs[-3:]
    _, kinds, depth, cols = w_ref.shape
    band = depth // 2
    quarters = len(places) // 2

    def copy(step, core, j, source):
        to = lax.rem(at_ref[CORE] + core, 2)
        at = pl.ds(pl.multiple_of(to * band, band), band)
        return pltpu.make_async_copy(source, w_ref.at[step, j, at], sems.at[step, core, j])

    for step, (by, half) in enumerate(halves):
        y_off = lax.rem(at_ref[T] + (by + quarters) - at_ref[Y], quarters)
        where = y_off * 2 + lax.rem(at_ref[Z] + half, 2)
        for place, cores in enumerate(places):

            @pl.when(where == place)
            def _(step=step, cores=cores):
                for core, pieces in enumerate(cores):
                    for j, (which, at) in enumerate(pieces):
                        copy(step, core, j, shards[which].at[*at]).start()

    heads, _, _ = g_ref.shape
    for h in range(heads):
        for j in range(kinds):
            at = (j * heads + h) * HS
            flat_ref[at : at + HS, :] = g_ref[h, :, j * HS : (j + 1) * HS].T
    total = sum(
        g_ref[h, :, j * HS : (j + 1) * HS].astype(F32)
        * p_ref[h, :, j * HS : (j + 1) * HS].astype(F32)
        for h in range(heads)
        for j in range(kinds)
    )
    stat = jnp.sum(total.T, axis=0, keepdims=True) * (1.0 / width)
    stat_ref[...] = stat
    for ref in outs:
        if ref.shape[0] % 128:
            write_stat(ref, ref.shape[0] - 16, stat)

    for step, (which, at) in enumerate(spots):
        for core in range(2):
            for j in range(kinds):
                copy(step, core, j, shards[0].at[0]).wait()
        total = sum(
            dot(w_ref[step, j], flat_ref[j * cols : (j + 1) * cols, :], 1, 0)
            for j in range(kinds)
        )
        outs[which][at : at + depth, :] = total.astype(BF)


def norm_halves(ids, grads, proj, shards, places, halves, spots, sizes, width, after=()):
    heads, rows, _ = grads.shape
    kinds = 3
    band, cols = shards[0].shape[-2:]
    n = len(spots)
    sizes = (*sizes, 1)
    vmem = pl.BlockSpec(memory_space=pltpu.VMEM)
    free = pl.BlockSpec(memory_space=pl.ANY)
    return pl.pallas_call(
        functools.partial(norm_kernel, width, halves, spots, places, len(shards)),
        in_specs=[pl.BlockSpec(memory_space=pltpu.SMEM), vmem, vmem]
        + [free] * (len(shards) + len(after)),
        out_specs=(vmem,) * len(sizes),
        out_shape=tuple(shape(s, rows) for s in sizes[:-1]) + (shape(1, rows, dtype=F32),),
        scratch_shapes=[
            pltpu.VMEM((n, kinds, 2 * band, cols), BF),
            pltpu.VMEM((kinds * cols, rows), BF),
            pltpu.SemaphoreType.DMA((n, 2, kinds)),
        ],
        compiler_params=PARAMS,
        cost_estimate=cost(1, 1),
    )(ids, grads, proj, *shards, *after)


def add_kernel(up_part, up_in, stat_in, down_part, down_in, stat_ref, *refs):
    up_out, down_out = refs[-2:]
    half = up_part.shape[0]
    for part, came, out in ((up_part, up_in, up_out), (down_part, down_in, down_out)):
        out[:half, :] = (part[...].astype(F32) + came[...].astype(F32)).astype(BF)
    write_stat(up_out, half, stat_ref[...] + read_stat(stat_in, 0))
    write_stat(down_out, half, stat_ref[...])


def add_messages(up_part, up_in, down_part, down_in, stat, after=()):
    half, rows = up_part.shape
    block = pl.BlockSpec((half, rows), lambda i: (0, 0))
    out = pl.BlockSpec((half + 16, rows), lambda i: (0, 0))
    end = pl.BlockSpec((16, rows), lambda i: (2 * half // 16, 0))
    return pl.pallas_call(
        add_kernel,
        grid=(1,),
        out_shape=(shape(half + 16, rows),) * 2,
        in_specs=[block, block, end, block, block, pl.BlockSpec((1, rows), lambda i: (0, 0))]
        + [pl.BlockSpec(memory_space=pl.ANY)] * len(after),
        out_specs=(out, out),
        compiler_params=PARAMS,
        cost_estimate=cost(1, 1),
    )(up_part, up_in, up_in, down_part, down_in, stat, *after)


def finish_kernel(at_ref, own0, own1, up0, up1, down0, down1, tok_ref, root_ref, stat_ref, *refs):
    out_ref = refs[-1]
    half = own0.shape[0]
    stat = stat_ref[...] + read_stat(up0, half) + read_stat(down1, half)
    stat = jnp.broadcast_to(stat, (HS, stat.shape[1])).T[:, 0:1]
    root = root_ref[...]
    parts = (
        (own0[...], up0[:half, :], down0[half : 2 * half, :]),
        (own1[...], up1[half : 2 * half, :], down1[:half, :]),
    )
    for i, part in enumerate(parts):
        span = slice(i * half, (i + 1) * half)
        total = sum(p.astype(F32) for p in part)
        unit = tok_ref[:, span].astype(F32) / root
        out_ref[:, span] = ((total.T - unit * stat) / root).astype(BF)


def finish(ids, parts, tokens, root, stat, after=()):
    half, rows = parts[0].shape
    share = 2 * half
    tile = HS
    some = lambda a: pl.BlockSpec((a.shape[0], tile), lambda i, at: (0, i))
    return pl.pallas_call(
        finish_kernel,
        grid_spec=pltpu.PrefetchScalarGridSpec(
            num_scalar_prefetch=1,
            grid=(rows // tile,),
            in_specs=[some(p) for p in parts]
            + [pl.BlockSpec((tile, share), lambda i, at: (i, at[T]))]
            + [pl.BlockSpec((tile, 1), lambda i, at: (i, 0)), some(stat)]
            + [pl.BlockSpec(memory_space=pl.ANY)] * len(after),
            out_specs=pl.BlockSpec((tile, share), lambda i, at: (i, 0)),
        ),
        out_shape=shape(rows, share),
        compiler_params=PARAMS,
        cost_estimate=cost(BUSY, 1),
    )(ids, *parts, tokens, root, stat, *after)


def outer_kernel(tile, spots, at_ref, *refs):
    arrays, (mine_ref, other_ref, out_ref, a_ref, g_ref, sems) = refs[:-6], refs[-6:]
    n, rows, _ = mine_ref.shape
    depth = a_ref.shape[0]
    copies = []
    for step in range(depth // tile):
        span = pl.ds(step * tile, tile)
        some = []
        for i, (which, at, _, _) in enumerate(spots):
            to = a_ref.at[span, pl.ds(i * rows, rows)]
            some.append(pltpu.make_async_copy(arrays[which].at[at, span], to, sems.at[step, i]))
            some[-1].start()
        copies.append(some)
    for i, (_, _, by, frame) in enumerate(spots):
        ref = other_ref if frame else mine_ref
        g_ref[i * rows : (i + 1) * rows, :] = ref[lax.rem(at_ref[X] + by, n)]
    for step, some in enumerate(copies):
        for copy in some:
            copy.wait()
        span = slice(step * tile, (step + 1) * tile)
        out_ref[span, :] = jnp.dot(
            a_ref[span, :], g_ref[...], preferred_element_type=F32
        ).astype(BF)


def outer(ids, arrays, spots, mine, other):
    _, depth, rows = arrays[0].shape
    cols = mine.shape[2]
    n = len(spots)
    tile = 512
    vmem = pl.BlockSpec(memory_space=pltpu.VMEM)
    return pl.pallas_call(
        functools.partial(outer_kernel, tile, spots),
        in_specs=[pl.BlockSpec(memory_space=pltpu.SMEM)]
        + [pl.BlockSpec(memory_space=pl.ANY)] * len(arrays)
        + [vmem, vmem],
        out_specs=vmem,
        out_shape=shape(depth, cols),
        scratch_shapes=[
            pltpu.VMEM((depth, n * rows), BF),
            pltpu.VMEM((n * rows, cols), BF),
            pltpu.SemaphoreType.DMA((depth // tile, n)),
        ],
        compiler_params=PARAMS,
        cost_estimate=cost(1, 1),
    )(ids, *arrays, mine, other)


def split_kernel(at_ref, part_ref, *refs):
    keep_ref, give_ref = refs[-2:]
    n, _, rows, _ = part_ref.shape
    for ref, which in ((keep_ref, at_ref[Z]), (give_ref, 1 - at_ref[Z])):
        ref[...] = sum(part_ref[i, which].astype(F32) for i in range(n)).astype(ref.dtype)


def split(ids, part, after=()):
    _, _, rows, cols = part.shape
    vmem = pl.BlockSpec(memory_space=pltpu.VMEM)
    return pl.pallas_call(
        split_kernel,
        in_specs=[pl.BlockSpec(memory_space=pltpu.SMEM), vmem]
        + [pl.BlockSpec(memory_space=pl.ANY)] * len(after),
        out_specs=(vmem, vmem),
        out_shape=(shape(rows, cols, dtype=F32), shape(rows, cols)),
        compiler_params=PARAMS,
        cost_estimate=cost(1, 1),
    )(ids, part, *after)


def merge_kernel(keep_ref, came_ref, att_ref, *refs):
    out_ref = refs[-1]
    total = (keep_ref[...] + came_ref[...].astype(F32)).astype(BF)
    cols = total.shape[1]
    for i in range(out_ref.shape[0]):
        out_ref[i, :, :cols] = total
        out_ref[i, :, cols:] = att_ref[i]


def merge(keep, came, att, after=()):
    rows, cols = keep.shape
    n, _, more = att.shape
    vmem = pl.BlockSpec(memory_space=pltpu.VMEM)
    return pl.pallas_call(
        merge_kernel,
        out_shape=shape(n, rows, cols + more),
        in_specs=[vmem] * 3 + [pl.BlockSpec(memory_space=pl.ANY)] * len(after),
        out_specs=vmem,
        compiler_params=PARAMS,
        cost_estimate=cost(1, 1),
    )(keep, came, att, *after)


def unpack_kernel(in_ref, w_ref, att_ref):
    for h in range(in_ref.shape[0]):
        span = slice(h * HS, (h + 1) * HS)
        for j in range(3):
            w_ref[j, :, span] = in_ref[h, :, j * HS : (j + 1) * HS].astype(F32)
        att_ref[:, span] = in_ref[h, :, 3 * HS :]


def unpack(last):
    heads, rows, more = last.shape
    tile = rows // 4
    return pl.pallas_call(
        unpack_kernel,
        grid=(rows // tile,),
        in_specs=[pl.BlockSpec((heads, tile, more), lambda i: (0, i, 0))],
        out_specs=(
            pl.BlockSpec((3, tile, heads * HS), lambda i: (0, i, 0)),
            pl.BlockSpec((tile, heads * HS), lambda i: (i, 0)),
        ),
        out_shape=(shape(3, rows, heads * HS, dtype=F32), shape(rows, heads * HS)),
        compiler_params=PARAMS,
        cost_estimate=cost(1, 1),
    )(last)


def gate(arrays, after=(), pieces=()):
    n, m = len(arrays), len(arrays) + len(after)
    free = pl.BlockSpec(memory_space=pl.ANY)

    def kernel(*refs):
        outs, sems = refs[m + n : -1], refs[-1]
        copies = [
            pltpu.make_async_copy(refs[which].at[pl.ds(at, 1)], out, sems.at[i])
            for i, ((which, at), out) in enumerate(zip(pieces, outs))
        ]
        for copy in copies:
            copy.start()
        for copy in copies:
            copy.wait()

    return pl.pallas_call(
        kernel,
        in_specs=[free] * m,
        out_specs=(free,) * n + (pl.BlockSpec(memory_space=pltpu.VMEM),) * len(pieces),
        out_shape=tuple(shape(*a.shape) for a in arrays)
        + tuple(shape(1, *arrays[which].shape[1:]) for which, _ in pieces),
        scratch_shapes=[pltpu.SemaphoreType.DMA((max(len(pieces), 1),))],
        input_output_aliases={i: i for i in range(n)},
        compiler_params=PARAMS,
        cost_estimate=cost(1, 1),
    )(*arrays, *after)


def shift(x, axis, by):
    n = lax.axis_size(axis)
    return lax.ppermute(x, axis, [(i, (i + by) % n) for i in range(n)])


def per_device(tokens, weights, cotangent):
    _, rows, width = tokens.shape
    w_rows, _, cols = weights.shape
    heads = cols // HS
    n_x, n_y = (lax.axis_size(a) for a in ("x", "y"))
    ids = jnp.stack([lax.axis_index(a) for a in ("core", "x", "zh", "y", "zl")])
    tokens = tokens.reshape(rows, width)
    half = width // lax.axis_size("zh") // 2

    swap = lambda a: shift(a, "core", 1)
    own = weights.transpose(1, 0, 2)
    left, right, other = shift(own, "y", 1), shift(own, "y", -1), shift(own, "zl", 1)
    root, mine, given, theirs, pair = unit_rows(ids, tokens, swap(tokens), w_rows)
    left, right, other = gate((left, right, other), (pair,))

    x_left, x_right = shift(pair, "x", 1), shift(pair, "x", -1)

    dout = cotangent.reshape(rows, heads, HS).transpose(1, 0, 2)
    dout = lax.all_to_all(dout, "x", 0, 0, tiled=True).reshape(n_x * rows, HS)
    near = ((0, 0), (3, 0), (1, 0), (0, 1))
    *sums, stack_0 = project(ids, mine, theirs, (own, left, right, other), near)
    far, other_left, other_right, *pieces = gate(
        (shift(left, "y", 1), shift(left, "zl", 1), shift(other, "y", -1)),
        (dout, *sums),
        ((0, 0), (1, 1), (2, 2)),
    )
    then = ((2, 0), (3, 1), (1, 1))
    keep, give, stack_1 = project(
        ids, mine, theirs, (far, other_left, other_right), then, sums, BF
    )
    *pieces, give = gate(
        (shift(pieces[0], "zl", 1), shift(pieces[1], "y", 1), shift(pieces[2], "y", -1), give)
    )
    pieces = (*pieces, *(swap(p) for p in pieces))
    proj = project_last(ids, mine, given, keep, swap(give), pieces, (2, 1), heads)

    x_left, x_right, far_0, far_1 = gate((x_left, x_right), pieces=((0, 0), (1, 1)))
    far_0, far_1 = shift(far_0, "x", 1), shift(far_1, "x", -1)
    blocks = (pair, x_left, x_right, far_0, far_1)
    spots = ((0, 0, 0, 0), (0, 1, 0, 1), (1, 0, 3, 0), (1, 1, 3, 1), (2, 0, 1, 0), (2, 1, 1, 1), (3, 0, 2, 0), (4, 0, 2, 1))
    qkv = lax.all_to_all(proj, "x", 0, 0, tiled=True).reshape(n_x * rows, 3 * HS)
    att, head_grads, stack_0, stack_1 = attention(
        qkv, dout, (stack_0, stack_1), (far_0, far_1)
    )

    shards = (*pieces, stack_0, swap(stack_0), stack_1, swap(stack_1))
    places = {(2, 1): [[(3 * core + j, (0,)) for j in range(3)] for core in range(2)]}
    for first, keys in ((6, near), (8, then)):
        for i, key in enumerate(keys):
            places[key] = [[(first + core, (i, j)) for j in range(3)] for core in range(2)]
    places = [places[(by, z)] for by in range(n_y) for z in range(2)]

    head_grads = head_grads.reshape(n_x, rows, 3 * HS)
    grads = lax.all_to_all(head_grads, "x", 0, 0, tiled=True)
    part = outer(ids, blocks, spots, head_grads, swap(head_grads))

    up, down, stat = norm_halves(
        ids, grads, proj, shards, places,
        ((2, 0), (1, 1), (2, 1), (3, 0)),
        ((0, 0), (0, half), (1, 0), (1, half)),
        (2 * half + 16, 2 * half),
        width,
    )
    up, down = shift(up, "zh", 1), shift(down, "zh", -1)
    up_part, down_part, own0, own1, _ = norm_halves(
        ids, grads, proj, shards, places,
        ((1, 0), (3, 1), (0, 0), (0, 1)),
        ((0, 0), (1, 0), (2, 0), (3, 0)),
        (half,) * 4,
        width,
        (stat,),
    )
    part = lax.all_to_all(part, "y", 0, 0, tiled=True).reshape(n_y, 2, w_rows, 3 * HS)
    keep, give = split(ids, part, (own0,))
    came = shift(give, "zl", 1)
    up_2, down_2 = add_messages(up_part, up, down_part, down, stat, (came,))
    last = merge(keep, came, att.reshape(n_x, rows, HS))
    up_2, down_2 = shift(up_2, "zh", 1), shift(down_2, "zh", -1)
    last = lax.all_to_all(last, "x", 0, 0, tiled=True)
    token_grad = finish(ids, (own0, own1, up_2, up, down, down_2), tokens, root, stat)
    weight_grad, attended = unpack(last)
    return attended[None], token_grad[None], weight_grad.transpose(1, 0, 2)


def solution(mesh):
    fine = Mesh(mesh.devices.reshape(4, 2, 2, 4, 4), ("y", "zl", "core", "x", "zh"))
    dp = ("y", "zl", "core")
    return jax.shard_map(
        per_device,
        mesh=fine,
        in_specs=(P(dp, "x", None), P(dp, None, "zh"), P(dp, "x", "zh")),
        out_specs=(P(dp, "x", "zh"), P(dp, "x", "zh"), P(dp, None, "zh")),
        check_vma=False,
    )
```

```python
import functools
import math

import jax
import jax.numpy as jnp
from jax import lax
from jax.experimental import pallas as pl
from jax.experimental.pallas import tpu as pltpu
from jax.sharding import Mesh
from jax.sharding import PartitionSpec as P

HS = 128
CORE, X, T, Y, Z = range(5)
BF = jnp.bfloat16
BUSY = 2 * 10**10
F32 = jnp.float32
PARAMS = pltpu.CompilerParams(vmem_limit_bytes=60 * 1024 * 1024)


def dot(a, b, ca, cb):
    return lax.dot_general(a, b, (((ca,), (cb,)), ((), ())), preferred_element_type=F32)


def cost(flops, nbytes, exps=0):
    return pl.CostEstimate(flops=flops, bytes_accessed=nbytes, transcendentals=exps)


def shape(*dims, dtype=BF):
    return jax.ShapeDtypeStruct(dims, dtype)


def unit_kernel(at_ref, tok_ref, other_ref, root_ref, mine_ref, given_ref, theirs_ref, both_ref, *, band):
    core = at_ref[CORE]
    for n, ref in enumerate((tok_ref, other_ref)):
        tok = ref[...].astype(F32)
        root = jnp.sqrt(jnp.mean(tok * tok, -1, keepdims=True) + 1e-05)
        outs = [(theirs_ref, core)]
        if n == 0:
            root_ref[...] = root
            outs = [(mine_ref, core), (given_ref, 1 - core)]
        for i in range(mine_ref.shape[1] // band):
            for k, (out, which) in enumerate(outs):
                at = pl.multiple_of((2 * i + which) * band, band)
                unit = (ref[:, pl.ds(at, band)].astype(F32) / root).astype(BF)
                out[:, i * band : (i + 1) * band] = unit
                if k == 0:
                    both_ref[n, i * band : (i + 1) * band, :] = unit.T


def unit_rows(ids, tokens, others, band):
    rows, width = tokens.shape
    tile = 128
    half = width // 2
    row = pl.BlockSpec((tile, width), lambda i, at: (i, 0))
    return pl.pallas_call(
        functools.partial(unit_kernel, band=band),
        grid_spec=pltpu.PrefetchScalarGridSpec(
            num_scalar_prefetch=1,
            grid=(rows // tile,),
            in_specs=[row, row],
            out_specs=(pl.BlockSpec((tile, 1), lambda i, at: (i, 0)),)
            + (pl.BlockSpec((tile, half), lambda i, at: (i, 0)),) * 3
            + (pl.BlockSpec((2, half, tile), lambda i, at: (0, 0, i)),),
        ),
        out_shape=(shape(rows, 1, dtype=F32),)
        + (shape(rows, half),) * 3
        + (shape(2, half, rows),),
        compiler_params=PARAMS,
        cost_estimate=cost(BUSY, 1),
    )(ids, tokens, others)


def project_kernel(offsets, first, at_ref, mine_ref, theirs_ref, *refs):
    keep_ref, give_ref, stack_ref, sems = refs[-4:]
    n = len(offsets)
    shards, sums = refs[:n], refs[n:-4]
    copies = [pltpu.make_async_copy(w, stack_ref.at[i], sems.at[i]) for i, w in enumerate(shards)]
    for copy in copies:
        copy.start()
    kinds, depth, cols = shards[0].shape
    bands = [
        pl.ds(pl.multiple_of(place_of(at_ref, *offset) * depth, depth), depth) for offset in offsets
    ]
    for i, (rows, out) in enumerate(((mine_ref, keep_ref), (theirs_ref, give_ref))):
        for j in range(kinds):
            span = slice(j * cols, (j + 1) * cols)
            total = None if first else sums[i][:, span]
            for band, shard in zip(bands, shards):
                part = jnp.dot(rows[:, band], shard[j], preferred_element_type=F32)
                total = part if total is None else total + part
            out[:, span] = total.astype(out.dtype)
    for copy in copies:
        copy.wait()


def place_of(at_ref, y, z):
    return lax.rem(at_ref[Y] + y, 4) * 2 + lax.rem(at_ref[Z] + z, 2)


def project(ids, mine, theirs, shards, offsets, sums=(), give=F32):
    rows, _ = mine.shape
    n = len(shards)
    vmem = pl.BlockSpec(memory_space=pltpu.VMEM)
    cols = 3 * shards[0].shape[-1]
    return pl.pallas_call(
        functools.partial(project_kernel, offsets, not sums),
        in_specs=[pl.BlockSpec(memory_space=pltpu.SMEM)] + [vmem] * (2 + n + len(sums)),
        out_specs=(vmem, vmem, pl.BlockSpec(memory_space=pl.ANY)),
        out_shape=(
            shape(rows, cols, dtype=F32),
            shape(rows, cols, dtype=give),
            shape(n, *shards[0].shape),
        ),
        scratch_shapes=[pltpu.SemaphoreType.DMA((n,))],
        compiler_params=PARAMS,
        cost_estimate=cost(1, 1),
    )(ids, mine, theirs, *shards, *sums)


def project_last_kernel(offset, carried, at_ref, mine_ref, given_ref, keep_ref, came_ref, cot_ref, *refs):
    shards, heads_ref = refs[:6], refs[-1 - carried]
    depth, cols = shards[0].shape[-2:]
    band = pl.ds(pl.multiple_of(place_of(at_ref, *offset) * depth, depth), depth)
    heads = range(heads_ref.shape[0])
    for j in range(3):
        span = slice(j * cols, (j + 1) * cols)
        total = keep_ref[:, span] + came_ref[:, span].astype(F32)
        total += jnp.dot(mine_ref[:, band], shards[j][0], preferred_element_type=F32)
        total += jnp.dot(given_ref[:, band], shards[3 + j][0], preferred_element_type=F32)
        for h in heads:
            heads_ref[h, :, j * HS : (j + 1) * HS] = total[:, h * HS : (h + 1) * HS].astype(BF)
    for h in heads:
        heads_ref[h, :, 3 * HS :] = cot_ref[:, h * HS : (h + 1) * HS]


def project_last(ids, mine, given, keep, came, cotangent, pieces, offset, heads, carry):
    rows, cols = keep.shape
    n = len(carry)
    vmem = pl.BlockSpec(memory_space=pltpu.VMEM)
    free = pl.BlockSpec(memory_space=pl.ANY)
    return pl.pallas_call(
        functools.partial(project_last_kernel, offset, n),
        in_specs=[pl.BlockSpec(memory_space=pltpu.SMEM)]
        + [vmem] * (5 + len(pieces))
        + [free] * n,
        out_specs=(vmem,) + (free,) * n,
        out_shape=(shape(heads, rows, cols // heads + HS),) + tuple(shape(*c.shape) for c in carry),
        input_output_aliases={6 + len(pieces) + i: 1 + i for i in range(n)},
        compiler_params=PARAMS,
        cost_estimate=cost(1, 1),
    )(ids, mine, given, keep, came, cotangent, *pieces, *carry)


def attention_kernel(q_rows, qkv_ref, *refs):
    att_ref, grad_ref, dk_ref, dv_ref = refs[-4:]
    scale = 1.0 / math.sqrt(HS)
    key = qkv_ref[:, HS : 2 * HS]
    value = qkv_ref[:, 2 * HS : 3 * HS]
    key_t = key.T
    value_t = value.T
    for i in range(qkv_ref.shape[0] // q_rows):
        rows = pl.ds(i * q_rows, q_rows)
        query = qkv_ref[rows, 0:HS]
        dout = qkv_ref[rows, 3 * HS :]
        scores = dot(key, query, 1, 1) * (scale * math.log2(math.e))
        top = jnp.max(scores, axis=0, keepdims=True)
        expo = jnp.exp2(scores - top)
        prob = expo * (1.0 / jnp.sum(expo, axis=0, keepdims=True))
        prob_bf = prob.astype(BF)
        att = dot(value_t, prob_bf, 1, 0).T.astype(BF)
        att_ref[rows, :] = att
        row_dot = jnp.sum(
            dout.astype(F32).T * att.astype(F32).T, axis=0, keepdims=True
        )
        dprob = dot(value, dout, 1, 1)
        dscore = (prob * (dprob - row_dot)).astype(BF)
        grad_ref[rows, 0:HS] = (dot(key_t, dscore, 1, 0) * scale).T.astype(BF)
        dv = dot(prob_bf, dout, 1, 0)
        dk = dot(dscore, query, 1, 0)
        if i == 0:
            dv_ref[...] = dv
            dk_ref[...] = dk
        else:
            dv_ref[...] += dv
            dk_ref[...] += dk
    grad_ref[:, HS : 2 * HS] = (dk_ref[...] * scale).astype(BF)
    grad_ref[:, 2 * HS : 3 * HS] = dv_ref[...].astype(BF)


def attention(qkv, after):
    n = qkv.shape[0]
    vmem = pl.BlockSpec(memory_space=pltpu.VMEM)
    return pl.pallas_call(
        functools.partial(attention_kernel, min(256, n)),
        out_shape=(shape(n, HS), shape(n, 3 * HS)),
        in_specs=[vmem] + [pl.BlockSpec(memory_space=pl.ANY)] * len(after),
        out_specs=(vmem,) * 2,
        scratch_shapes=[pltpu.VMEM((n, HS), F32), pltpu.VMEM((n, HS), F32)],
        compiler_params=PARAMS,
        cost_estimate=cost(BUSY, 1),
    )(qkv, *after)


def write_stat(ref, at, stat):
    ref[at:, :] = jnp.zeros((ref.shape[0] - at, ref.shape[1]), BF)
    rest = stat
    for i in range(3):
        top = rest.astype(BF)
        ref[at + i : at + i + 1, :] = top
        rest = rest - top.astype(F32)


def read_stat(ref, at):
    return sum(ref[at + i : at + i + 1, :].astype(F32) for i in range(3))


def norm_kernel(width, halves, spots, places, n_in, at_ref, g_ref, p_ref, *refs):
    shards = refs[:n_in]
    n_out = max(spot[0] for spot in spots) + 1
    outs, stat_ref = refs[-4 - n_out : -4], refs[-4]
    w_ref, flat_ref, sems = refs[-3:]
    _, kinds, depth, cols = w_ref.shape
    band = depth // 2
    quarters = len(places) // 2

    def copy(step, core, j, source):
        to = lax.rem(at_ref[CORE] + core, 2)
        at = pl.ds(pl.multiple_of(to * band, band), band)
        return pltpu.make_async_copy(source, w_ref.at[step, j, at], sems.at[step, core, j])

    for step, (by, half) in enumerate(halves):
        y_off = lax.rem(at_ref[T] + (by + quarters) - at_ref[Y], quarters)
        where = y_off * 2 + lax.rem(at_ref[Z] + half, 2)
        for place, cores in enumerate(places):

            @pl.when(where == place)
            def _(step=step, cores=cores):
                for core, pieces in enumerate(cores):
                    for j, (which, at) in enumerate(pieces):
                        copy(step, core, j, shards[which].at[*at]).start()

    heads, _, _ = g_ref.shape
    for h in range(heads):
        for j in range(kinds):
            at = (j * heads + h) * HS
            flat_ref[at : at + HS, :] = g_ref[h, :, j * HS : (j + 1) * HS].T
    total = sum(
        g_ref[h, :, j * HS : (j + 1) * HS].astype(F32)
        * p_ref[h, :, j * HS : (j + 1) * HS].astype(F32)
        for h in range(heads)
        for j in range(kinds)
    )
    stat = jnp.sum(total.T, axis=0, keepdims=True) * (1.0 / width)
    stat_ref[...] = stat
    for ref in outs:
        if ref.shape[0] % 128:
            write_stat(ref, ref.shape[0] - 16, stat)

    for step, (which, at) in enumerate(spots):
        for core in range(2):
            for j in range(kinds):
                copy(step, core, j, shards[0].at[0]).wait()
        total = sum(
            dot(w_ref[step, j], flat_ref[j * cols : (j + 1) * cols, :], 1, 0)
            for j in range(kinds)
        )
        outs[which][at : at + depth, :] = total.astype(BF)


def norm_halves(ids, grads, proj, shards, places, halves, spots, sizes, width, after=()):
    heads, rows, _ = grads.shape
    kinds = 3
    band, cols = shards[0].shape[-2:]
    n = len(spots)
    sizes = (*sizes, 1)
    vmem = pl.BlockSpec(memory_space=pltpu.VMEM)
    free = pl.BlockSpec(memory_space=pl.ANY)
    return pl.pallas_call(
        functools.partial(norm_kernel, width, halves, spots, places, len(shards)),
        in_specs=[pl.BlockSpec(memory_space=pltpu.SMEM), vmem, vmem]
        + [free] * (len(shards) + len(after)),
        out_specs=(vmem,) * len(sizes),
        out_shape=tuple(shape(s, rows) for s in sizes[:-1]) + (shape(1, rows, dtype=F32),),
        scratch_shapes=[
            pltpu.VMEM((n, kinds, 2 * band, cols), BF),
            pltpu.VMEM((kinds * cols, rows), BF),
            pltpu.SemaphoreType.DMA((n, 2, kinds)),
        ],
        compiler_params=PARAMS,
        cost_estimate=cost(1, 1),
    )(ids, grads, proj, *shards, *after)


def add_kernel(up_part, up_in, stat_in, down_part, down_in, stat_ref, *refs):
    up_out, down_out = refs[-2:]
    half = up_part.shape[0]
    for part, came, out in ((up_part, up_in, up_out), (down_part, down_in, down_out)):
        out[:half, :] = (part[...].astype(F32) + came[...].astype(F32)).astype(BF)
    write_stat(up_out, half, stat_ref[...] + read_stat(stat_in, 0))
    write_stat(down_out, half, stat_ref[...])


def add_messages(up_part, up_in, down_part, down_in, stat, after=()):
    half, rows = up_part.shape
    block = pl.BlockSpec((half, rows), lambda i: (0, 0))
    out = pl.BlockSpec((half + 16, rows), lambda i: (0, 0))
    end = pl.BlockSpec((16, rows), lambda i: (2 * half // 16, 0))
    return pl.pallas_call(
        add_kernel,
        grid=(1,),
        out_shape=(shape(half + 16, rows),) * 2,
        in_specs=[block, block, end, block, block, pl.BlockSpec((1, rows), lambda i: (0, 0))]
        + [pl.BlockSpec(memory_space=pl.ANY)] * len(after),
        out_specs=(out, out),
        compiler_params=PARAMS,
        cost_estimate=cost(1, 1),
    )(up_part, up_in, up_in, down_part, down_in, stat, *after)


def finish_kernel(at_ref, own0, own1, up0, up1, down0, down1, tok_ref, root_ref, stat_ref, *refs):
    out_ref = refs[-1]
    half = own0.shape[0]
    stat = stat_ref[...] + read_stat(up0, half) + read_stat(down1, half)
    stat = jnp.broadcast_to(stat, (HS, stat.shape[1])).T[:, 0:1]
    root = root_ref[...]
    parts = (
        (own0[...], up0[:half, :], down0[half : 2 * half, :]),
        (own1[...], up1[half : 2 * half, :], down1[:half, :]),
    )
    for i, part in enumerate(parts):
        span = slice(i * half, (i + 1) * half)
        total = sum(p.astype(F32) for p in part)
        unit = tok_ref[:, span].astype(F32) / root
        out_ref[:, span] = ((total.T - unit * stat) / root).astype(BF)


def finish(ids, parts, tokens, root, stat, after=()):
    half, rows = parts[0].shape
    share = 2 * half
    tile = HS
    some = lambda a: pl.BlockSpec((a.shape[0], tile), lambda i, at: (0, i))
    return pl.pallas_call(
        finish_kernel,
        grid_spec=pltpu.PrefetchScalarGridSpec(
            num_scalar_prefetch=1,
            grid=(rows // tile,),
            in_specs=[some(p) for p in parts]
            + [pl.BlockSpec((tile, share), lambda i, at: (i, at[T]))]
            + [pl.BlockSpec((tile, 1), lambda i, at: (i, 0)), some(stat)]
            + [pl.BlockSpec(memory_space=pl.ANY)] * len(after),
            out_specs=pl.BlockSpec((tile, share), lambda i, at: (i, 0)),
        ),
        out_shape=shape(rows, share),
        compiler_params=PARAMS,
        cost_estimate=cost(BUSY, 1),
    )(ids, *parts, tokens, root, stat, *after)


def outer_kernel(tile, spots, at_ref, *refs):
    arrays, (mine_ref, other_ref, out_ref, a_ref, g_ref, sems) = refs[:-6], refs[-6:]
    n, rows, _ = mine_ref.shape
    depth = a_ref.shape[0]
    copies = []
    for step in range(depth // tile):
        span = pl.ds(step * tile, tile)
        some = []
        for i, (which, at, _, _) in enumerate(spots):
            to = a_ref.at[span, pl.ds(i * rows, rows)]
            some.append(pltpu.make_async_copy(arrays[which].at[at, span], to, sems.at[step, i]))
            some[-1].start()
        copies.append(some)
    for i, (_, _, by, frame) in enumerate(spots):
        ref = other_ref if frame else mine_ref
        g_ref[i * rows : (i + 1) * rows, :] = ref[lax.rem(at_ref[X] + by, n)]
    for step, some in enumerate(copies):
        for copy in some:
            copy.wait()
        span = slice(step * tile, (step + 1) * tile)
        out_ref[span, :] = jnp.dot(
            a_ref[span, :], g_ref[...], preferred_element_type=F32
        ).astype(BF)


def outer(ids, arrays, spots, mine, other):
    _, depth, rows = arrays[0].shape
    cols = mine.shape[2]
    n = len(spots)
    tile = 512
    vmem = pl.BlockSpec(memory_space=pltpu.VMEM)
    return pl.pallas_call(
        functools.partial(outer_kernel, tile, spots),
        in_specs=[pl.BlockSpec(memory_space=pltpu.SMEM)]
        + [pl.BlockSpec(memory_space=pl.ANY)] * len(arrays)
        + [vmem, vmem],
        out_specs=vmem,
        out_shape=shape(depth, cols),
        scratch_shapes=[
            pltpu.VMEM((depth, n * rows), BF),
            pltpu.VMEM((n * rows, cols), BF),
            pltpu.SemaphoreType.DMA((depth // tile, n)),
        ],
        compiler_params=PARAMS,
        cost_estimate=cost(1, 1),
    )(ids, *arrays, mine, other)


def split_kernel(at_ref, part_ref, *refs):
    keep_ref, give_ref = refs[-2:]
    n, _, rows, _ = part_ref.shape
    for ref, which in ((keep_ref, at_ref[Z]), (give_ref, 1 - at_ref[Z])):
        ref[...] = sum(part_ref[i, which].astype(F32) for i in range(n)).astype(ref.dtype)


def split(ids, part, after=()):
    _, _, rows, cols = part.shape
    vmem = pl.BlockSpec(memory_space=pltpu.VMEM)
    return pl.pallas_call(
        split_kernel,
        in_specs=[pl.BlockSpec(memory_space=pltpu.SMEM), vmem]
        + [pl.BlockSpec(memory_space=pl.ANY)] * len(after),
        out_specs=(vmem, vmem),
        out_shape=(shape(rows, cols, dtype=F32), shape(rows, cols)),
        compiler_params=PARAMS,
        cost_estimate=cost(1, 1),
    )(ids, part, *after)


def merge_kernel(keep_ref, came_ref, att_ref, *refs):
    out_ref = refs[-1]
    total = (keep_ref[...] + came_ref[...].astype(F32)).astype(BF)
    cols = total.shape[1]
    for i in range(out_ref.shape[0]):
        out_ref[i, :, :cols] = total
        out_ref[i, :, cols:] = att_ref[i]


def merge(keep, came, att, after=()):
    rows, cols = keep.shape
    n, _, more = att.shape
    vmem = pl.BlockSpec(memory_space=pltpu.VMEM)
    return pl.pallas_call(
        merge_kernel,
        out_shape=shape(n, rows, cols + more),
        in_specs=[vmem] * 3 + [pl.BlockSpec(memory_space=pl.ANY)] * len(after),
        out_specs=vmem,
        compiler_params=PARAMS,
        cost_estimate=cost(1, 1),
    )(keep, came, att, *after)


def unpack_kernel(in_ref, w_ref, att_ref):
    for h in range(in_ref.shape[0]):
        span = slice(h * HS, (h + 1) * HS)
        for j in range(3):
            w_ref[j, :, span] = in_ref[h, :, j * HS : (j + 1) * HS].astype(F32)
        att_ref[:, span] = in_ref[h, :, 3 * HS :]


def unpack(last):
    heads, rows, more = last.shape
    tile = rows // 4
    return pl.pallas_call(
        unpack_kernel,
        grid=(rows // tile,),
        in_specs=[pl.BlockSpec((heads, tile, more), lambda i: (0, i, 0))],
        out_specs=(
            pl.BlockSpec((3, tile, heads * HS), lambda i: (0, i, 0)),
            pl.BlockSpec((tile, heads * HS), lambda i: (i, 0)),
        ),
        out_shape=(shape(3, rows, heads * HS, dtype=F32), shape(rows, heads * HS)),
        compiler_params=PARAMS,
        cost_estimate=cost(1, 1),
    )(last)


def gate(arrays, after=(), pieces=()):
    n, m = len(arrays), len(arrays) + len(after)
    free = pl.BlockSpec(memory_space=pl.ANY)

    def kernel(*refs):
        outs, sems = refs[m + n : -1], refs[-1]
        copies = [
            pltpu.make_async_copy(refs[which].at[pl.ds(at, 1)], out, sems.at[i])
            for i, ((which, at), out) in enumerate(zip(pieces, outs))
        ]
        for copy in copies:
            copy.start()
        for copy in copies:
            copy.wait()

    return pl.pallas_call(
        kernel,
        in_specs=[free] * m,
        out_specs=(free,) * n + (pl.BlockSpec(memory_space=pltpu.VMEM),) * len(pieces),
        out_shape=tuple(shape(*a.shape) for a in arrays)
        + tuple(shape(1, *arrays[which].shape[1:]) for which, _ in pieces),
        scratch_shapes=[pltpu.SemaphoreType.DMA((max(len(pieces), 1),))],
        input_output_aliases={i: i for i in range(n)},
        compiler_params=PARAMS,
        cost_estimate=cost(1, 1),
    )(*arrays, *after)


def shift(x, axis, by):
    n = lax.axis_size(axis)
    return lax.ppermute(x, axis, [(i, (i + by) % n) for i in range(n)])


def per_device(tokens, weights, cotangent):
    _, rows, width = tokens.shape
    w_rows, _, cols = weights.shape
    heads = cols // HS
    n_x, n_y = (lax.axis_size(a) for a in ("x", "y"))
    ids = jnp.stack([lax.axis_index(a) for a in ("core", "x", "zh", "y", "zl")])
    tokens = tokens.reshape(rows, width)
    half = width // lax.axis_size("zh") // 2

    swap = lambda a: shift(a, "core", 1)
    own = weights.transpose(1, 0, 2)
    left, right, other = shift(own, "y", 1), shift(own, "y", -1), shift(own, "zl", 1)
    root, mine, given, theirs, pair = unit_rows(ids, tokens, swap(tokens), w_rows)
    left, right, other = gate((left, right, other), (pair,))

    x_left, x_right = shift(pair, "x", 1), shift(pair, "x", -1)

    near = ((0, 0), (3, 0), (1, 0), (0, 1))
    *sums, stack_0 = project(ids, mine, theirs, (own, left, right, other), near)
    far, other_left, other_right, *pieces = gate(
        (shift(left, "y", 1), shift(left, "zl", 1), shift(other, "y", -1)),
        sums,
        ((0, 0), (1, 1), (2, 2)),
    )
    then = ((2, 0), (3, 1), (1, 1))
    keep, give, stack_1 = project(
        ids, mine, theirs, (far, other_left, other_right), then, sums, BF
    )
    *pieces, give = gate(
        (shift(pieces[0], "zl", 1), shift(pieces[1], "y", 1), shift(pieces[2], "y", -1), give)
    )
    pieces = (*pieces, *(swap(p) for p in pieces))
    proj, stack_0, stack_1 = project_last(
        ids, mine, given, keep, swap(give), cotangent.reshape(rows, cols), pieces, (2, 1), heads,
        (stack_0, stack_1),
    )

    x_left, x_right, far_0, far_1 = gate((x_left, x_right), (proj,), ((0, 0), (1, 1)))
    far_0, far_1 = shift(far_0, "x", 1), shift(far_1, "x", -1)
    blocks = (pair, x_left, x_right, far_0, far_1)
    spots = ((0, 0, 0, 0), (0, 1, 0, 1), (1, 0, 3, 0), (1, 1, 3, 1), (2, 0, 1, 0), (2, 1, 1, 1), (3, 0, 2, 0), (4, 0, 2, 1))
    qkv = lax.all_to_all(proj, "x", 0, 0, tiled=True).reshape(n_x * rows, 4 * HS)
    att, head_grads = attention(qkv, (x_left, x_right))

    shards = (*pieces, stack_0, swap(stack_0), stack_1, swap(stack_1))
    places = {(2, 1): [[(3 * core + j, (0,)) for j in range(3)] for core in range(2)]}
    for first, keys in ((6, near), (8, then)):
        for i, key in enumerate(keys):
            places[key] = [[(first + core, (i, j)) for j in range(3)] for core in range(2)]
    places = [places[(by, z)] for by in range(n_y) for z in range(2)]

    head_grads = head_grads.reshape(n_x, rows, 3 * HS)
    grads = lax.all_to_all(head_grads, "x", 0, 0, tiled=True)
    part = outer(ids, blocks, spots, head_grads, swap(head_grads))

    up, down, stat = norm_halves(
        ids, grads, proj, shards, places,
        ((2, 0), (1, 1), (2, 1), (3, 0)),
        ((0, 0), (0, half), (1, 0), (1, half)),
        (2 * half + 16, 2 * half),
        width,
    )
    up, down = shift(up, "zh", 1), shift(down, "zh", -1)
    up_part, down_part, own0, own1, _ = norm_halves(
        ids, grads, proj, shards, places,
        ((1, 0), (3, 1), (0, 0), (0, 1)),
        ((0, 0), (1, 0), (2, 0), (3, 0)),
        (half,) * 4,
        width,
        (stat,),
    )
    part = lax.all_to_all(part, "y", 0, 0, tiled=True).reshape(n_y, 2, w_rows, 3 * HS)
    keep, give = split(ids, part, (own0,))
    came = shift(give, "zl", 1)
    up_2, down_2 = add_messages(up_part, up, down_part, down, stat, (came,))
    last = merge(keep, came, att.reshape(n_x, rows, HS))
    up_2, down_2 = shift(up_2, "zh", 1), shift(down_2, "zh", -1)
    last = lax.all_to_all(last, "x", 0, 0, tiled=True)
    token_grad = finish(ids, (own0, own1, up_2, up, down, down_2), tokens, root, stat)
    weight_grad, attended = unpack(last)
    return attended[None], token_grad[None], weight_grad.transpose(1, 0, 2)


def solution(mesh):
    fine = Mesh(mesh.devices.reshape(4, 2, 2, 4, 4), ("y", "zl", "core", "x", "zh"))
    dp = ("y", "zl", "core")
    return jax.shard_map(
        per_device,
        mesh=fine,
        in_specs=(P(dp, "x", None), P(dp, None, "zh"), P(dp, "x", "zh")),
        out_specs=(P(dp, "x", "zh"), P(dp, "x", "zh"), P(dp, None, "zh")),
        check_vma=False,
    )
```

```python
import functools
import math

import jax
import jax.numpy as jnp
from jax import lax
from jax.experimental import pallas as pl
from jax.experimental.pallas import tpu as pltpu
from jax.sharding import Mesh
from jax.sharding import PartitionSpec as P

HS = 128
CORE, X, T, Y, Z = range(5)
BF = jnp.bfloat16
BUSY = 2 * 10**10
F32 = jnp.float32
PARAMS = pltpu.CompilerParams(vmem_limit_bytes=60 * 1024 * 1024)
SMALL = pltpu.CompilerParams(vmem_limit_bytes=24 * 1024 * 1024)


def dot(a, b, ca, cb):
    return lax.dot_general(a, b, (((ca,), (cb,)), ((), ())), preferred_element_type=F32)


def cost(flops, nbytes, exps=0):
    return pl.CostEstimate(flops=flops, bytes_accessed=nbytes, transcendentals=exps)


def shape(*dims, dtype=BF):
    return jax.ShapeDtypeStruct(dims, dtype)


def unit_kernel(at_ref, tok_ref, other_ref, root_ref, mine_ref, given_ref, theirs_ref, both_ref, *, band):
    core = at_ref[CORE]
    for n, ref in enumerate((tok_ref, other_ref)):
        tok = ref[...].astype(F32)
        root = jnp.sqrt(jnp.mean(tok * tok, -1, keepdims=True) + 1e-05)
        outs = [(theirs_ref, core)]
        if n == 0:
            root_ref[...] = root
            outs = [(mine_ref, core), (given_ref, 1 - core)]
        for i in range(mine_ref.shape[1] // band):
            for k, (out, which) in enumerate(outs):
                at = pl.multiple_of((2 * i + which) * band, band)
                unit = (ref[:, pl.ds(at, band)].astype(F32) / root).astype(BF)
                out[:, i * band : (i + 1) * band] = unit
                if k == 0:
                    both_ref[n, i * band : (i + 1) * band, :] = unit.T


def unit_rows(ids, tokens, others, band):
    rows, width = tokens.shape
    tile = 128
    half = width // 2
    row = pl.BlockSpec((tile, width), lambda i, at: (i, 0))
    return pl.pallas_call(
        functools.partial(unit_kernel, band=band),
        grid_spec=pltpu.PrefetchScalarGridSpec(
            num_scalar_prefetch=1,
            grid=(rows // tile,),
            in_specs=[row, row],
            out_specs=(pl.BlockSpec((tile, 1), lambda i, at: (i, 0)),)
            + (pl.BlockSpec((tile, half), lambda i, at: (i, 0)),) * 3
            + (pl.BlockSpec((2, half, tile), lambda i, at: (0, 0, i)),),
        ),
        out_shape=(shape(rows, 1, dtype=F32),)
        + (shape(rows, half),) * 3
        + (shape(2, half, rows),),
        compiler_params=PARAMS,
        cost_estimate=cost(BUSY, 1),
    )(ids, tokens, others)


def project_kernel(offsets, first, at_ref, mine_ref, theirs_ref, *refs):
    keep_ref, give_ref, stack_ref, sems = refs[-4:]
    n = len(offsets)
    shards, sums = refs[:n], refs[n:-4]
    copies = [pltpu.make_async_copy(w, stack_ref.at[i], sems.at[i]) for i, w in enumerate(shards)]
    for copy in copies:
        copy.start()
    kinds, depth, cols = shards[0].shape
    bands = [
        pl.ds(pl.multiple_of(place_of(at_ref, *offset) * depth, depth), depth) for offset in offsets
    ]
    for i, (rows, out) in enumerate(((mine_ref, keep_ref), (theirs_ref, give_ref))):
        for j in range(kinds):
            span = slice(j * cols, (j + 1) * cols)
            total = None if first else sums[i][:, span]
            for band, shard in zip(bands, shards):
                part = jnp.dot(rows[:, band], shard[j], preferred_element_type=F32)
                total = part if total is None else total + part
            out[:, span] = total.astype(out.dtype)
    for copy in copies:
        copy.wait()


def place_of(at_ref, y, z):
    return lax.rem(at_ref[Y] + y, 4) * 2 + lax.rem(at_ref[Z] + z, 2)


def project(ids, mine, theirs, shards, offsets, sums=(), give=F32):
    rows, _ = mine.shape
    n = len(shards)
    vmem = pl.BlockSpec(memory_space=pltpu.VMEM)
    cols = 3 * shards[0].shape[-1]
    return pl.pallas_call(
        functools.partial(project_kernel, offsets, not sums),
        in_specs=[pl.BlockSpec(memory_space=pltpu.SMEM)] + [vmem] * (2 + n + len(sums)),
        out_specs=(vmem, vmem, pl.BlockSpec(memory_space=pl.ANY)),
        out_shape=(
            shape(rows, cols, dtype=F32),
            shape(rows, cols, dtype=give),
            shape(n, *shards[0].shape),
        ),
        scratch_shapes=[pltpu.SemaphoreType.DMA((n,))],
        compiler_params=PARAMS,
        cost_estimate=cost(1, 1),
    )(ids, mine, theirs, *shards, *sums)


def project_last_kernel(offset, carried, at_ref, mine_ref, given_ref, keep_ref, came_ref, cot_ref, *refs):
    shards, x_refs = refs[:6], refs[6:8]
    heads_ref, *cuts, sems = refs[-4 - carried : -1 - carried] + refs[-1:]
    copies = [
        pltpu.make_async_copy(ref.at[pl.ds(i, 1)], cut, sems.at[i])
        for i, (ref, cut) in enumerate(zip(x_refs, cuts))
    ]
    for copy in copies:
        copy.start()
    depth, cols = shards[0].shape[-2:]
    band = pl.ds(pl.multiple_of(place_of(at_ref, *offset) * depth, depth), depth)
    heads = range(heads_ref.shape[0])
    for j in range(3):
        span = slice(j * cols, (j + 1) * cols)
        total = keep_ref[:, span] + came_ref[:, span].astype(F32)
        total += jnp.dot(mine_ref[:, band], shards[j][0], preferred_element_type=F32)
        total += jnp.dot(given_ref[:, band], shards[3 + j][0], preferred_element_type=F32)
        for h in heads:
            heads_ref[h, :, j * HS : (j + 1) * HS] = total[:, h * HS : (h + 1) * HS].astype(BF)
    for h in heads:
        heads_ref[h, :, 3 * HS :] = cot_ref[:, h * HS : (h + 1) * HS]
    for copy in copies:
        copy.wait()


def project_last(ids, mine, given, keep, came, cotangent, pieces, offset, heads, cut, carry):
    rows, cols = keep.shape
    n = len(carry)
    vmem = pl.BlockSpec(memory_space=pltpu.VMEM)
    free = pl.BlockSpec(memory_space=pl.ANY)
    return pl.pallas_call(
        functools.partial(project_last_kernel, offset, n),
        in_specs=[pl.BlockSpec(memory_space=pltpu.SMEM)]
        + [vmem] * (5 + len(pieces))
        + [free] * (2 + n),
        out_specs=(vmem,) * 3 + (free,) * n,
        out_shape=(shape(heads, rows, cols // heads + HS),)
        + tuple(shape(1, *c.shape[1:]) for c in cut)
        + tuple(shape(*c.shape) for c in carry),
        scratch_shapes=[pltpu.SemaphoreType.DMA((2,))],
        input_output_aliases={8 + len(pieces) + i: 3 + i for i in range(n)},
        compiler_params=PARAMS,
        cost_estimate=cost(1, 1),
    )(ids, mine, given, keep, came, cotangent, *pieces, *cut, *carry)


def attention_kernel(q_rows, qkv_ref, *refs):
    att_ref, grad_ref, dk_ref, dv_ref = refs[-4:]
    scale = 1.0 / math.sqrt(HS)
    key = qkv_ref[:, HS : 2 * HS]
    value = qkv_ref[:, 2 * HS : 3 * HS]
    key_t = key.T
    value_t = value.T
    for i in range(qkv_ref.shape[0] // q_rows):
        rows = pl.ds(i * q_rows, q_rows)
        query = qkv_ref[rows, 0:HS]
        dout = qkv_ref[rows, 3 * HS :]
        scores = dot(key, query, 1, 1) * (scale * math.log2(math.e))
        top = jnp.max(scores, axis=0, keepdims=True)
        expo = jnp.exp2(scores - top)
        prob = expo * (1.0 / jnp.sum(expo, axis=0, keepdims=True))
        prob_bf = prob.astype(BF)
        att = dot(value_t, prob_bf, 1, 0).T.astype(BF)
        att_ref[rows, :] = att
        row_dot = jnp.sum(
            dout.astype(F32).T * att.astype(F32).T, axis=0, keepdims=True
        )
        dprob = dot(value, dout, 1, 1)
        dscore = (prob * (dprob - row_dot)).astype(BF)
        grad_ref[rows, 0:HS] = (dot(key_t, dscore, 1, 0) * scale).T.astype(BF)
        dv = dot(prob_bf, dout, 1, 0)
        dk = dot(dscore, query, 1, 0)
        if i == 0:
            dv_ref[...] = dv
            dk_ref[...] = dk
        else:
            dv_ref[...] += dv
            dk_ref[...] += dk
    grad_ref[:, HS : 2 * HS] = (dk_ref[...] * scale).astype(BF)
    grad_ref[:, 2 * HS : 3 * HS] = dv_ref[...].astype(BF)


def attention(qkv, after):
    n = qkv.shape[0]
    vmem = pl.BlockSpec(memory_space=pltpu.VMEM)
    return pl.pallas_call(
        functools.partial(attention_kernel, min(256, n)),
        out_shape=(shape(n, HS), shape(n, 3 * HS)),
        in_specs=[vmem] + [pl.BlockSpec(memory_space=pl.ANY)] * len(after),
        out_specs=(vmem,) * 2,
        scratch_shapes=[pltpu.VMEM((n, HS), F32), pltpu.VMEM((n, HS), F32)],
        compiler_params=PARAMS,
        cost_estimate=cost(BUSY, 1),
    )(qkv, *after)


def write_stat(ref, at, stat):
    ref[at:, :] = jnp.zeros((ref.shape[0] - at, ref.shape[1]), BF)
    rest = stat
    for i in range(3):
        top = rest.astype(BF)
        ref[at + i : at + i + 1, :] = top
        rest = rest - top.astype(F32)


def read_stat(ref, at):
    return sum(ref[at + i : at + i + 1, :].astype(F32) for i in range(3))


def norm_kernel(width, halves, spots, places, n_in, at_ref, g_ref, p_ref, *refs):
    shards = refs[:n_in]
    n_out = max(spot[0] for spot in spots) + 1
    outs, stat_ref = refs[-4 - n_out : -4], refs[-4]
    w_ref, flat_ref, sems = refs[-3:]
    _, kinds, depth, cols = w_ref.shape
    band = depth // 2
    quarters = len(places) // 2

    def copy(step, core, j, source):
        to = lax.rem(at_ref[CORE] + core, 2)
        at = pl.ds(pl.multiple_of(to * band, band), band)
        return pltpu.make_async_copy(source, w_ref.at[step, j, at], sems.at[step, core, j])

    for step, (by, half) in enumerate(halves):
        y_off = lax.rem(at_ref[T] + (by + quarters) - at_ref[Y], quarters)
        where = y_off * 2 + lax.rem(at_ref[Z] + half, 2)
        for place, cores in enumerate(places):

            @pl.when(where == place)
            def _(step=step, cores=cores):
                for core, pieces in enumerate(cores):
                    for j, (which, at) in enumerate(pieces):
                        copy(step, core, j, shards[which].at[*at]).start()

    heads, _, _ = g_ref.shape
    for h in range(heads):
        for j in range(kinds):
            at = (j * heads + h) * HS
            flat_ref[at : at + HS, :] = g_ref[h, :, j * HS : (j + 1) * HS].T
    total = sum(
        g_ref[h, :, j * HS : (j + 1) * HS].astype(F32)
        * p_ref[h, :, j * HS : (j + 1) * HS].astype(F32)
        for h in range(heads)
        for j in range(kinds)
    )
    stat = jnp.sum(total.T, axis=0, keepdims=True) * (1.0 / width)
    stat_ref[...] = stat
    for ref in outs:
        if ref.shape[0] % 128:
            write_stat(ref, ref.shape[0] - 16, stat)

    for step, (which, at) in enumerate(spots):
        for core in range(2):
            for j in range(kinds):
                copy(step, core, j, shards[0].at[0]).wait()
        total = sum(
            dot(w_ref[step, j], flat_ref[j * cols : (j + 1) * cols, :], 1, 0)
            for j in range(kinds)
        )
        outs[which][at : at + depth, :] = total.astype(BF)


def norm_halves(ids, grads, proj, shards, places, halves, spots, sizes, width, after=()):
    heads, rows, _ = grads.shape
    kinds = 3
    band, cols = shards[0].shape[-2:]
    n = len(spots)
    sizes = (*sizes, 1)
    vmem = pl.BlockSpec(memory_space=pltpu.VMEM)
    free = pl.BlockSpec(memory_space=pl.ANY)
    return pl.pallas_call(
        functools.partial(norm_kernel, width, halves, spots, places, len(shards)),
        in_specs=[pl.BlockSpec(memory_space=pltpu.SMEM), vmem, vmem]
        + [free] * (len(shards) + len(after)),
        out_specs=(vmem,) * len(sizes),
        out_shape=tuple(shape(s, rows) for s in sizes[:-1]) + (shape(1, rows, dtype=F32),),
        scratch_shapes=[
            pltpu.VMEM((n, kinds, 2 * band, cols), BF),
            pltpu.VMEM((kinds * cols, rows), BF),
            pltpu.SemaphoreType.DMA((n, 2, kinds)),
        ],
        compiler_params=PARAMS,
        cost_estimate=cost(1, 1),
    )(ids, grads, proj, *shards, *after)


def add_kernel(up_part, up_in, stat_in, down_part, down_in, stat_ref, *refs):
    up_out, down_out = refs[-2:]
    half = up_part.shape[0]
    for part, came, out in ((up_part, up_in, up_out), (down_part, down_in, down_out)):
        out[:half, :] = (part[...].astype(F32) + came[...].astype(F32)).astype(BF)
    write_stat(up_out, half, stat_ref[...] + read_stat(stat_in, 0))
    write_stat(down_out, half, stat_ref[...])


def add_messages(up_part, up_in, down_part, down_in, stat, after=()):
    half, rows = up_part.shape
    block = pl.BlockSpec((half, rows), lambda i: (0, 0))
    out = pl.BlockSpec((half + 16, rows), lambda i: (0, 0))
    end = pl.BlockSpec((16, rows), lambda i: (2 * half // 16, 0))
    return pl.pallas_call(
        add_kernel,
        grid=(1,),
        out_shape=(shape(half + 16, rows),) * 2,
        in_specs=[block, block, end, block, block, pl.BlockSpec((1, rows), lambda i: (0, 0))]
        + [pl.BlockSpec(memory_space=pl.ANY)] * len(after),
        out_specs=(out, out),
        compiler_params=PARAMS,
        cost_estimate=cost(1, 1),
    )(up_part, up_in, up_in, down_part, down_in, stat, *after)


def finish_kernel(at_ref, own0, own1, up0, up1, down0, down1, tok_ref, root_ref, stat_ref, *refs):
    out_ref = refs[-1]
    half = own0.shape[0]
    stat = stat_ref[...] + read_stat(up0, half) + read_stat(down1, half)
    stat = jnp.broadcast_to(stat, (HS, stat.shape[1])).T[:, 0:1]
    root = root_ref[...]
    parts = (
        (own0[...], up0[:half, :], down0[half : 2 * half, :]),
        (own1[...], up1[half : 2 * half, :], down1[:half, :]),
    )
    for i, part in enumerate(parts):
        span = slice(i * half, (i + 1) * half)
        total = sum(p.astype(F32) for p in part)
        unit = tok_ref[:, span].astype(F32) / root
        out_ref[:, span] = ((total.T - unit * stat) / root).astype(BF)


def finish(ids, parts, tokens, root, stat, after=()):
    half, rows = parts[0].shape
    share = 2 * half
    tile = HS
    some = lambda a: pl.BlockSpec((a.shape[0], tile), lambda i, at: (0, i))
    return pl.pallas_call(
        finish_kernel,
        grid_spec=pltpu.PrefetchScalarGridSpec(
            num_scalar_prefetch=1,
            grid=(rows // tile,),
            in_specs=[some(p) for p in parts]
            + [pl.BlockSpec((tile, share), lambda i, at: (i, at[T]))]
            + [pl.BlockSpec((tile, 1), lambda i, at: (i, 0)), some(stat)]
            + [pl.BlockSpec(memory_space=pl.ANY)] * len(after),
            out_specs=pl.BlockSpec((tile, share), lambda i, at: (i, 0)),
        ),
        out_shape=shape(rows, share),
        compiler_params=PARAMS,
        cost_estimate=cost(BUSY, 1),
    )(ids, *parts, tokens, root, stat, *after)


def outer_kernel(tile, spots, at_ref, *refs):
    out_ref, a_ref, g_ref, sems = refs[-4:]
    m = max(spot[0] for spot in spots) + 1
    arrays, (mine_ref, other_ref) = refs[:m], refs[m : m + 2]
    n, rows, _ = mine_ref.shape
    depth = a_ref.shape[0]
    copies = []
    for step in range(depth // tile):
        span = pl.ds(step * tile, tile)
        some = []
        for i, (which, at, _, _) in enumerate(spots):
            to = a_ref.at[span, pl.ds(i * rows, rows)]
            some.append(pltpu.make_async_copy(arrays[which].at[at, span], to, sems.at[step, i]))
            some[-1].start()
        copies.append(some)
    for i, (_, _, by, frame) in enumerate(spots):
        ref = other_ref if frame else mine_ref
        g_ref[i * rows : (i + 1) * rows, :] = ref[lax.rem(at_ref[X] + by, n)]
    for step, some in enumerate(copies):
        for copy in some:
            copy.wait()
        span = slice(step * tile, (step + 1) * tile)
        out_ref[span, :] = jnp.dot(
            a_ref[span, :], g_ref[...], preferred_element_type=F32
        ).astype(BF)


def outer(ids, arrays, spots, mine, other, after):
    _, depth, rows = arrays[0].shape
    cols = mine.shape[2]
    n = len(spots)
    tile = 512
    vmem = pl.BlockSpec(memory_space=pltpu.VMEM)
    return pl.pallas_call(
        functools.partial(outer_kernel, tile, spots),
        in_specs=[pl.BlockSpec(memory_space=pltpu.SMEM)]
        + [pl.BlockSpec(memory_space=pl.ANY)] * len(arrays)
        + [vmem, vmem]
        + [pl.BlockSpec(memory_space=pl.ANY)] * len(after),
        out_specs=vmem,
        out_shape=shape(depth, cols),
        scratch_shapes=[
            pltpu.VMEM((depth, n * rows), BF),
            pltpu.VMEM((n * rows, cols), BF),
            pltpu.SemaphoreType.DMA((depth // tile, n)),
        ],
        compiler_params=PARAMS,
        cost_estimate=cost(1, 1),
    )(ids, *arrays, mine, other, *after)


def split_kernel(at_ref, part_ref, *refs):
    keep_ref, give_ref = refs[-2:]
    n, _, rows, _ = part_ref.shape
    for ref, which in ((keep_ref, at_ref[Z]), (give_ref, 1 - at_ref[Z])):
        ref[...] = sum(part_ref[i, which].astype(F32) for i in range(n)).astype(ref.dtype)


def split(ids, part, after=()):
    _, _, rows, cols = part.shape
    vmem = pl.BlockSpec(memory_space=pltpu.VMEM)
    return pl.pallas_call(
        split_kernel,
        in_specs=[pl.BlockSpec(memory_space=pltpu.SMEM), vmem]
        + [pl.BlockSpec(memory_space=pl.ANY)] * len(after),
        out_specs=(vmem, vmem),
        out_shape=(shape(rows, cols, dtype=F32), shape(rows, cols)),
        compiler_params=PARAMS,
        cost_estimate=cost(1, 1),
    )(ids, part, *after)


def merge_kernel(keep_ref, came_ref, att_ref, *refs):
    out_ref = refs[-1]
    total = (keep_ref[...] + came_ref[...].astype(F32)).astype(BF)
    cols = total.shape[1]
    for i in range(out_ref.shape[0]):
        out_ref[i, :, :cols] = total
        out_ref[i, :, cols:] = att_ref[i]


def merge(keep, came, att, after=()):
    rows, cols = keep.shape
    n, _, more = att.shape
    vmem = pl.BlockSpec(memory_space=pltpu.VMEM)
    return pl.pallas_call(
        merge_kernel,
        out_shape=shape(n, rows, cols + more),
        in_specs=[vmem] * 3 + [pl.BlockSpec(memory_space=pl.ANY)] * len(after),
        out_specs=vmem,
        compiler_params=PARAMS,
        cost_estimate=cost(1, 1),
    )(keep, came, att, *after)


def unpack_kernel(in_ref, w_ref, att_ref):
    for h in range(in_ref.shape[0]):
        span = slice(h * HS, (h + 1) * HS)
        for j in range(3):
            w_ref[j, :, span] = in_ref[h, :, j * HS : (j + 1) * HS].astype(F32)
        att_ref[:, span] = in_ref[h, :, 3 * HS :]


def unpack(last):
    heads, rows, more = last.shape
    tile = rows // 4
    return pl.pallas_call(
        unpack_kernel,
        grid=(rows // tile,),
        in_specs=[pl.BlockSpec((heads, tile, more), lambda i: (0, i, 0))],
        out_specs=(
            pl.BlockSpec((3, tile, heads * HS), lambda i: (0, i, 0)),
            pl.BlockSpec((tile, heads * HS), lambda i: (i, 0)),
        ),
        out_shape=(shape(3, rows, heads * HS, dtype=F32), shape(rows, heads * HS)),
        compiler_params=SMALL,
        cost_estimate=cost(1, 1),
    )(last)


def gate(arrays, after=(), pieces=()):
    n, m = len(arrays), len(arrays) + len(after)
    free = pl.BlockSpec(memory_space=pl.ANY)

    def kernel(*refs):
        outs, sems = refs[m + n : -1], refs[-1]
        copies = [
            pltpu.make_async_copy(refs[which].at[pl.ds(at, 1)], out, sems.at[i])
            for i, ((which, at), out) in enumerate(zip(pieces, outs))
        ]
        for copy in copies:
            copy.start()
        for copy in copies:
            copy.wait()

    return pl.pallas_call(
        kernel,
        in_specs=[free] * m,
        out_specs=(free,) * n + (pl.BlockSpec(memory_space=pltpu.VMEM),) * len(pieces),
        out_shape=tuple(shape(*a.shape) for a in arrays)
        + tuple(shape(1, *arrays[which].shape[1:]) for which, _ in pieces),
        scratch_shapes=[pltpu.SemaphoreType.DMA((max(len(pieces), 1),))],
        input_output_aliases={i: i for i in range(n)},
        compiler_params=PARAMS,
        cost_estimate=cost(1, 1),
    )(*arrays, *after)


def shift(x, axis, by):
    n = lax.axis_size(axis)
    return lax.ppermute(x, axis, [(i, (i + by) % n) for i in range(n)])


def per_device(tokens, weights, cotangent):
    _, rows, width = tokens.shape
    w_rows, _, cols = weights.shape
    heads = cols // HS
    n_x, n_y = (lax.axis_size(a) for a in ("x", "y"))
    ids = jnp.stack([lax.axis_index(a) for a in ("core", "x", "zh", "y", "zl")])
    tokens = tokens.reshape(rows, width)
    half = width // lax.axis_size("zh") // 2

    swap = lambda a: shift(a, "core", 1)
    own = weights.transpose(1, 0, 2)
    left, right, other = shift(own, "y", 1), shift(own, "y", -1), shift(own, "zl", 1)
    root, mine, given, theirs, pair = unit_rows(ids, tokens, swap(tokens), w_rows)
    left, right, other = gate((left, right, other), (pair,))

    x_left, x_right = shift(pair, "x", 1), shift(pair, "x", -1)

    near = ((0, 0), (3, 0), (1, 0), (0, 1))
    *sums, stack_0 = project(ids, mine, theirs, (own, left, right, other), near)
    far, other_left, other_right, *pieces = gate(
        (shift(left, "y", 1), shift(left, "zl", 1), shift(other, "y", -1)),
        sums,
        ((0, 0), (1, 1), (2, 2)),
    )
    then = ((2, 0), (3, 1), (1, 1))
    keep, give, stack_1 = project(
        ids, mine, theirs, (far, other_left, other_right), then, sums, BF
    )
    *pieces, give = gate(
        (shift(pieces[0], "zl", 1), shift(pieces[1], "y", 1), shift(pieces[2], "y", -1), give)
    )
    pieces = (*pieces, *(swap(p) for p in pieces))
    proj, far_0, far_1, stack_0, stack_1 = project_last(
        ids, mine, given, keep, swap(give), cotangent.reshape(rows, cols), pieces, (2, 1), heads,
        (x_left, x_right), (stack_0, stack_1),
    )

    far_0, far_1 = shift(far_0, "x", 1), shift(far_1, "x", -1)
    blocks = (pair, x_left, x_right, far_0, far_1)
    spots = ((0, 0, 0, 0), (0, 1, 0, 1), (1, 0, 3, 0), (1, 1, 3, 1), (2, 0, 1, 0), (2, 1, 1, 1), (3, 0, 2, 0), (4, 0, 2, 1))
    qkv = lax.all_to_all(proj, "x", 0, 0, tiled=True).reshape(n_x * rows, 4 * HS)
    att, head_grads = attention(qkv, ())

    shards = (*pieces, stack_0, swap(stack_0), stack_1, swap(stack_1))
    places = {(2, 1): [[(3 * core + j, (0,)) for j in range(3)] for core in range(2)]}
    for first, keys in ((6, near), (8, then)):
        for i, key in enumerate(keys):
            places[key] = [[(first + core, (i, j)) for j in range(3)] for core in range(2)]
    places = [places[(by, z)] for by in range(n_y) for z in range(2)]

    head_grads = head_grads.reshape(n_x, rows, 3 * HS)
    grads = lax.all_to_all(head_grads, "x", 0, 0, tiled=True)
    part = outer(ids, blocks, spots, head_grads, swap(head_grads), (shards[7], shards[9]))

    up, down, stat = norm_halves(
        ids, grads, proj, shards, places,
        ((2, 0), (1, 1), (2, 1), (3, 0)),
        ((0, 0), (0, half), (1, 0), (1, half)),
        (2 * half + 16, 2 * half),
        width,
    )
    up, down = shift(up, "zh", 1), shift(down, "zh", -1)
    up_part, down_part, own0, own1, _ = norm_halves(
        ids, grads, proj, shards, places,
        ((1, 0), (3, 1), (0, 0), (0, 1)),
        ((0, 0), (1, 0), (2, 0), (3, 0)),
        (half,) * 4,
        width,
        (stat,),
    )
    part = lax.all_to_all(part, "y", 0, 0, tiled=True).reshape(n_y, 2, w_rows, 3 * HS)
    keep, give = split(ids, part, (own0,))
    came = shift(give, "zl", 1)
    up_2, down_2 = add_messages(up_part, up, down_part, down, stat, (came,))
    last = merge(keep, came, att.reshape(n_x, rows, HS))
    up_2, down_2 = shift(up_2, "zh", 1), shift(down_2, "zh", -1)
    last = lax.all_to_all(last, "x", 0, 0, tiled=True)
    token_grad = finish(ids, (own0, own1, up_2, up, down, down_2), tokens, root, stat)
    weight_grad, attended = unpack(last)
    return attended[None], token_grad[None], weight_grad.transpose(1, 0, 2)


def solution(mesh):
    fine = Mesh(mesh.devices.reshape(4, 2, 2, 4, 4), ("y", "zl", "core", "x", "zh"))
    dp = ("y", "zl", "core")
    return jax.shard_map(
        per_device,
        mesh=fine,
        in_specs=(P(dp, "x", None), P(dp, None, "zh"), P(dp, "x", "zh")),
        out_specs=(P(dp, "x", "zh"), P(dp, "x", "zh"), P(dp, None, "zh")),
        check_vma=False,
    )
```

```python
import functools
import math

import jax
import jax.numpy as jnp
from jax import lax
from jax.experimental import pallas as pl
from jax.experimental.pallas import tpu as pltpu
from jax.sharding import Mesh
from jax.sharding import PartitionSpec as P

HS = 128
CORE, X, T, Y, Z = range(5)
BF = jnp.bfloat16
BUSY = 2 * 10**10
F32 = jnp.float32
PARAMS = pltpu.CompilerParams(vmem_limit_bytes=60 * 1024 * 1024)
SMALL = pltpu.CompilerParams(vmem_limit_bytes=24 * 1024 * 1024)


def dot(a, b, ca, cb):
    return lax.dot_general(a, b, (((ca,), (cb,)), ((), ())), preferred_element_type=F32)


def cost(flops, nbytes, exps=0):
    return pl.CostEstimate(flops=flops, bytes_accessed=nbytes, transcendentals=exps)


def shape(*dims, dtype=BF):
    return jax.ShapeDtypeStruct(dims, dtype)


def unit_kernel(at_ref, tok_ref, other_ref, root_ref, mine_ref, given_ref, theirs_ref, mine_t_ref, theirs_t_ref, *, band):
    core = at_ref[CORE]
    for n, ref in enumerate((tok_ref, other_ref)):
        tok = ref[...].astype(F32)
        root = jnp.sqrt(jnp.mean(tok * tok, -1, keepdims=True) + 1e-05)
        outs = [(theirs_ref, core)]
        if n == 0:
            root_ref[...] = root
            outs = [(mine_ref, core), (given_ref, 1 - core)]
        for i in range(mine_ref.shape[1] // band):
            for k, (out, which) in enumerate(outs):
                at = pl.multiple_of((2 * i + which) * band, band)
                unit = (ref[:, pl.ds(at, band)].astype(F32) / root).astype(BF)
                out[:, i * band : (i + 1) * band] = unit
                if k == 0:
                    (mine_t_ref, theirs_t_ref)[n][0, i * band : (i + 1) * band, :] = unit.T


def unit_rows(ids, tokens, others, band):
    rows, width = tokens.shape
    tile = 128
    half = width // 2
    row = pl.BlockSpec((tile, width), lambda i, at: (i, 0))
    return pl.pallas_call(
        functools.partial(unit_kernel, band=band),
        grid_spec=pltpu.PrefetchScalarGridSpec(
            num_scalar_prefetch=1,
            grid=(rows // tile,),
            in_specs=[row, row],
            out_specs=(pl.BlockSpec((tile, 1), lambda i, at: (i, 0)),)
            + (pl.BlockSpec((tile, half), lambda i, at: (i, 0)),) * 3
            + (pl.BlockSpec((1, half, tile), lambda i, at: (0, 0, i)),) * 2,
        ),
        out_shape=(shape(rows, 1, dtype=F32),)
        + (shape(rows, half),) * 3
        + (shape(1, half, rows),) * 2,
        compiler_params=PARAMS,
        cost_estimate=cost(BUSY, 1),
    )(ids, tokens, others)


def project_kernel(offsets, n_sums, at_ref, mine_ref, theirs_ref, *refs):
    keep_ref, give_ref, stack_ref, sems = refs[-4:]
    n = len(offsets)
    shards, sums = refs[:n], refs[n : n + n_sums]
    copies = [pltpu.make_async_copy(w, stack_ref.at[i], sems.at[i]) for i, w in enumerate(shards)]
    for copy in copies:
        copy.start()
    kinds, depth, cols = shards[0].shape
    bands = [
        pl.ds(pl.multiple_of(place_of(at_ref, *offset) * depth, depth), depth) for offset in offsets
    ]
    for i, (rows, out) in enumerate(((mine_ref, keep_ref), (theirs_ref, give_ref))):
        for j in range(kinds):
            span = slice(j * cols, (j + 1) * cols)
            total = sums[i][:, span] if n_sums else None
            for band, shard in zip(bands, shards):
                part = jnp.dot(rows[:, band], shard[j], preferred_element_type=F32)
                total = part if total is None else total + part
            out[:, span] = total.astype(out.dtype)
    for copy in copies:
        copy.wait()


def place_of(at_ref, y, z):
    return lax.rem(at_ref[Y] + y, 4) * 2 + lax.rem(at_ref[Z] + z, 2)


def project(ids, mine, theirs, shards, offsets, sums=(), give=F32, after=()):
    rows, _ = mine.shape
    n = len(shards)
    vmem = pl.BlockSpec(memory_space=pltpu.VMEM)
    cols = 3 * shards[0].shape[-1]
    return pl.pallas_call(
        functools.partial(project_kernel, offsets, len(sums)),
        in_specs=[pl.BlockSpec(memory_space=pltpu.SMEM)]
        + [vmem] * (2 + n + len(sums))
        + [pl.BlockSpec(memory_space=pl.ANY)] * len(after),
        out_specs=(vmem, vmem, pl.BlockSpec(memory_space=pl.ANY)),
        out_shape=(
            shape(rows, cols, dtype=F32),
            shape(rows, cols, dtype=give),
            shape(n, *shards[0].shape),
        ),
        scratch_shapes=[pltpu.SemaphoreType.DMA((n,))],
        compiler_params=PARAMS,
        cost_estimate=cost(1, 1),
    )(ids, mine, theirs, *shards, *sums, *after)


def project_last_kernel(offset, carried, at_ref, mine_ref, given_ref, keep_ref, came_ref, cot_ref, *refs):
    shards, heads_ref = refs[:6], refs[-1 - carried]
    depth, cols = shards[0].shape[-2:]
    band = pl.ds(pl.multiple_of(place_of(at_ref, *offset) * depth, depth), depth)
    heads = range(heads_ref.shape[0])
    for j in range(3):
        span = slice(j * cols, (j + 1) * cols)
        total = keep_ref[:, span] + came_ref[:, span].astype(F32)
        total += jnp.dot(mine_ref[:, band], shards[j][0], preferred_element_type=F32)
        total += jnp.dot(given_ref[:, band], shards[3 + j][0], preferred_element_type=F32)
        for h in heads:
            heads_ref[h, :, j * HS : (j + 1) * HS] = total[:, h * HS : (h + 1) * HS].astype(BF)
    for h in heads:
        heads_ref[h, :, 3 * HS :] = cot_ref[:, h * HS : (h + 1) * HS]


def project_last(ids, mine, given, keep, came, cotangent, pieces, offset, heads, carry, after):
    rows, cols = keep.shape
    n = len(carry)
    vmem = pl.BlockSpec(memory_space=pltpu.VMEM)
    free = pl.BlockSpec(memory_space=pl.ANY)
    return pl.pallas_call(
        functools.partial(project_last_kernel, offset, n),
        in_specs=[pl.BlockSpec(memory_space=pltpu.SMEM)]
        + [vmem] * (5 + len(pieces))
        + [free] * (n + len(after)),
        out_specs=(vmem,) + (free,) * n,
        out_shape=(shape(heads, rows, cols // heads + HS),) + tuple(shape(*c.shape) for c in carry),
        input_output_aliases={6 + len(pieces) + i: 1 + i for i in range(n)},
        compiler_params=PARAMS,
        cost_estimate=cost(1, 1),
    )(ids, mine, given, keep, came, cotangent, *pieces, *carry, *after)


def attention_kernel(q_rows, qkv_ref, *refs):
    att_ref, grad_ref, dk_ref, dv_ref = refs[-4:]
    scale = 1.0 / math.sqrt(HS)
    key = qkv_ref[:, HS : 2 * HS]
    value = qkv_ref[:, 2 * HS : 3 * HS]
    key_t = key.T
    value_t = value.T
    for i in range(qkv_ref.shape[0] // q_rows):
        rows = pl.ds(i * q_rows, q_rows)
        query = qkv_ref[rows, 0:HS]
        dout = qkv_ref[rows, 3 * HS :]
        scores = dot(key, query, 1, 1) * (scale * math.log2(math.e))
        top = jnp.max(scores, axis=0, keepdims=True)
        expo = jnp.exp2(scores - top)
        prob = expo * (1.0 / jnp.sum(expo, axis=0, keepdims=True))
        prob_bf = prob.astype(BF)
        att = dot(value_t, prob_bf, 1, 0).T.astype(BF)
        att_ref[rows, :] = att
        row_dot = jnp.sum(
            dout.astype(F32).T * att.astype(F32).T, axis=0, keepdims=True
        )
        dprob = dot(value, dout, 1, 1)
        dscore = (prob * (dprob - row_dot)).astype(BF)
        grad_ref[rows, 0:HS] = (dot(key_t, dscore, 1, 0) * scale).T.astype(BF)
        dv = dot(prob_bf, dout, 1, 0)
        dk = dot(dscore, query, 1, 0)
        if i == 0:
            dv_ref[...] = dv
            dk_ref[...] = dk
        else:
            dv_ref[...] += dv
            dk_ref[...] += dk
    grad_ref[:, HS : 2 * HS] = (dk_ref[...] * scale).astype(BF)
    grad_ref[:, 2 * HS : 3 * HS] = dv_ref[...].astype(BF)


def attention(qkv, after):
    n = qkv.shape[0]
    vmem = pl.BlockSpec(memory_space=pltpu.VMEM)
    return pl.pallas_call(
        functools.partial(attention_kernel, min(256, n)),
        out_shape=(shape(n, HS), shape(n, 3 * HS)),
        in_specs=[vmem] + [pl.BlockSpec(memory_space=pl.ANY)] * len(after),
        out_specs=(vmem,) * 2,
        scratch_shapes=[pltpu.VMEM((n, HS), F32), pltpu.VMEM((n, HS), F32)],
        compiler_params=PARAMS,
        cost_estimate=cost(BUSY, 1),
    )(qkv, *after)


def write_stat(ref, at, stat):
    ref[at:, :] = jnp.zeros((ref.shape[0] - at, ref.shape[1]), BF)
    rest = stat
    for i in range(3):
        top = rest.astype(BF)
        ref[at + i : at + i + 1, :] = top
        rest = rest - top.astype(F32)


def read_stat(ref, at):
    return sum(ref[at + i : at + i + 1, :].astype(F32) for i in range(3))


def norm_kernel(width, halves, spots, places, n_in, at_ref, g_ref, p_ref, *refs):
    shards = refs[:n_in]
    n_out = max(spot[0] for spot in spots) + 1
    outs, stat_ref = refs[-4 - n_out : -4], refs[-4]
    w_ref, flat_ref, sems = refs[-3:]
    _, kinds, depth, cols = w_ref.shape
    band = depth // 2
    quarters = len(places) // 2

    def copy(step, core, j, source):
        to = lax.rem(at_ref[CORE] + core, 2)
        at = pl.ds(pl.multiple_of(to * band, band), band)
        return pltpu.make_async_copy(source, w_ref.at[step, j, at], sems.at[step, core, j])

    for step, (by, half) in enumerate(halves):
        y_off = lax.rem(at_ref[T] + (by + quarters) - at_ref[Y], quarters)
        where = y_off * 2 + lax.rem(at_ref[Z] + half, 2)
        for place, cores in enumerate(places):

            @pl.when(where == place)
            def _(step=step, cores=cores):
                for core, pieces in enumerate(cores):
                    for j, (which, at) in enumerate(pieces):
                        copy(step, core, j, shards[which].at[*at]).start()

    heads, _, _ = g_ref.shape
    for h in range(heads):
        for j in range(kinds):
            at = (j * heads + h) * HS
            flat_ref[at : at + HS, :] = g_ref[h, :, j * HS : (j + 1) * HS].T
    total = sum(
        g_ref[h, :, j * HS : (j + 1) * HS].astype(F32)
        * p_ref[h, :, j * HS : (j + 1) * HS].astype(F32)
        for h in range(heads)
        for j in range(kinds)
    )
    stat = jnp.sum(total.T, axis=0, keepdims=True) * (1.0 / width)
    stat_ref[...] = stat
    for ref in outs:
        if ref.shape[0] % 128:
            write_stat(ref, ref.shape[0] - 16, stat)

    for step, (which, at) in enumerate(spots):
        for core in range(2):
            for j in range(kinds):
                copy(step, core, j, shards[0].at[0]).wait()
        total = sum(
            dot(w_ref[step, j], flat_ref[j * cols : (j + 1) * cols, :], 1, 0)
            for j in range(kinds)
        )
        outs[which][at : at + depth, :] = total.astype(BF)


def norm_halves(ids, grads, proj, shards, places, halves, spots, sizes, width, after=()):
    heads, rows, _ = grads.shape
    kinds = 3
    band, cols = shards[0].shape[-2:]
    n = len(spots)
    sizes = (*sizes, 1)
    vmem = pl.BlockSpec(memory_space=pltpu.VMEM)
    free = pl.BlockSpec(memory_space=pl.ANY)
    return pl.pallas_call(
        functools.partial(norm_kernel, width, halves, spots, places, len(shards)),
        in_specs=[pl.BlockSpec(memory_space=pltpu.SMEM), vmem, vmem]
        + [free] * (len(shards) + len(after)),
        out_specs=(vmem,) * len(sizes),
        out_shape=tuple(shape(s, rows) for s in sizes[:-1]) + (shape(1, rows, dtype=F32),),
        scratch_shapes=[
            pltpu.VMEM((n, kinds, 2 * band, cols), BF),
            pltpu.VMEM((kinds * cols, rows), BF),
            pltpu.SemaphoreType.DMA((n, 2, kinds)),
        ],
        compiler_params=PARAMS,
        cost_estimate=cost(1, 1),
    )(ids, grads, proj, *shards, *after)


def add_kernel(up_part, up_in, stat_in, down_part, down_in, stat_ref, *refs):
    up_out, down_out = refs[-2:]
    half = up_part.shape[0]
    for part, came, out in ((up_part, up_in, up_out), (down_part, down_in, down_out)):
        out[:half, :] = (part[...].astype(F32) + came[...].astype(F32)).astype(BF)
    write_stat(up_out, half, stat_ref[...] + read_stat(stat_in, 0))
    write_stat(down_out, half, stat_ref[...])


def add_messages(up_part, up_in, down_part, down_in, stat, after=()):
    half, rows = up_part.shape
    block = pl.BlockSpec((half, rows), lambda i: (0, 0))
    out = pl.BlockSpec((half + 16, rows), lambda i: (0, 0))
    end = pl.BlockSpec((16, rows), lambda i: (2 * half // 16, 0))
    return pl.pallas_call(
        add_kernel,
        grid=(1,),
        out_shape=(shape(half + 16, rows),) * 2,
        in_specs=[block, block, end, block, block, pl.BlockSpec((1, rows), lambda i: (0, 0))]
        + [pl.BlockSpec(memory_space=pl.ANY)] * len(after),
        out_specs=(out, out),
        compiler_params=PARAMS,
        cost_estimate=cost(1, 1),
    )(up_part, up_in, up_in, down_part, down_in, stat, *after)


def finish_kernel(at_ref, own0, own1, up0, up1, down0, down1, tok_ref, root_ref, stat_ref, *refs):
    out_ref = refs[-1]
    half = own0.shape[0]
    stat = stat_ref[...] + read_stat(up0, half) + read_stat(down1, half)
    stat = jnp.broadcast_to(stat, (HS, stat.shape[1])).T[:, 0:1]
    root = root_ref[...]
    parts = (
        (own0[...], up0[:half, :], down0[half : 2 * half, :]),
        (own1[...], up1[half : 2 * half, :], down1[:half, :]),
    )
    for i, part in enumerate(parts):
        span = slice(i * half, (i + 1) * half)
        total = sum(p.astype(F32) for p in part)
        unit = tok_ref[:, span].astype(F32) / root
        out_ref[:, span] = ((total.T - unit * stat) / root).astype(BF)


def finish(ids, parts, tokens, root, stat, after=()):
    half, rows = parts[0].shape
    share = 2 * half
    tile = HS
    some = lambda a: pl.BlockSpec((a.shape[0], tile), lambda i, at: (0, i))
    return pl.pallas_call(
        finish_kernel,
        grid_spec=pltpu.PrefetchScalarGridSpec(
            num_scalar_prefetch=1,
            grid=(rows // tile,),
            in_specs=[some(p) for p in parts]
            + [pl.BlockSpec((tile, share), lambda i, at: (i, at[T]))]
            + [pl.BlockSpec((tile, 1), lambda i, at: (i, 0)), some(stat)]
            + [pl.BlockSpec(memory_space=pl.ANY)] * len(after),
            out_specs=pl.BlockSpec((tile, share), lambda i, at: (i, 0)),
        ),
        out_shape=shape(rows, share),
        compiler_params=PARAMS,
        cost_estimate=cost(BUSY, 1),
    )(ids, *parts, tokens, root, stat, *after)


def outer_kernel(tile, spots, at_ref, *refs):
    out_ref, a_ref, g_ref, sems = refs[-4:]
    m = max(spot[0] for spot in spots) + 1
    arrays, (mine_ref, other_ref) = refs[:m], refs[m : m + 2]
    n, rows, _ = mine_ref.shape
    depth = a_ref.shape[0]
    copies = []
    for step in range(depth // tile):
        span = pl.ds(step * tile, tile)
        some = []
        for i, (which, at, _, _) in enumerate(spots):
            to = a_ref.at[span, pl.ds(i * rows, rows)]
            some.append(pltpu.make_async_copy(arrays[which].at[at, span], to, sems.at[step, i]))
            some[-1].start()
        copies.append(some)
    for i, (_, _, by, frame) in enumerate(spots):
        ref = other_ref if frame else mine_ref
        g_ref[i * rows : (i + 1) * rows, :] = ref[lax.rem(at_ref[X] + by, n)]
    for step, some in enumerate(copies):
        for copy in some:
            copy.wait()
        span = slice(step * tile, (step + 1) * tile)
        out_ref[span, :] = jnp.dot(
            a_ref[span, :], g_ref[...], preferred_element_type=F32
        ).astype(BF)


def outer(ids, arrays, spots, mine, other, after):
    _, depth, rows = arrays[0].shape
    cols = mine.shape[2]
    n = len(spots)
    tile = 512
    vmem = pl.BlockSpec(memory_space=pltpu.VMEM)
    return pl.pallas_call(
        functools.partial(outer_kernel, tile, spots),
        in_specs=[pl.BlockSpec(memory_space=pltpu.SMEM)]
        + [pl.BlockSpec(memory_space=pl.ANY)] * len(arrays)
        + [vmem, vmem]
        + [pl.BlockSpec(memory_space=pl.ANY)] * len(after),
        out_specs=vmem,
        out_shape=shape(depth, cols),
        scratch_shapes=[
            pltpu.VMEM((depth, n * rows), BF),
            pltpu.VMEM((n * rows, cols), BF),
            pltpu.SemaphoreType.DMA((depth // tile, n)),
        ],
        compiler_params=PARAMS,
        cost_estimate=cost(1, 1),
    )(ids, *arrays, mine, other, *after)


def split_kernel(at_ref, part_ref, *refs):
    keep_ref, give_ref = refs[-2:]
    n, _, rows, _ = part_ref.shape
    for ref, which in ((keep_ref, at_ref[Z]), (give_ref, 1 - at_ref[Z])):
        ref[...] = sum(part_ref[i, which].astype(F32) for i in range(n)).astype(ref.dtype)


def split(ids, part, after=()):
    _, _, rows, cols = part.shape
    vmem = pl.BlockSpec(memory_space=pltpu.VMEM)
    return pl.pallas_call(
        split_kernel,
        in_specs=[pl.BlockSpec(memory_space=pltpu.SMEM), vmem]
        + [pl.BlockSpec(memory_space=pl.ANY)] * len(after),
        out_specs=(vmem, vmem),
        out_shape=(shape(rows, cols, dtype=F32), shape(rows, cols)),
        compiler_params=PARAMS,
        cost_estimate=cost(1, 1),
    )(ids, part, *after)


def merge_kernel(keep_ref, came_ref, att_ref, *refs):
    out_ref = refs[-1]
    total = (keep_ref[...] + came_ref[...].astype(F32)).astype(BF)
    cols = total.shape[1]
    for i in range(out_ref.shape[0]):
        out_ref[i, :, :cols] = total
        out_ref[i, :, cols:] = att_ref[i]


def merge(keep, came, att, after=()):
    rows, cols = keep.shape
    n, _, more = att.shape
    vmem = pl.BlockSpec(memory_space=pltpu.VMEM)
    return pl.pallas_call(
        merge_kernel,
        out_shape=shape(n, rows, cols + more),
        in_specs=[vmem] * 3 + [pl.BlockSpec(memory_space=pl.ANY)] * len(after),
        out_specs=vmem,
        compiler_params=PARAMS,
        cost_estimate=cost(1, 1),
    )(keep, came, att, *after)


def unpack_kernel(in_ref, w_ref, att_ref):
    for h in range(in_ref.shape[0]):
        span = slice(h * HS, (h + 1) * HS)
        for j in range(3):
            w_ref[j, :, span] = in_ref[h, :, j * HS : (j + 1) * HS].astype(F32)
        att_ref[:, span] = in_ref[h, :, 3 * HS :]


def unpack(last):
    heads, rows, more = last.shape
    tile = rows // 4
    return pl.pallas_call(
        unpack_kernel,
        grid=(rows // tile,),
        in_specs=[pl.BlockSpec((heads, tile, more), lambda i: (0, i, 0))],
        out_specs=(
            pl.BlockSpec((3, tile, heads * HS), lambda i: (0, i, 0)),
            pl.BlockSpec((tile, heads * HS), lambda i: (i, 0)),
        ),
        out_shape=(shape(3, rows, heads * HS, dtype=F32), shape(rows, heads * HS)),
        compiler_params=SMALL,
        cost_estimate=cost(1, 1),
    )(last)


def gate(arrays, after=(), pieces=()):
    n, m = len(arrays), len(arrays) + len(after)
    free = pl.BlockSpec(memory_space=pl.ANY)

    def kernel(*refs):
        outs, sems = refs[m + n : -1], refs[-1]
        copies = [
            pltpu.make_async_copy(refs[which].at[pl.ds(at, 1)], out, sems.at[i])
            for i, ((which, at), out) in enumerate(zip(pieces, outs))
        ]
        for copy in copies:
            copy.start()
        for copy in copies:
            copy.wait()

    return pl.pallas_call(
        kernel,
        in_specs=[free] * m,
        out_specs=(free,) * n + (pl.BlockSpec(memory_space=pltpu.VMEM),) * len(pieces),
        out_shape=tuple(shape(*a.shape) for a in arrays)
        + tuple(shape(1, *arrays[which].shape[1:]) for which, _ in pieces),
        scratch_shapes=[pltpu.SemaphoreType.DMA((max(len(pieces), 1),))],
        input_output_aliases={i: i for i in range(n)},
        compiler_params=PARAMS,
        cost_estimate=cost(1, 1),
    )(*arrays, *after)


def shift(x, axis, by):
    n = lax.axis_size(axis)
    return lax.ppermute(x, axis, [(i, (i + by) % n) for i in range(n)])


def per_device(tokens, weights, cotangent):
    _, rows, width = tokens.shape
    w_rows, _, cols = weights.shape
    heads = cols // HS
    n_x, n_y = (lax.axis_size(a) for a in ("x", "y"))
    ids = jnp.stack([lax.axis_index(a) for a in ("core", "x", "zh", "y", "zl")])
    tokens = tokens.reshape(rows, width)
    half = width // lax.axis_size("zh") // 2

    swap = lambda a: shift(a, "core", 1)
    own = weights.transpose(1, 0, 2)
    left, right, other = shift(own, "y", 1), shift(own, "y", -1), shift(own, "zl", 1)
    root, mine, given, theirs, mine_t, theirs_t = unit_rows(ids, tokens, swap(tokens), w_rows)
    left, right, other = gate((left, right, other), (mine_t,))

    left_0, right_1 = shift(mine_t, "x", 1), shift(theirs_t, "x", -1)
    left_1, right_0 = shift(theirs_t, "x", 1), shift(mine_t, "x", -1)

    near = ((0, 0), (3, 0), (1, 0), (0, 1))
    *sums, stack_0 = project(ids, mine, theirs, (own, left, right, other), near, after=(left_0, right_1))
    far, other_left, other_right, *pieces = gate(
        (shift(left, "y", 1), shift(left, "zl", 1), shift(other, "y", -1)),
        sums,
        ((0, 0), (1, 1), (2, 2)),
    )
    then = ((2, 0), (3, 1), (1, 1))
    keep, give, stack_1 = project(
        ids, mine, theirs, (far, other_left, other_right), then, sums, BF
    )
    *pieces, give = gate(
        (shift(pieces[0], "zl", 1), shift(pieces[1], "y", 1), shift(pieces[2], "y", -1), give)
    )
    pieces = (*pieces, *(swap(p) for p in pieces))
    proj, stack_0, stack_1 = project_last(
        ids, mine, given, keep, swap(give), cotangent.reshape(rows, cols), pieces, (2, 1), heads,
        (stack_0, stack_1), (left_1, right_0),
    )

    far_0, far_1 = shift(left_0, "x", 1), shift(right_1, "x", -1)
    blocks = (mine_t, theirs_t, left_0, left_1, right_0, right_1, far_0, far_1)
    spots = tuple((i, 0, by, i % 2) for i, by in enumerate((0, 0, 3, 3, 1, 1, 2, 2)))
    qkv = lax.all_to_all(proj, "x", 0, 0, tiled=True).reshape(n_x * rows, 4 * HS)
    att, head_grads = attention(qkv, (far_0, far_1))

    shards = (*pieces, stack_0, swap(stack_0), stack_1, swap(stack_1))
    places = {(2, 1): [[(3 * core + j, (0,)) for j in range(3)] for core in range(2)]}
    for first, keys in ((6, near), (8, then)):
        for i, key in enumerate(keys):
            places[key] = [[(first + core, (i, j)) for j in range(3)] for core in range(2)]
    places = [places[(by, z)] for by in range(n_y) for z in range(2)]

    head_grads = head_grads.reshape(n_x, rows, 3 * HS)
    grads = lax.all_to_all(head_grads, "x", 0, 0, tiled=True)
    part = outer(ids, blocks, spots, head_grads, swap(head_grads), (shards[7], shards[9]))

    up, down, stat = norm_halves(
        ids, grads, proj, shards, places,
        ((2, 0), (1, 1), (2, 1), (3, 0)),
        ((0, 0), (0, half), (1, 0), (1, half)),
        (2 * half + 16, 2 * half),
        width,
    )
    up, down = shift(up, "zh", 1), shift(down, "zh", -1)
    up_part, down_part, own0, own1, _ = norm_halves(
        ids, grads, proj, shards, places,
        ((1, 0), (3, 1), (0, 0), (0, 1)),
        ((0, 0), (1, 0), (2, 0), (3, 0)),
        (half,) * 4,
        width,
        (stat,),
    )
    part = lax.all_to_all(part, "y", 0, 0, tiled=True).reshape(n_y, 2, w_rows, 3 * HS)
    keep, give = split(ids, part, (own0,))
    came = shift(give, "zl", 1)
    up_2, down_2 = add_messages(up_part, up, down_part, down, stat, (came,))
    last = merge(keep, came, att.reshape(n_x, rows, HS))
    up_2, down_2 = shift(up_2, "zh", 1), shift(down_2, "zh", -1)
    last = lax.all_to_all(last, "x", 0, 0, tiled=True)
    token_grad = finish(ids, (own0, own1, up_2, up, down, down_2), tokens, root, stat)
    weight_grad, attended = unpack(last)
    return attended[None], token_grad[None], weight_grad.transpose(1, 0, 2)


def solution(mesh):
    fine = Mesh(mesh.devices.reshape(4, 2, 2, 4, 4), ("y", "zl", "core", "x", "zh"))
    dp = ("y", "zl", "core")
    return jax.shard_map(
        per_device,
        mesh=fine,
        in_specs=(P(dp, "x", None), P(dp, None, "zh"), P(dp, "x", "zh")),
        out_specs=(P(dp, "x", "zh"), P(dp, "x", "zh"), P(dp, None, "zh")),
        check_vma=False,
    )
```

```python
import functools
import math

import jax
import jax.numpy as jnp
from jax import lax
from jax.experimental import pallas as pl
from jax.experimental.pallas import tpu as pltpu
from jax.sharding import Mesh
from jax.sharding import PartitionSpec as P

HS = 128
CORE, X, T, Y, Z = range(5)
BF = jnp.bfloat16
BUSY = 2 * 10**10
F32 = jnp.float32
PARAMS = pltpu.CompilerParams(vmem_limit_bytes=60 * 1024 * 1024)
SMALL = pltpu.CompilerParams(vmem_limit_bytes=24 * 1024 * 1024)


def dot(a, b, ca, cb):
    return lax.dot_general(a, b, (((ca,), (cb,)), ((), ())), preferred_element_type=F32)


def cost(flops, nbytes, exps=0):
    return pl.CostEstimate(flops=flops, bytes_accessed=nbytes, transcendentals=exps)


def shape(*dims, dtype=BF):
    return jax.ShapeDtypeStruct(dims, dtype)


def unit_kernel(at_ref, tok_ref, root_ref, *refs, band):
    tok = tok_ref[...].astype(F32)
    root = jnp.sqrt(jnp.mean(tok * tok, -1, keepdims=True) + 1e-05)
    root_ref[...] = root
    core = at_ref[CORE]
    mine_ref, mine_t_ref = refs[:2]
    for i in range(mine_ref.shape[1] // band):
        span = slice(i * band, (i + 1) * band)
        for ref, which in zip((mine_ref, *refs[2:]), (core, 1 - core)):
            at = pl.multiple_of((2 * i + which) * band, band)
            unit = (tok_ref[:, pl.ds(at, band)].astype(F32) / root).astype(BF)
            ref[:, span] = unit
            if ref is mine_ref:
                mine_t_ref[0, span, :] = unit.T


def unit_rows(ids, tokens, band, both):
    rows, width = tokens.shape
    tile = 128
    half = width // 2
    row = pl.BlockSpec((tile, half), lambda i, at: (i, 0))
    return pl.pallas_call(
        functools.partial(unit_kernel, band=band),
        grid_spec=pltpu.PrefetchScalarGridSpec(
            num_scalar_prefetch=1,
            grid=(rows // tile,),
            in_specs=[pl.BlockSpec((tile, width), lambda i, at: (i, 0))],
            out_specs=(pl.BlockSpec((tile, 1), lambda i, at: (i, 0)), row)
            + (pl.BlockSpec((1, half, tile), lambda i, at: (0, 0, i)),)
            + (row,) * both,
        ),
        out_shape=(shape(rows, 1, dtype=F32), shape(rows, half), shape(1, half, rows))
        + (shape(rows, half),) * both,
        compiler_params=PARAMS,
        cost_estimate=cost(BUSY, 1),
    )(ids, tokens)


def project_kernel(offsets, n_sums, at_ref, mine_ref, theirs_ref, *refs):
    keep_ref, give_ref, stack_ref, sems = refs[-4:]
    n = len(offsets)
    shards, sums = refs[:n], refs[n : n + n_sums]
    copies = [pltpu.make_async_copy(w, stack_ref.at[i], sems.at[i]) for i, w in enumerate(shards)]
    for copy in copies:
        copy.start()
    kinds, depth, cols = shards[0].shape
    bands = [
        pl.ds(pl.multiple_of(place_of(at_ref, *offset) * depth, depth), depth) for offset in offsets
    ]
    for i, (rows, out) in enumerate(((mine_ref, keep_ref), (theirs_ref, give_ref))):
        for j in range(kinds):
            span = slice(j * cols, (j + 1) * cols)
            total = sums[i][:, span] if n_sums else None
            for band, shard in zip(bands, shards):
                part = jnp.dot(rows[:, band], shard[j], preferred_element_type=F32)
                total = part if total is None else total + part
            out[:, span] = total.astype(out.dtype)
    for copy in copies:
        copy.wait()


def place_of(at_ref, y, z):
    return lax.rem(at_ref[Y] + y, 4) * 2 + lax.rem(at_ref[Z] + z, 2)


def project(ids, mine, theirs, shards, offsets, sums=(), give=F32, after=()):
    rows, _ = mine.shape
    n = len(shards)
    vmem = pl.BlockSpec(memory_space=pltpu.VMEM)
    cols = 3 * shards[0].shape[-1]
    return pl.pallas_call(
        functools.partial(project_kernel, offsets, len(sums)),
        in_specs=[pl.BlockSpec(memory_space=pltpu.SMEM)]
        + [vmem] * (2 + n + len(sums))
        + [pl.BlockSpec(memory_space=pl.ANY)] * len(after),
        out_specs=(vmem, vmem, pl.BlockSpec(memory_space=pl.ANY)),
        out_shape=(
            shape(rows, cols, dtype=F32),
            shape(rows, cols, dtype=give),
            shape(n, *shards[0].shape),
        ),
        scratch_shapes=[pltpu.SemaphoreType.DMA((n,))],
        compiler_params=PARAMS,
        cost_estimate=cost(1, 1),
    )(ids, mine, theirs, *shards, *sums, *after)


def project_last_kernel(offset, carried, at_ref, mine_ref, given_ref, keep_ref, came_ref, cot_ref, *refs):
    shards, heads_ref = refs[:6], refs[-1 - carried]
    depth, cols = shards[0].shape[-2:]
    band = pl.ds(pl.multiple_of(place_of(at_ref, *offset) * depth, depth), depth)
    heads = range(heads_ref.shape[0])
    for j in range(3):
        span = slice(j * cols, (j + 1) * cols)
        total = keep_ref[:, span] + came_ref[:, span].astype(F32)
        total += jnp.dot(mine_ref[:, band], shards[j][0], preferred_element_type=F32)
        total += jnp.dot(given_ref[:, band], shards[3 + j][0], preferred_element_type=F32)
        for h in heads:
            heads_ref[h, :, j * HS : (j + 1) * HS] = total[:, h * HS : (h + 1) * HS].astype(BF)
    for h in heads:
        heads_ref[h, :, 3 * HS :] = cot_ref[:, h * HS : (h + 1) * HS]


def project_last(ids, mine, given, keep, came, cotangent, pieces, offset, heads, carry, after):
    rows, cols = keep.shape
    n = len(carry)
    vmem = pl.BlockSpec(memory_space=pltpu.VMEM)
    free = pl.BlockSpec(memory_space=pl.ANY)
    return pl.pallas_call(
        functools.partial(project_last_kernel, offset, n),
        in_specs=[pl.BlockSpec(memory_space=pltpu.SMEM)]
        + [vmem] * (5 + len(pieces))
        + [free] * (n + len(after)),
        out_specs=(vmem,) + (free,) * n,
        out_shape=(shape(heads, rows, cols // heads + HS),) + tuple(shape(*c.shape) for c in carry),
        input_output_aliases={6 + len(pieces) + i: 1 + i for i in range(n)},
        compiler_params=PARAMS,
        cost_estimate=cost(1, 1),
    )(ids, mine, given, keep, came, cotangent, *pieces, *carry, *after)


def attention_kernel(q_rows, qkv_ref, *refs):
    att_ref, grad_ref, dk_ref, dv_ref = refs[-4:]
    scale = 1.0 / math.sqrt(HS)
    key = qkv_ref[:, HS : 2 * HS]
    value = qkv_ref[:, 2 * HS : 3 * HS]
    key_t = key.T
    value_t = value.T
    for i in range(qkv_ref.shape[0] // q_rows):
        rows = pl.ds(i * q_rows, q_rows)
        query = qkv_ref[rows, 0:HS]
        dout = qkv_ref[rows, 3 * HS :]
        scores = dot(key, query, 1, 1)
        to_log2 = scale * math.log2(math.e)
        top = jnp.max(scores, axis=0, keepdims=True) * to_log2
        expo = jnp.exp2(scores * to_log2 - top)
        prob = expo * (1.0 / jnp.sum(expo, axis=0, keepdims=True))
        prob_bf = prob.astype(BF)
        att = dot(value_t, prob_bf, 1, 0).T.astype(BF)
        att_ref[rows, :] = att
        row_dot = jnp.sum((dout.astype(F32) * att.astype(F32)).T, axis=0, keepdims=True)
        dprob = dot(value, dout, 1, 1)
        dscore = (prob * (dprob - row_dot)).astype(BF)
        grad_ref[rows, 0:HS] = (dot(key_t, dscore, 1, 0) * scale).T.astype(BF)
        dv = dot(prob_bf, dout, 1, 0)
        dk = dot(dscore, query, 1, 0)
        if i == 0:
            dv_ref[...] = dv
            dk_ref[...] = dk
        else:
            dv_ref[...] += dv
            dk_ref[...] += dk
    grad_ref[:, HS : 2 * HS] = (dk_ref[...] * scale).astype(BF)
    grad_ref[:, 2 * HS : 3 * HS] = dv_ref[...].astype(BF)


def attention(qkv, after):
    n = qkv.shape[0]
    vmem = pl.BlockSpec(memory_space=pltpu.VMEM)
    return pl.pallas_call(
        functools.partial(attention_kernel, n),
        out_shape=(shape(n, HS), shape(n, 3 * HS)),
        in_specs=[vmem] + [pl.BlockSpec(memory_space=pl.ANY)] * len(after),
        out_specs=(vmem,) * 2,
        scratch_shapes=[pltpu.VMEM((n, HS), F32), pltpu.VMEM((n, HS), F32)],
        compiler_params=PARAMS,
        cost_estimate=cost(BUSY, 1),
    )(qkv, *after)


def write_stat(ref, at, stat):
    ref[at:, :] = jnp.zeros((ref.shape[0] - at, ref.shape[1]), BF)
    rest = stat
    for i in range(3):
        top = rest.astype(BF)
        ref[at + i : at + i + 1, :] = top
        rest = rest - top.astype(F32)


def read_stat(ref, at):
    return sum(ref[at + i : at + i + 1, :].astype(F32) for i in range(3))


def norm_kernel(width, halves, spots, places, n_in, at_ref, g_ref, p_ref, *refs):
    shards = refs[:n_in]
    n_out = max(spot[0] for spot in spots) + 1
    outs, stat_ref = refs[-4 - n_out : -4], refs[-4]
    w_ref, flat_ref, sems = refs[-3:]
    _, kinds, depth, cols = w_ref.shape
    band = depth // 2
    quarters = len(places) // 2

    def copy(step, core, j, source):
        to = lax.rem(at_ref[CORE] + core, 2)
        at = pl.ds(pl.multiple_of(to * band, band), band)
        return pltpu.make_async_copy(source, w_ref.at[step, j, at], sems.at[step, core, j])

    for step, (by, half) in enumerate(halves):
        y_off = lax.rem(at_ref[T] + (by + quarters) - at_ref[Y], quarters)
        where = y_off * 2 + lax.rem(at_ref[Z] + half, 2)
        for place, cores in enumerate(places):

            @pl.when(where == place)
            def _(step=step, cores=cores):
                for core, pieces in enumerate(cores):
                    for j, (which, at) in enumerate(pieces):
                        copy(step, core, j, shards[which].at[*at]).start()

    heads, _, _ = g_ref.shape
    for h in range(heads):
        for j in range(kinds):
            at = (j * heads + h) * HS
            flat_ref[at : at + HS, :] = g_ref[h, :, j * HS : (j + 1) * HS].T
    total = sum(
        g_ref[h, :, j * HS : (j + 1) * HS].astype(F32)
        * p_ref[h, :, j * HS : (j + 1) * HS].astype(F32)
        for h in range(heads)
        for j in range(kinds)
    )
    stat = jnp.sum(total.T, axis=0, keepdims=True) * (1.0 / width)
    stat_ref[...] = stat
    for ref in outs:
        if ref.shape[0] % 128:
            write_stat(ref, ref.shape[0] - 16, stat)

    for step, (which, at) in enumerate(spots):
        for core in range(2):
            for j in range(kinds):
                copy(step, core, j, shards[0].at[0]).wait()
        total = sum(
            dot(w_ref[step, j], flat_ref[j * cols : (j + 1) * cols, :], 1, 0)
            for j in range(kinds)
        )
        outs[which][at : at + depth, :] = total.astype(BF)


def norm_halves(ids, grads, proj, shards, places, halves, spots, sizes, width, after=()):
    heads, rows, _ = grads.shape
    kinds = 3
    band, cols = shards[0].shape[-2:]
    n = len(spots)
    sizes = (*sizes, 1)
    vmem = pl.BlockSpec(memory_space=pltpu.VMEM)
    free = pl.BlockSpec(memory_space=pl.ANY)
    return pl.pallas_call(
        functools.partial(norm_kernel, width, halves, spots, places, len(shards)),
        in_specs=[pl.BlockSpec(memory_space=pltpu.SMEM), vmem, vmem]
        + [free] * (len(shards) + len(after)),
        out_specs=(vmem,) * len(sizes),
        out_shape=tuple(shape(s, rows) for s in sizes[:-1]) + (shape(1, rows, dtype=F32),),
        scratch_shapes=[
            pltpu.VMEM((n, kinds, 2 * band, cols), BF),
            pltpu.VMEM((kinds * cols, rows), BF),
            pltpu.SemaphoreType.DMA((n, 2, kinds)),
        ],
        compiler_params=PARAMS,
        cost_estimate=cost(1, 1),
    )(ids, grads, proj, *shards, *after)


def add_kernel(up_part, up_in, stat_in, down_part, down_in, stat_ref, *refs):
    up_out, down_out = refs[-2:]
    half = up_part.shape[0]
    for part, came, out in ((up_part, up_in, up_out), (down_part, down_in, down_out)):
        out[:half, :] = (part[...].astype(F32) + came[...].astype(F32)).astype(BF)
    write_stat(up_out, half, stat_ref[...] + read_stat(stat_in, 0))
    write_stat(down_out, half, stat_ref[...])


def add_messages(up_part, up_in, down_part, down_in, stat, after=()):
    half, rows = up_part.shape
    block = pl.BlockSpec((half, rows), lambda i: (0, 0))
    out = pl.BlockSpec((half + 16, rows), lambda i: (0, 0))
    end = pl.BlockSpec((16, rows), lambda i: (2 * half // 16, 0))
    return pl.pallas_call(
        add_kernel,
        grid=(1,),
        out_shape=(shape(half + 16, rows),) * 2,
        in_specs=[block, block, end, block, block, pl.BlockSpec((1, rows), lambda i: (0, 0))]
        + [pl.BlockSpec(memory_space=pl.ANY)] * len(after),
        out_specs=(out, out),
        compiler_params=PARAMS,
        cost_estimate=cost(1, 1),
    )(up_part, up_in, up_in, down_part, down_in, stat, *after)


def finish_kernel(at_ref, own0, own1, up0, up1, down0, down1, tok_ref, root_ref, stat_ref, *refs):
    out_ref = refs[-1]
    half = own0.shape[0]
    stat = stat_ref[...] + read_stat(up0, half) + read_stat(down1, half)
    stat = jnp.broadcast_to(stat, (HS, stat.shape[1])).T[:, 0:1]
    root = root_ref[...]
    parts = (
        (own0[...], up0[:half, :], down0[half : 2 * half, :]),
        (own1[...], up1[half : 2 * half, :], down1[:half, :]),
    )
    for i, part in enumerate(parts):
        span = slice(i * half, (i + 1) * half)
        total = sum(p.astype(F32) for p in part)
        unit = tok_ref[:, span].astype(F32) / root
        out_ref[:, span] = ((total.T - unit * stat) / root).astype(BF)


def finish(ids, parts, tokens, root, stat, after=()):
    half, rows = parts[0].shape
    share = 2 * half
    tile = HS
    some = lambda a: pl.BlockSpec((a.shape[0], tile), lambda i, at: (0, i))
    return pl.pallas_call(
        finish_kernel,
        grid_spec=pltpu.PrefetchScalarGridSpec(
            num_scalar_prefetch=1,
            grid=(rows // tile,),
            in_specs=[some(p) for p in parts]
            + [pl.BlockSpec((tile, share), lambda i, at: (i, at[T]))]
            + [pl.BlockSpec((tile, 1), lambda i, at: (i, 0)), some(stat)]
            + [pl.BlockSpec(memory_space=pl.ANY)] * len(after),
            out_specs=pl.BlockSpec((tile, share), lambda i, at: (i, 0)),
        ),
        out_shape=shape(rows, share),
        compiler_params=PARAMS,
        cost_estimate=cost(BUSY, 1),
    )(ids, *parts, tokens, root, stat, *after)


def outer_kernel(tile, spots, at_ref, *refs):
    out_ref, a_ref, g_ref, sems = refs[-4:]
    m = max(spot[0] for spot in spots) + 1
    arrays, (mine_ref, other_ref) = refs[:m], refs[m : m + 2]
    n, rows, _ = mine_ref.shape
    depth = a_ref.shape[0]
    copies = []
    for step in range(depth // tile):
        span = pl.ds(step * tile, tile)
        some = []
        for i, (which, at, _, _) in enumerate(spots):
            to = a_ref.at[span, pl.ds(i * rows, rows)]
            some.append(pltpu.make_async_copy(arrays[which].at[at, span], to, sems.at[step, i]))
            some[-1].start()
        copies.append(some)
    for i, (_, _, by, frame) in enumerate(spots):
        ref = other_ref if frame else mine_ref
        g_ref[i * rows : (i + 1) * rows, :] = ref[lax.rem(at_ref[X] + by, n)]
    for step, some in enumerate(copies):
        for copy in some:
            copy.wait()
        span = slice(step * tile, (step + 1) * tile)
        out_ref[span, :] = jnp.dot(
            a_ref[span, :], g_ref[...], preferred_element_type=F32
        ).astype(BF)


def outer(ids, arrays, spots, mine, other, after):
    _, depth, rows = arrays[0].shape
    cols = mine.shape[2]
    n = len(spots)
    tile = 512
    vmem = pl.BlockSpec(memory_space=pltpu.VMEM)
    return pl.pallas_call(
        functools.partial(outer_kernel, tile, spots),
        in_specs=[pl.BlockSpec(memory_space=pltpu.SMEM)]
        + [pl.BlockSpec(memory_space=pl.ANY)] * len(arrays)
        + [vmem, vmem]
        + [pl.BlockSpec(memory_space=pl.ANY)] * len(after),
        out_specs=vmem,
        out_shape=shape(depth, cols),
        scratch_shapes=[
            pltpu.VMEM((depth, n * rows), BF),
            pltpu.VMEM((n * rows, cols), BF),
            pltpu.SemaphoreType.DMA((depth // tile, n)),
        ],
        compiler_params=PARAMS,
        cost_estimate=cost(1, 1),
    )(ids, *arrays, mine, other, *after)


def split_kernel(at_ref, part_ref, *refs):
    keep_ref, give_ref = refs[-2:]
    n, _, rows, _ = part_ref.shape
    for ref, which in ((keep_ref, at_ref[Z]), (give_ref, 1 - at_ref[Z])):
        ref[...] = sum(part_ref[i, which].astype(F32) for i in range(n)).astype(ref.dtype)


def split(ids, part, after=()):
    _, _, rows, cols = part.shape
    vmem = pl.BlockSpec(memory_space=pltpu.VMEM)
    return pl.pallas_call(
        split_kernel,
        in_specs=[pl.BlockSpec(memory_space=pltpu.SMEM), vmem]
        + [pl.BlockSpec(memory_space=pl.ANY)] * len(after),
        out_specs=(vmem, vmem),
        out_shape=(shape(rows, cols, dtype=F32), shape(rows, cols)),
        compiler_params=PARAMS,
        cost_estimate=cost(1, 1),
    )(ids, part, *after)


def merge_kernel(keep_ref, came_ref, att_ref, *refs):
    out_ref = refs[-1]
    total = (keep_ref[...] + came_ref[...].astype(F32)).astype(BF)
    cols = total.shape[1]
    for i in range(out_ref.shape[0]):
        out_ref[i, :, :cols] = total
        out_ref[i, :, cols:] = att_ref[i]


def merge(keep, came, att, after=()):
    rows, cols = keep.shape
    n, _, more = att.shape
    vmem = pl.BlockSpec(memory_space=pltpu.VMEM)
    return pl.pallas_call(
        merge_kernel,
        out_shape=shape(n, rows, cols + more),
        in_specs=[vmem] * 3 + [pl.BlockSpec(memory_space=pl.ANY)] * len(after),
        out_specs=vmem,
        compiler_params=PARAMS,
        cost_estimate=cost(1, 1),
    )(keep, came, att, *after)


def unpack_kernel(in_ref, w_ref, att_ref):
    for h in range(in_ref.shape[0]):
        span = slice(h * HS, (h + 1) * HS)
        for j in range(3):
            w_ref[j, :, span] = in_ref[h, :, j * HS : (j + 1) * HS].astype(F32)
        att_ref[:, span] = in_ref[h, :, 3 * HS :]


def unpack(last):
    heads, rows, more = last.shape
    tile = rows // 4
    return pl.pallas_call(
        unpack_kernel,
        grid=(rows // tile,),
        in_specs=[pl.BlockSpec((heads, tile, more), lambda i: (0, i, 0))],
        out_specs=(
            pl.BlockSpec((3, tile, heads * HS), lambda i: (0, i, 0)),
            pl.BlockSpec((tile, heads * HS), lambda i: (i, 0)),
        ),
        out_shape=(shape(3, rows, heads * HS, dtype=F32), shape(rows, heads * HS)),
        compiler_params=SMALL,
        cost_estimate=cost(1, 1),
    )(last)


def gate(arrays, after=(), pieces=()):
    n, m = len(arrays), len(arrays) + len(after)
    free = pl.BlockSpec(memory_space=pl.ANY)

    def kernel(*refs):
        outs, sems = refs[m + n : -1], refs[-1]
        copies = [
            pltpu.make_async_copy(refs[which].at[pl.ds(at, 1)], out, sems.at[i])
            for i, ((which, at), out) in enumerate(zip(pieces, outs))
        ]
        for copy in copies:
            copy.start()
        for copy in copies:
            copy.wait()

    return pl.pallas_call(
        kernel,
        in_specs=[free] * m,
        out_specs=(free,) * n + (pl.BlockSpec(memory_space=pltpu.VMEM),) * len(pieces),
        out_shape=tuple(shape(*a.shape) for a in arrays)
        + tuple(shape(1, *arrays[which].shape[1:]) for which, _ in pieces),
        scratch_shapes=[pltpu.SemaphoreType.DMA((max(len(pieces), 1),))],
        input_output_aliases={i: i for i in range(n)},
        compiler_params=PARAMS,
        cost_estimate=cost(1, 1),
    )(*arrays, *after)


def shift(x, axis, by):
    n = lax.axis_size(axis)
    return lax.ppermute(x, axis, [(i, (i + by) % n) for i in range(n)])


def per_device(tokens, weights, cotangent):
    _, rows, width = tokens.shape
    w_rows, _, cols = weights.shape
    heads = cols // HS
    n_x, n_y = (lax.axis_size(a) for a in ("x", "y"))
    ids = jnp.stack([lax.axis_index(a) for a in ("core", "x", "zh", "y", "zl")])
    tokens = tokens.reshape(rows, width)
    half = width // lax.axis_size("zh") // 2

    swap = lambda a: shift(a, "core", 1)
    own = weights.transpose(1, 0, 2)
    left, right, other = shift(own, "y", 1), shift(own, "y", -1), shift(own, "zl", 1)
    root, mine, mine_t, given = unit_rows(ids, tokens, w_rows, True)
    _, theirs, theirs_t = unit_rows(ids, swap(tokens), w_rows, False)
    left, right, other = gate((left, right, other), (theirs,))

    left_0, right_0 = shift(mine_t, "x", 1), shift(mine_t, "x", -1)
    left_1, right_1 = shift(theirs_t, "x", 1), shift(theirs_t, "x", -1)

    near = ((0, 0), (3, 0), (1, 0), (0, 1))
    *sums, stack_0 = project(ids, mine, theirs, (own, left, right, other), near, after=(left_0, right_0))
    far, other_left, other_right, *pieces = gate(
        (shift(left, "y", 1), shift(left, "zl", 1), shift(other, "y", -1)),
        sums,
        ((0, 0), (1, 1), (2, 2)),
    )
    then = ((2, 0), (3, 1), (1, 1))
    keep, give, stack_1 = project(
        ids, mine, theirs, (far, other_left, other_right), then, sums, BF
    )
    *pieces, give = gate(
        (shift(pieces[0], "zl", 1), shift(pieces[1], "y", 1), shift(pieces[2], "y", -1), give)
    )
    pieces = (*pieces, *(swap(p) for p in pieces))
    proj, stack_0, stack_1 = project_last(
        ids, mine, given, keep, swap(give), cotangent.reshape(rows, cols), pieces, (2, 1), heads,
        (stack_0, stack_1), (left_1, right_1),
    )

    far_0, far_1 = shift(left_0, "x", 1), shift(right_1, "x", -1)
    blocks = (mine_t, theirs_t, left_0, left_1, right_0, right_1, far_0, far_1)
    spots = tuple((i, 0, by, i % 2) for i, by in enumerate((0, 0, 3, 3, 1, 1, 2, 2)))
    qkv = lax.all_to_all(proj, "x", 0, 0, tiled=True).reshape(n_x * rows, 4 * HS)
    att, head_grads = attention(qkv, (far_0, far_1))

    shards = (*pieces, stack_0, swap(stack_0), stack_1, swap(stack_1))
    places = {(2, 1): [[(3 * core + j, (0,)) for j in range(3)] for core in range(2)]}
    for first, keys in ((6, near), (8, then)):
        for i, key in enumerate(keys):
            places[key] = [[(first + core, (i, j)) for j in range(3)] for core in range(2)]
    places = [places[(by, z)] for by in range(n_y) for z in range(2)]

    head_grads = head_grads.reshape(n_x, rows, 3 * HS)
    grads = lax.all_to_all(head_grads, "x", 0, 0, tiled=True)
    part = outer(ids, blocks, spots, head_grads, swap(head_grads), (shards[7], shards[9]))

    up, down, stat = norm_halves(
        ids, grads, proj, shards, places,
        ((2, 0), (1, 1), (2, 1), (3, 0)),
        ((0, 0), (0, half), (1, 0), (1, half)),
        (2 * half + 16, 2 * half),
        width,
    )
    up, down = shift(up, "zh", 1), shift(down, "zh", -1)
    up_part, down_part, own0, own1, _ = norm_halves(
        ids, grads, proj, shards, places,
        ((1, 0), (3, 1), (0, 0), (0, 1)),
        ((0, 0), (1, 0), (2, 0), (3, 0)),
        (half,) * 4,
        width,
        (stat,),
    )
    part = lax.all_to_all(part, "y", 0, 0, tiled=True).reshape(n_y, 2, w_rows, 3 * HS)
    keep, give = split(ids, part, (own0,))
    came = shift(give, "zl", 1)
    up_2, down_2 = add_messages(up_part, up, down_part, down, stat, (came,))
    last = merge(keep, came, att.reshape(n_x, rows, HS))
    up_2, down_2 = shift(up_2, "zh", 1), shift(down_2, "zh", -1)
    last = lax.all_to_all(last, "x", 0, 0, tiled=True)
    token_grad = finish(ids, (own0, own1, up_2, up, down, down_2), tokens, root, stat)
    weight_grad, attended = unpack(last)
    return attended[None], token_grad[None], weight_grad.transpose(1, 0, 2)


def solution(mesh):
    fine = Mesh(mesh.devices.reshape(4, 2, 2, 4, 4), ("y", "zl", "core", "x", "zh"))
    dp = ("y", "zl", "core")
    return jax.shard_map(
        per_device,
        mesh=fine,
        in_specs=(P(dp, "x", None), P(dp, None, "zh"), P(dp, "x", "zh")),
        out_specs=(P(dp, "x", "zh"), P(dp, "x", "zh"), P(dp, None, "zh")),
        check_vma=False,
    )
```

```python
import functools
import math

import jax
import jax.numpy as jnp
from jax import lax
from jax.experimental import pallas as pl
from jax.experimental.pallas import tpu as pltpu
from jax.sharding import Mesh
from jax.sharding import PartitionSpec as P

HS = 128
CORE, X, T, Y, Z = range(5)
BF = jnp.bfloat16
BUSY = 2 * 10**10
F32 = jnp.float32
PARAMS = pltpu.CompilerParams(vmem_limit_bytes=60 * 1024 * 1024)
SMALL = pltpu.CompilerParams(vmem_limit_bytes=24 * 1024 * 1024)


def dot(a, b, ca, cb):
    return lax.dot_general(a, b, (((ca,), (cb,)), ((), ())), preferred_element_type=F32)


def cost(flops, nbytes, exps=0):
    return pl.CostEstimate(flops=flops, bytes_accessed=nbytes, transcendentals=exps)


def shape(*dims, dtype=BF):
    return jax.ShapeDtypeStruct(dims, dtype)


def unit_kernel(at_ref, tok_ref, root_ref, *refs, band):
    tok = tok_ref[...].astype(F32)
    root = jnp.sqrt(jnp.mean(tok * tok, -1, keepdims=True) + 1e-05)
    root_ref[...] = root
    core = at_ref[CORE]
    mine_ref, mine_t_ref = refs[:2]
    for i in range(mine_ref.shape[1] // band):
        span = slice(i * band, (i + 1) * band)
        for ref, which in zip((mine_ref, *refs[2:]), (core, 1 - core)):
            at = pl.multiple_of((2 * i + which) * band, band)
            unit = (tok_ref[:, pl.ds(at, band)].astype(F32) / root).astype(BF)
            ref[:, span] = unit
            if ref is mine_ref:
                mine_t_ref[0, span, :] = unit.T


def unit_rows(ids, tokens, band, both):
    rows, width = tokens.shape
    tile = 128
    half = width // 2
    row = pl.BlockSpec((tile, half), lambda i, at: (i, 0))
    return pl.pallas_call(
        functools.partial(unit_kernel, band=band),
        grid_spec=pltpu.PrefetchScalarGridSpec(
            num_scalar_prefetch=1,
            grid=(rows // tile,),
            in_specs=[pl.BlockSpec((tile, width), lambda i, at: (i, 0))],
            out_specs=(pl.BlockSpec((tile, 1), lambda i, at: (i, 0)), row)
            + (pl.BlockSpec((1, half, tile), lambda i, at: (0, 0, i)),)
            + (row,) * both,
        ),
        out_shape=(shape(rows, 1, dtype=F32), shape(rows, half), shape(1, half, rows))
        + (shape(rows, half),) * both,
        compiler_params=PARAMS,
        cost_estimate=cost(BUSY, 1),
    )(ids, tokens)


def project_kernel(offsets, n_sums, at_ref, mine_ref, theirs_ref, *refs):
    keep_ref, give_ref, stack_ref, sems = refs[-4:]
    n = len(offsets)
    shards, sums = refs[:n], refs[n : n + n_sums]
    copies = [pltpu.make_async_copy(w, stack_ref.at[i], sems.at[i]) for i, w in enumerate(shards)]
    for copy in copies:
        copy.start()
    kinds, depth, cols = shards[0].shape
    bands = [
        pl.ds(pl.multiple_of(place_of(at_ref, *offset) * depth, depth), depth) for offset in offsets
    ]
    for i, (rows, out) in enumerate(((mine_ref, keep_ref), (theirs_ref, give_ref))):
        for j in range(kinds):
            span = slice(j * cols, (j + 1) * cols)
            total = sums[i][:, span] if n_sums else None
            for band, shard in zip(bands, shards):
                part = jnp.dot(rows[:, band], shard[j], preferred_element_type=F32)
                total = part if total is None else total + part
            out[:, span] = total.astype(out.dtype)
    for copy in copies:
        copy.wait()


def place_of(at_ref, y, z):
    return lax.rem(at_ref[Y] + y, 4) * 2 + lax.rem(at_ref[Z] + z, 2)


def project(ids, mine, theirs, shards, offsets, sums=(), give=F32, after=()):
    rows, _ = mine.shape
    n = len(shards)
    vmem = pl.BlockSpec(memory_space=pltpu.VMEM)
    cols = 3 * shards[0].shape[-1]
    return pl.pallas_call(
        functools.partial(project_kernel, offsets, len(sums)),
        in_specs=[pl.BlockSpec(memory_space=pltpu.SMEM)]
        + [vmem] * (2 + n + len(sums))
        + [pl.BlockSpec(memory_space=pl.ANY)] * len(after),
        out_specs=(vmem, vmem, pl.BlockSpec(memory_space=pl.ANY)),
        out_shape=(
            shape(rows, cols, dtype=F32),
            shape(rows, cols, dtype=give),
            shape(n, *shards[0].shape),
        ),
        scratch_shapes=[pltpu.SemaphoreType.DMA((n,))],
        compiler_params=PARAMS,
        cost_estimate=cost(1, 1),
    )(ids, mine, theirs, *shards, *sums, *after)


def project_last_kernel(offset, carried, at_ref, mine_ref, given_ref, keep_ref, came_ref, cot_ref, *refs):
    shards, heads_ref = refs[:6], refs[-1 - carried]
    depth, cols = shards[0].shape[-2:]
    band = pl.ds(pl.multiple_of(place_of(at_ref, *offset) * depth, depth), depth)
    heads = range(heads_ref.shape[0])
    for j in range(3):
        span = slice(j * cols, (j + 1) * cols)
        total = keep_ref[:, span] + came_ref[:, span].astype(F32)
        total += jnp.dot(mine_ref[:, band], shards[j][0], preferred_element_type=F32)
        total += jnp.dot(given_ref[:, band], shards[3 + j][0], preferred_element_type=F32)
        for h in heads:
            heads_ref[h, :, j * HS : (j + 1) * HS] = total[:, h * HS : (h + 1) * HS].astype(BF)
    for h in heads:
        heads_ref[h, :, 3 * HS :] = cot_ref[:, h * HS : (h + 1) * HS]


def project_last(ids, mine, given, keep, came, cotangent, pieces, offset, heads, carry, after):
    rows, cols = keep.shape
    n = len(carry)
    vmem = pl.BlockSpec(memory_space=pltpu.VMEM)
    free = pl.BlockSpec(memory_space=pl.ANY)
    return pl.pallas_call(
        functools.partial(project_last_kernel, offset, n),
        in_specs=[pl.BlockSpec(memory_space=pltpu.SMEM)]
        + [vmem] * (5 + len(pieces))
        + [free] * (n + len(after)),
        out_specs=(vmem,) + (free,) * n,
        out_shape=(shape(heads, rows, cols // heads + HS),) + tuple(shape(*c.shape) for c in carry),
        input_output_aliases={6 + len(pieces) + i: 1 + i for i in range(n)},
        compiler_params=PARAMS,
        cost_estimate=cost(1, 1),
    )(ids, mine, given, keep, came, cotangent, *pieces, *carry, *after)


def attention_kernel(q_rows, qkv_ref, *refs):
    att_ref, grad_ref, dk_ref, dv_ref = refs[-4:]
    scale = 1.0 / math.sqrt(HS)
    key = qkv_ref[:, HS : 2 * HS]
    value = qkv_ref[:, 2 * HS : 3 * HS]
    key_t = key.T
    value_t = value.T
    for i in range(qkv_ref.shape[0] // q_rows):
        rows = pl.ds(i * q_rows, q_rows)
        query = qkv_ref[rows, 0:HS]
        dout = qkv_ref[rows, 3 * HS :]
        scores = dot(key, query, 1, 1)
        to_log2 = scale * math.log2(math.e)
        top = jnp.max(scores, axis=0, keepdims=True) * to_log2
        expo = jnp.exp2(scores * to_log2 - top)
        prob = expo * (1.0 / jnp.sum(expo, axis=0, keepdims=True))
        prob_bf = prob.astype(BF)
        att = dot(value_t, prob_bf, 1, 0).T.astype(BF)
        att_ref[rows, :] = att
        row_dot = jnp.sum((dout.astype(F32) * att.astype(F32)).T, axis=0, keepdims=True)
        dprob = dot(value, dout, 1, 1)
        dscore = (prob * (dprob - row_dot)).astype(BF)
        grad_ref[rows, 0:HS] = (dot(key_t, dscore, 1, 0) * scale).T.astype(BF)
        dv = dot(prob_bf, dout, 1, 0)
        dk = dot(dscore, query, 1, 0)
        if i == 0:
            dv_ref[...] = dv
            dk_ref[...] = dk
        else:
            dv_ref[...] += dv
            dk_ref[...] += dk
    grad_ref[:, HS : 2 * HS] = (dk_ref[...] * scale).astype(BF)
    grad_ref[:, 2 * HS : 3 * HS] = dv_ref[...].astype(BF)


def attention(qkv, after):
    n = qkv.shape[0]
    vmem = pl.BlockSpec(memory_space=pltpu.VMEM)
    return pl.pallas_call(
        functools.partial(attention_kernel, n),
        out_shape=(shape(n, HS), shape(n, 3 * HS)),
        in_specs=[vmem] + [pl.BlockSpec(memory_space=pl.ANY)] * len(after),
        out_specs=(vmem,) * 2,
        scratch_shapes=[pltpu.VMEM((n, HS), F32), pltpu.VMEM((n, HS), F32)],
        compiler_params=PARAMS,
        cost_estimate=cost(BUSY, 1),
    )(qkv, *after)


def write_stat(ref, at, stat):
    ref[at:, :] = jnp.zeros((ref.shape[0] - at, ref.shape[1]), BF)
    rest = stat
    for i in range(3):
        top = rest.astype(BF)
        ref[at + i : at + i + 1, :] = top
        rest = rest - top.astype(F32)


def read_stat(ref, at):
    return sum(ref[at + i : at + i + 1, :].astype(F32) for i in range(3))


def norm_kernel(width, halves, spots, places, n_in, at_ref, g_ref, p_ref, *refs):
    shards = refs[:n_in]
    n_out = max(spot[0] for spot in spots) + 1
    outs, stat_ref = refs[-4 - n_out : -4], refs[-4]
    w_ref, flat_ref, sems = refs[-3:]
    _, kinds, depth, cols = w_ref.shape
    band = depth // 2
    quarters = len(places) // 2

    def copy(step, core, j, source):
        to = lax.rem(at_ref[CORE] + core, 2)
        at = pl.ds(pl.multiple_of(to * band, band), band)
        return pltpu.make_async_copy(source, w_ref.at[step, j, at], sems.at[step, core, j])

    for step, (by, half) in enumerate(halves):
        y_off = lax.rem(at_ref[T] + (by + quarters) - at_ref[Y], quarters)
        where = y_off * 2 + lax.rem(at_ref[Z] + half, 2)
        for place, cores in enumerate(places):

            @pl.when(where == place)
            def _(step=step, cores=cores):
                for core, pieces in enumerate(cores):
                    for j, (which, at) in enumerate(pieces):
                        copy(step, core, j, shards[which].at[*at]).start()

    heads, _, _ = g_ref.shape
    for h in range(heads):
        for j in range(kinds):
            at = (j * heads + h) * HS
            flat_ref[at : at + HS, :] = g_ref[h, :, j * HS : (j + 1) * HS].T
    total = sum(
        g_ref[h, :, j * HS : (j + 1) * HS].astype(F32)
        * p_ref[h, :, j * HS : (j + 1) * HS].astype(F32)
        for h in range(heads)
        for j in range(kinds)
    )
    stat = jnp.sum(total.T, axis=0, keepdims=True) * (1.0 / width)
    stat_ref[...] = stat
    for ref in outs:
        if ref.shape[0] % 128:
            write_stat(ref, ref.shape[0] - 16, stat)

    for step, (which, at) in enumerate(spots):
        for core in range(2):
            for j in range(kinds):
                copy(step, core, j, shards[0].at[0]).wait()
        total = sum(
            dot(w_ref[step, j], flat_ref[j * cols : (j + 1) * cols, :], 1, 0)
            for j in range(kinds)
        )
        outs[which][at : at + depth, :] = total.astype(BF)


def norm_halves(ids, grads, proj, shards, places, halves, spots, sizes, width, after=()):
    heads, rows, _ = grads.shape
    kinds = 3
    band, cols = shards[0].shape[-2:]
    n = len(spots)
    sizes = (*sizes, 1)
    vmem = pl.BlockSpec(memory_space=pltpu.VMEM)
    free = pl.BlockSpec(memory_space=pl.ANY)
    return pl.pallas_call(
        functools.partial(norm_kernel, width, halves, spots, places, len(shards)),
        in_specs=[pl.BlockSpec(memory_space=pltpu.SMEM), vmem, vmem]
        + [free] * (len(shards) + len(after)),
        out_specs=(vmem,) * len(sizes),
        out_shape=tuple(shape(s, rows) for s in sizes[:-1]) + (shape(1, rows, dtype=F32),),
        scratch_shapes=[
            pltpu.VMEM((n, kinds, 2 * band, cols), BF),
            pltpu.VMEM((kinds * cols, rows), BF),
            pltpu.SemaphoreType.DMA((n, 2, kinds)),
        ],
        compiler_params=PARAMS,
        cost_estimate=cost(1, 1),
    )(ids, grads, proj, *shards, *after)


def add_kernel(up_part, up_in, stat_in, up_direct, down_part, down_in, down_direct, stat_ref, *refs):
    up_out, down_out = refs[-2:]
    half = up_part.shape[0]
    for part, came, direct, out in (
        (up_part, up_in, up_direct, up_out),
        (down_part, down_in, down_direct, down_out),
    ):
        out[:half, :] = (part[...].astype(F32) + came[...].astype(F32)).astype(BF)
        out[half : 2 * half, :] = direct[...]
    write_stat(up_out, 2 * half, stat_ref[...] + read_stat(stat_in, 0))
    write_stat(down_out, 2 * half, stat_ref[...])


def add_messages(up_part, up_in, up_direct, down_part, down_in, down_direct, stat, after):
    half, rows = up_part.shape
    block = pl.BlockSpec((half, rows), lambda i: (0, 0))
    out = pl.BlockSpec((2 * half + 16, rows), lambda i: (0, 0))
    end = pl.BlockSpec((16, rows), lambda i: (half // 16, 0))
    return pl.pallas_call(
        add_kernel,
        grid=(1,),
        out_shape=(shape(2 * half + 16, rows),) * 2,
        in_specs=[block, block, end]
        + [block] * 4
        + [pl.BlockSpec((1, rows), lambda i: (0, 0)), pl.BlockSpec(memory_space=pl.ANY)],
        out_specs=(out, out),
        compiler_params=PARAMS,
        cost_estimate=cost(1, 1),
    )(up_part, up_in, up_in, up_direct, down_part, down_in, down_direct, stat, after)


def finish_kernel(at_ref, own0, own1, up, down, tok_ref, root_ref, stat_ref, *refs):
    out_ref = refs[-1]
    half = own0.shape[0]
    stat = stat_ref[...] + read_stat(up, 2 * half) + read_stat(down, 2 * half)
    stat = jnp.broadcast_to(stat, (HS, stat.shape[1])).T[:, 0:1]
    root = root_ref[...]
    parts = (
        (own0[...], up[:half, :], down[half : 2 * half, :]),
        (own1[...], up[half : 2 * half, :], down[:half, :]),
    )
    for i, part in enumerate(parts):
        span = slice(i * half, (i + 1) * half)
        total = sum(p.astype(F32) for p in part)
        unit = tok_ref[:, span].astype(F32) / root
        out_ref[:, span] = ((total.T - unit * stat) / root).astype(BF)


def finish(ids, parts, tokens, root, stat, after=()):
    half, rows = parts[0].shape
    share = 2 * half
    tile = HS
    some = lambda a: pl.BlockSpec((a.shape[0], tile), lambda i, at: (0, i))
    return pl.pallas_call(
        finish_kernel,
        grid_spec=pltpu.PrefetchScalarGridSpec(
            num_scalar_prefetch=1,
            grid=(rows // tile,),
            in_specs=[some(p) for p in parts]
            + [pl.BlockSpec((tile, share), lambda i, at: (i, at[T]))]
            + [pl.BlockSpec((tile, 1), lambda i, at: (i, 0)), some(stat)]
            + [pl.BlockSpec(memory_space=pl.ANY)] * len(after),
            out_specs=pl.BlockSpec((tile, share), lambda i, at: (i, 0)),
        ),
        out_shape=shape(rows, share),
        compiler_params=PARAMS,
        cost_estimate=cost(BUSY, 1),
    )(ids, *parts, tokens, root, stat, *after)


def outer_kernel(tile, spots, at_ref, *refs):
    out_ref, a_ref, g_ref, sems = refs[-4:]
    m = max(spot[0] for spot in spots) + 1
    arrays, (mine_ref, other_ref) = refs[:m], refs[m : m + 2]
    n, rows, _ = mine_ref.shape
    depth = a_ref.shape[0]
    copies = []
    for step in range(depth // tile):
        span = pl.ds(step * tile, tile)
        some = []
        for i, (which, at, _, _) in enumerate(spots):
            to = a_ref.at[span, pl.ds(i * rows, rows)]
            some.append(pltpu.make_async_copy(arrays[which].at[at, span], to, sems.at[step, i]))
            some[-1].start()
        copies.append(some)
    for i, (_, _, by, frame) in enumerate(spots):
        ref = other_ref if frame else mine_ref
        g_ref[i * rows : (i + 1) * rows, :] = ref[lax.rem(at_ref[X] + by, n)]
    for step, some in enumerate(copies):
        for copy in some:
            copy.wait()
        span = slice(step * tile, (step + 1) * tile)
        out_ref[span, :] = jnp.dot(
            a_ref[span, :], g_ref[...], preferred_element_type=F32
        ).astype(BF)


def outer(ids, arrays, spots, mine, other, after):
    _, depth, rows = arrays[0].shape
    cols = mine.shape[2]
    n = len(spots)
    tile = 512
    vmem = pl.BlockSpec(memory_space=pltpu.VMEM)
    return pl.pallas_call(
        functools.partial(outer_kernel, tile, spots),
        in_specs=[pl.BlockSpec(memory_space=pltpu.SMEM)]
        + [pl.BlockSpec(memory_space=pl.ANY)] * len(arrays)
        + [vmem, vmem]
        + [pl.BlockSpec(memory_space=pl.ANY)] * len(after),
        out_specs=vmem,
        out_shape=shape(depth, cols),
        scratch_shapes=[
            pltpu.VMEM((depth, n * rows), BF),
            pltpu.VMEM((n * rows, cols), BF),
            pltpu.SemaphoreType.DMA((depth // tile, n)),
        ],
        compiler_params=PARAMS,
        cost_estimate=cost(1, 1),
    )(ids, *arrays, mine, other, *after)


def split_kernel(at_ref, part_ref, *refs):
    keep_ref, give_ref = refs[-2:]
    n, _, rows, _ = part_ref.shape
    for ref, which in ((keep_ref, at_ref[Z]), (give_ref, 1 - at_ref[Z])):
        ref[...] = sum(part_ref[i, which].astype(F32) for i in range(n)).astype(ref.dtype)


def split(ids, part, after=()):
    _, _, rows, cols = part.shape
    vmem = pl.BlockSpec(memory_space=pltpu.VMEM)
    return pl.pallas_call(
        split_kernel,
        in_specs=[pl.BlockSpec(memory_space=pltpu.SMEM), vmem]
        + [pl.BlockSpec(memory_space=pl.ANY)] * len(after),
        out_specs=(vmem, vmem),
        out_shape=(shape(rows, cols, dtype=F32), shape(rows, cols)),
        compiler_params=PARAMS,
        cost_estimate=cost(1, 1),
    )(ids, part, *after)


def merge_kernel(keep_ref, came_ref, att_ref, *refs):
    out_ref = refs[-1]
    total = (keep_ref[...] + came_ref[...].astype(F32)).astype(BF)
    cols = total.shape[1]
    for i in range(out_ref.shape[0]):
        out_ref[i, :, :cols] = total
        out_ref[i, :, cols:] = att_ref[i]


def merge(keep, came, att, after=()):
    rows, cols = keep.shape
    n, _, more = att.shape
    vmem = pl.BlockSpec(memory_space=pltpu.VMEM)
    return pl.pallas_call(
        merge_kernel,
        out_shape=shape(n, rows, cols + more),
        in_specs=[vmem] * 3 + [pl.BlockSpec(memory_space=pl.ANY)] * len(after),
        out_specs=vmem,
        compiler_params=PARAMS,
        cost_estimate=cost(1, 1),
    )(keep, came, att, *after)


def unpack_kernel(in_ref, w_ref, att_ref):
    for h in range(in_ref.shape[0]):
        span = slice(h * HS, (h + 1) * HS)
        for j in range(3):
            w_ref[j, :, span] = in_ref[h, :, j * HS : (j + 1) * HS].astype(F32)
        att_ref[:, span] = in_ref[h, :, 3 * HS :]


def unpack(last):
    heads, rows, more = last.shape
    tile = rows // 4
    return pl.pallas_call(
        unpack_kernel,
        grid=(rows // tile,),
        in_specs=[pl.BlockSpec((heads, tile, more), lambda i: (0, i, 0))],
        out_specs=(
            pl.BlockSpec((3, tile, heads * HS), lambda i: (0, i, 0)),
            pl.BlockSpec((tile, heads * HS), lambda i: (i, 0)),
        ),
        out_shape=(shape(3, rows, heads * HS, dtype=F32), shape(rows, heads * HS)),
        compiler_params=SMALL,
        cost_estimate=cost(1, 1),
    )(last)


def gate(arrays, after=(), pieces=()):
    n, m = len(arrays), len(arrays) + len(after)
    free = pl.BlockSpec(memory_space=pl.ANY)

    def kernel(*refs):
        outs, sems = refs[m + n : -1], refs[-1]
        copies = [
            pltpu.make_async_copy(refs[which].at[pl.ds(at, 1)], out, sems.at[i])
            for i, ((which, at), out) in enumerate(zip(pieces, outs))
        ]
        for copy in copies:
            copy.start()
        for copy in copies:
            copy.wait()

    return pl.pallas_call(
        kernel,
        in_specs=[free] * m,
        out_specs=(free,) * n + (pl.BlockSpec(memory_space=pltpu.VMEM),) * len(pieces),
        out_shape=tuple(shape(*a.shape) for a in arrays)
        + tuple(shape(1, *arrays[which].shape[1:]) for which, _ in pieces),
        scratch_shapes=[pltpu.SemaphoreType.DMA((max(len(pieces), 1),))],
        input_output_aliases={i: i for i in range(n)},
        compiler_params=PARAMS,
        cost_estimate=cost(1, 1),
    )(*arrays, *after)


def shift(x, axis, by):
    n = lax.axis_size(axis)
    return lax.ppermute(x, axis, [(i, (i + by) % n) for i in range(n)])


def per_device(tokens, weights, cotangent):
    _, rows, width = tokens.shape
    w_rows, _, cols = weights.shape
    heads = cols // HS
    n_x, n_y = (lax.axis_size(a) for a in ("x", "y"))
    ids = jnp.stack([lax.axis_index(a) for a in ("core", "x", "zh", "y", "zl")])
    tokens = tokens.reshape(rows, width)
    half = width // lax.axis_size("zh") // 2

    swap = lambda a: shift(a, "core", 1)
    own = weights.transpose(1, 0, 2)
    left, right, other = shift(own, "y", 1), shift(own, "y", -1), shift(own, "zl", 1)
    root, mine, mine_t, given = unit_rows(ids, tokens, w_rows, True)
    _, theirs, theirs_t = unit_rows(ids, swap(tokens), w_rows, False)
    left, right, other = gate((left, right, other), (theirs,))

    left_0, right_0 = shift(mine_t, "x", 1), shift(mine_t, "x", -1)
    left_1, right_1 = shift(theirs_t, "x", 1), shift(theirs_t, "x", -1)

    near = ((0, 0), (3, 0), (1, 0), (0, 1))
    *sums, stack_0 = project(ids, mine, theirs, (own, left, right, other), near, after=(left_0, right_0))
    far, other_left, other_right, *pieces = gate(
        (shift(left, "y", 1), shift(left, "zl", 1), shift(other, "y", -1)),
        sums,
        ((0, 0), (1, 1), (2, 2)),
    )
    then = ((2, 0), (3, 1), (1, 1))
    keep, give, stack_1 = project(
        ids, mine, theirs, (far, other_left, other_right), then, sums, BF
    )
    *pieces, give = gate(
        (shift(pieces[0], "zl", 1), shift(pieces[1], "y", 1), shift(pieces[2], "y", -1), give)
    )
    pieces = (*pieces, *(swap(p) for p in pieces))
    proj, stack_0, stack_1 = project_last(
        ids, mine, given, keep, swap(give), cotangent.reshape(rows, cols), pieces, (2, 1), heads,
        (stack_0, stack_1), (left_1, right_1),
    )

    far_0, far_1 = shift(left_0, "x", 1), shift(right_1, "x", -1)
    blocks = (mine_t, theirs_t, left_0, left_1, right_0, right_1, far_0, far_1)
    spots = tuple((i, 0, by, i % 2) for i, by in enumerate((0, 0, 3, 3, 1, 1, 2, 2)))
    qkv = lax.all_to_all(proj, "x", 0, 0, tiled=True).reshape(n_x * rows, 4 * HS)
    att, head_grads = attention(qkv, (far_0, far_1))

    shards = (*pieces, stack_0, swap(stack_0), stack_1, swap(stack_1))
    places = {(2, 1): [[(3 * core + j, (0,)) for j in range(3)] for core in range(2)]}
    for first, keys in ((6, near), (8, then)):
        for i, key in enumerate(keys):
            places[key] = [[(first + core, (i, j)) for j in range(3)] for core in range(2)]
    places = [places[(by, z)] for by in range(n_y) for z in range(2)]

    head_grads = head_grads.reshape(n_x, rows, 3 * HS)
    grads = lax.all_to_all(head_grads, "x", 0, 0, tiled=True)
    part = outer(ids, blocks, spots, head_grads, swap(head_grads), (shards[7], shards[9]))

    up, down, stat = norm_halves(
        ids, grads, proj, shards, places,
        ((2, 0), (2, 1)),
        ((0, 0), (1, 0)),
        (half + 16, half),
        width,
    )
    up, down = shift(up, "zh", 1), shift(down, "zh", -1)
    up_part, down_part, up_direct, down_direct, own0, own1, _ = norm_halves(
        ids, grads, proj, shards, places,
        ((1, 0), (3, 1), (1, 1), (3, 0), (0, 0), (0, 1)),
        tuple((i, 0) for i in range(6)),
        (half,) * 6,
        width,
        (stat,),
    )
    part = lax.all_to_all(part, "y", 0, 0, tiled=True).reshape(n_y, 2, w_rows, 3 * HS)
    keep, give = split(ids, part, (own0,))
    came = shift(give, "zl", 1)
    up_2, down_2 = add_messages(up_part, up, up_direct, down_part, down, down_direct, stat, came)
    last = merge(keep, came, att.reshape(n_x, rows, HS))
    up_2, down_2 = shift(up_2, "zh", 1), shift(down_2, "zh", -1)
    last = lax.all_to_all(last, "x", 0, 0, tiled=True)
    token_grad = finish(ids, (own0, own1, up_2, down_2), tokens, root, stat)
    weight_grad, attended = unpack(last)
    return attended[None], token_grad[None], weight_grad.transpose(1, 0, 2)


def solution(mesh):
    fine = Mesh(mesh.devices.reshape(4, 2, 2, 4, 4), ("y", "zl", "core", "x", "zh"))
    dp = ("y", "zl", "core")
    return jax.shard_map(
        per_device,
        mesh=fine,
        in_specs=(P(dp, "x", None), P(dp, None, "zh"), P(dp, "x", "zh")),
        out_specs=(P(dp, "x", "zh"), P(dp, "x", "zh"), P(dp, None, "zh")),
        check_vma=False,
    )
```

```python
import functools
import math

import jax
import jax.numpy as jnp
from jax import lax
from jax.experimental import pallas as pl
from jax.experimental.pallas import tpu as pltpu
from jax.sharding import Mesh
from jax.sharding import PartitionSpec as P

HS = 128
CORE, X, T, Y, Z = range(5)
BF = jnp.bfloat16
BUSY = 2 * 10**10
F32 = jnp.float32
PARAMS = pltpu.CompilerParams(vmem_limit_bytes=60 * 1024 * 1024)
SMALL = pltpu.CompilerParams(vmem_limit_bytes=24 * 1024 * 1024)


def dot(a, b, ca, cb):
    return lax.dot_general(a, b, (((ca,), (cb,)), ((), ())), preferred_element_type=F32)


def cost(flops, nbytes, exps=0):
    return pl.CostEstimate(flops=flops, bytes_accessed=nbytes, transcendentals=exps)


def shape(*dims, dtype=BF):
    return jax.ShapeDtypeStruct(dims, dtype)


def unit_kernel(at_ref, tok_ref, *refs, band, kinds):
    tok = tok_ref[...].astype(F32)
    root = jnp.sqrt(jnp.mean(tok * tok, -1, keepdims=True) + 1e-05)
    core = at_ref[CORE]
    outs = dict(zip(kinds, refs))
    if "root" in outs:
        outs["root"][...] = root
    for i in range(tok.shape[1] // (2 * band)):
        span = slice(i * band, (i + 1) * band)
        for names, which in ((("mine", "turned"), core), (("given",), 1 - core)):
            if not any(name in outs for name in names):
                continue
            at = pl.multiple_of((2 * i + which) * band, band)
            unit = (tok_ref[:, pl.ds(at, band)].astype(F32) / root).astype(BF)
            for name in names:
                if name == "turned" and name in outs:
                    outs[name][0, span, :] = unit.T
                elif name in outs:
                    outs[name][:, span] = unit


def unit_rows(ids, tokens, band, kinds, after=()):
    rows, width = tokens.shape
    tile = 128
    half = width // 2
    row = (pl.BlockSpec((tile, half), lambda i, at: (i, 0)), shape(rows, half))
    forms = {
        "root": (pl.BlockSpec((tile, 1), lambda i, at: (i, 0)), shape(rows, 1, dtype=F32)),
        "mine": row,
        "given": row,
        "turned": (
            pl.BlockSpec((1, half, tile), lambda i, at: (0, 0, i)),
            shape(1, half, rows),
        ),
    }

    def kernel(at_ref, tok_ref, *refs):
        unit_kernel(at_ref, tok_ref, *refs[len(after) :], band=band, kinds=kinds)

    return pl.pallas_call(
        kernel,
        grid_spec=pltpu.PrefetchScalarGridSpec(
            num_scalar_prefetch=1,
            grid=(rows // tile,),
            in_specs=[pl.BlockSpec((tile, width), lambda i, at: (i, 0))]
            + [pl.BlockSpec(memory_space=pl.ANY)] * len(after),
            out_specs=tuple(forms[kind][0] for kind in kinds),
        ),
        out_shape=tuple(forms[kind][1] for kind in kinds),
        compiler_params=PARAMS,
        cost_estimate=cost(BUSY, 1),
    )(ids, tokens, *after)


def project_kernel(offsets, n_sums, at_ref, mine_ref, theirs_ref, *refs):
    keep_ref, give_ref, stack_ref, sems = refs[-4:]
    n = len(offsets)
    shards, sums = refs[:n], refs[n : n + n_sums]
    copies = [pltpu.make_async_copy(w, stack_ref.at[i], sems.at[i]) for i, w in enumerate(shards)]
    for copy in copies:
        copy.start()
    kinds, depth, cols = shards[0].shape
    bands = [
        pl.ds(pl.multiple_of(place_of(at_ref, *offset) * depth, depth), depth) for offset in offsets
    ]
    for i, (rows, out) in enumerate(((mine_ref, keep_ref), (theirs_ref, give_ref))):
        for j in range(kinds):
            span = slice(j * cols, (j + 1) * cols)
            total = sums[i][:, span] if n_sums else None
            for band, shard in zip(bands, shards):
                part = jnp.dot(rows[:, band], shard[j], preferred_element_type=F32)
                total = part if total is None else total + part
            out[:, span] = total.astype(out.dtype)
    for copy in copies:
        copy.wait()


def place_of(at_ref, y, z):
    return lax.rem(at_ref[Y] + y, 4) * 2 + lax.rem(at_ref[Z] + z, 2)


def project(ids, mine, theirs, shards, offsets, sums=(), give=F32, after=()):
    rows, _ = mine.shape
    n = len(shards)
    vmem = pl.BlockSpec(memory_space=pltpu.VMEM)
    cols = 3 * shards[0].shape[-1]
    return pl.pallas_call(
        functools.partial(project_kernel, offsets, len(sums)),
        in_specs=[pl.BlockSpec(memory_space=pltpu.SMEM)]
        + [vmem] * (2 + n + len(sums))
        + [pl.BlockSpec(memory_space=pl.ANY)] * len(after),
        out_specs=(vmem, vmem, pl.BlockSpec(memory_space=pl.ANY)),
        out_shape=(
            shape(rows, cols, dtype=F32),
            shape(rows, cols, dtype=give),
            shape(n, *shards[0].shape),
        ),
        scratch_shapes=[pltpu.SemaphoreType.DMA((n,))],
        compiler_params=PARAMS,
        cost_estimate=cost(1, 1),
    )(ids, mine, theirs, *shards, *sums, *after)


def project_last_kernel(offset, carried, at_ref, mine_ref, given_ref, keep_ref, came_ref, cot_ref, *refs):
    shards, heads_ref = refs[:6], refs[-1 - carried]
    depth, cols = shards[0].shape[-2:]
    band = pl.ds(pl.multiple_of(place_of(at_ref, *offset) * depth, depth), depth)
    heads = range(heads_ref.shape[0])
    for j in range(3):
        span = slice(j * cols, (j + 1) * cols)
        total = keep_ref[:, span] + came_ref[:, span].astype(F32)
        total += jnp.dot(mine_ref[:, band], shards[j][0], preferred_element_type=F32)
        total += jnp.dot(given_ref[:, band], shards[3 + j][0], preferred_element_type=F32)
        for h in heads:
            heads_ref[h, :, j * HS : (j + 1) * HS] = total[:, h * HS : (h + 1) * HS].astype(BF)
    for h in heads:
        heads_ref[h, :, 3 * HS :] = cot_ref[:, h * HS : (h + 1) * HS]


def project_last(ids, mine, given, keep, came, cotangent, pieces, offset, heads, carry, after):
    rows, cols = keep.shape
    n = len(carry)
    vmem = pl.BlockSpec(memory_space=pltpu.VMEM)
    free = pl.BlockSpec(memory_space=pl.ANY)
    return pl.pallas_call(
        functools.partial(project_last_kernel, offset, n),
        in_specs=[pl.BlockSpec(memory_space=pltpu.SMEM)]
        + [vmem] * (5 + len(pieces))
        + [free] * (n + len(after)),
        out_specs=(vmem,) + (free,) * n,
        out_shape=(shape(heads, rows, cols // heads + HS),) + tuple(shape(*c.shape) for c in carry),
        input_output_aliases={6 + len(pieces) + i: 1 + i for i in range(n)},
        compiler_params=PARAMS,
        cost_estimate=cost(1, 1),
    )(ids, mine, given, keep, came, cotangent, *pieces, *carry, *after)


def attention_kernel(q_rows, qkv_ref, *refs):
    att_ref, grad_ref, dk_ref, dv_ref = refs[-4:]
    scale = 1.0 / math.sqrt(HS)
    key = qkv_ref[:, HS : 2 * HS]
    value = qkv_ref[:, 2 * HS : 3 * HS]
    key_t = key.T
    value_t = value.T
    for i in range(qkv_ref.shape[0] // q_rows):
        rows = pl.ds(i * q_rows, q_rows)
        query = qkv_ref[rows, 0:HS]
        dout = qkv_ref[rows, 3 * HS :]
        scores = dot(key, query, 1, 1)
        to_log2 = scale * math.log2(math.e)
        top = jnp.max(scores, axis=0, keepdims=True) * to_log2
        expo = jnp.exp2(scores * to_log2 - top)
        prob = expo * (1.0 / jnp.sum(expo, axis=0, keepdims=True))
        prob_bf = prob.astype(BF)
        att = dot(value_t, prob_bf, 1, 0).T.astype(BF)
        att_ref[rows, :] = att
        row_dot = jnp.sum((dout.astype(F32) * att.astype(F32)).T, axis=0, keepdims=True)
        dprob = dot(value, dout, 1, 1)
        dscore = (prob * (dprob - row_dot)).astype(BF)
        grad_ref[rows, 0:HS] = (dot(key_t, dscore, 1, 0) * scale).T.astype(BF)
        dv = dot(prob_bf, dout, 1, 0)
        dk = dot(dscore, query, 1, 0)
        if i == 0:
            dv_ref[...] = dv
            dk_ref[...] = dk
        else:
            dv_ref[...] += dv
            dk_ref[...] += dk
    grad_ref[:, HS : 2 * HS] = (dk_ref[...] * scale).astype(BF)
    grad_ref[:, 2 * HS : 3 * HS] = dv_ref[...].astype(BF)


def attention(qkv, after):
    n = qkv.shape[0]
    vmem = pl.BlockSpec(memory_space=pltpu.VMEM)
    return pl.pallas_call(
        functools.partial(attention_kernel, n),
        out_shape=(shape(n, HS), shape(n, 3 * HS)),
        in_specs=[vmem] + [pl.BlockSpec(memory_space=pl.ANY)] * len(after),
        out_specs=(vmem,) * 2,
        scratch_shapes=[pltpu.VMEM((n, HS), F32), pltpu.VMEM((n, HS), F32)],
        compiler_params=PARAMS,
        cost_estimate=cost(BUSY, 1),
    )(qkv, *after)


def write_stat(ref, at, stat):
    ref[at:, :] = jnp.zeros((ref.shape[0] - at, ref.shape[1]), BF)
    rest = stat
    for i in range(3):
        top = rest.astype(BF)
        ref[at + i : at + i + 1, :] = top
        rest = rest - top.astype(F32)


def read_stat(ref, at):
    return sum(ref[at + i : at + i + 1, :].astype(F32) for i in range(3))


def norm_kernel(width, halves, spots, places, n_in, at_ref, g_ref, p_ref, *refs):
    shards = refs[:n_in]
    n_out = max(spot[0] for spot in spots) + 1
    outs, stat_ref = refs[-4 - n_out : -4], refs[-4]
    w_ref, flat_ref, sems = refs[-3:]
    _, kinds, depth, cols = w_ref.shape
    band = depth // 2
    quarters = len(places) // 2

    def copy(step, core, j, source):
        to = lax.rem(at_ref[CORE] + core, 2)
        at = pl.ds(pl.multiple_of(to * band, band), band)
        return pltpu.make_async_copy(source, w_ref.at[step, j, at], sems.at[step, core, j])

    for step, (by, half) in enumerate(halves):
        y_off = lax.rem(at_ref[T] + (by + quarters) - at_ref[Y], quarters)
        where = y_off * 2 + lax.rem(at_ref[Z] + half, 2)
        for place, cores in enumerate(places):

            @pl.when(where == place)
            def _(step=step, cores=cores):
                for core, pieces in enumerate(cores):
                    for j, (which, at) in enumerate(pieces):
                        copy(step, core, j, shards[which].at[*at]).start()

    heads, _, _ = g_ref.shape
    for h in range(heads):
        for j in range(kinds):
            at = (j * heads + h) * HS
            flat_ref[at : at + HS, :] = g_ref[h, :, j * HS : (j + 1) * HS].T
    total = sum(
        g_ref[h, :, j * HS : (j + 1) * HS].astype(F32)
        * p_ref[h, :, j * HS : (j + 1) * HS].astype(F32)
        for h in range(heads)
        for j in range(kinds)
    )
    stat = jnp.sum(total.T, axis=0, keepdims=True) * (1.0 / width)
    stat_ref[...] = stat
    for ref in outs:
        if ref.shape[0] % 128:
            write_stat(ref, ref.shape[0] - 16, stat)

    for step, (which, at) in enumerate(spots):
        for core in range(2):
            for j in range(kinds):
                copy(step, core, j, shards[0].at[0]).wait()
        total = sum(
            dot(w_ref[step, j], flat_ref[j * cols : (j + 1) * cols, :], 1, 0)
            for j in range(kinds)
        )
        outs[which][at : at + depth, :] = total.astype(BF)


def norm_halves(ids, grads, proj, shards, places, halves, spots, sizes, width, after=()):
    heads, rows, _ = grads.shape
    kinds = 3
    band, cols = shards[0].shape[-2:]
    n = len(spots)
    sizes = (*sizes, 1)
    vmem = pl.BlockSpec(memory_space=pltpu.VMEM)
    free = pl.BlockSpec(memory_space=pl.ANY)
    return pl.pallas_call(
        functools.partial(norm_kernel, width, halves, spots, places, len(shards)),
        in_specs=[pl.BlockSpec(memory_space=pltpu.SMEM), vmem, vmem]
        + [free] * (len(shards) + len(after)),
        out_specs=(vmem,) * len(sizes),
        out_shape=tuple(shape(s, rows) for s in sizes[:-1]) + (shape(1, rows, dtype=F32),),
        scratch_shapes=[
            pltpu.VMEM((n, kinds, 2 * band, cols), BF),
            pltpu.VMEM((kinds * cols, rows), BF),
            pltpu.SemaphoreType.DMA((n, 2, kinds)),
        ],
        compiler_params=PARAMS,
        cost_estimate=cost(1, 1),
    )(ids, grads, proj, *shards, *after)


def add_kernel(up_part, up_in, stat_in, up_direct, down_part, down_in, down_direct, stat_ref, *refs):
    up_out, down_out = refs[-2:]
    half = up_part.shape[0]
    for part, came, direct, out in (
        (up_part, up_in, up_direct, up_out),
        (down_part, down_in, down_direct, down_out),
    ):
        out[:half, :] = (part[...].astype(F32) + came[...].astype(F32)).astype(BF)
        out[half : 2 * half, :] = direct[...]
    write_stat(up_out, 2 * half, stat_ref[...] + read_stat(stat_in, 0))
    write_stat(down_out, 2 * half, stat_ref[...])


def add_messages(up_part, up_in, up_direct, down_part, down_in, down_direct, stat, after):
    half, rows = up_part.shape
    block = pl.BlockSpec((half, rows), lambda i: (0, 0))
    out = pl.BlockSpec((2 * half + 16, rows), lambda i: (0, 0))
    end = pl.BlockSpec((16, rows), lambda i: (half // 16, 0))
    return pl.pallas_call(
        add_kernel,
        grid=(1,),
        out_shape=(shape(2 * half + 16, rows),) * 2,
        in_specs=[block, block, end]
        + [block] * 4
        + [pl.BlockSpec((1, rows), lambda i: (0, 0)), pl.BlockSpec(memory_space=pl.ANY)],
        out_specs=(out, out),
        compiler_params=PARAMS,
        cost_estimate=cost(1, 1),
    )(up_part, up_in, up_in, up_direct, down_part, down_in, down_direct, stat, after)


def finish_kernel(at_ref, own0, own1, up, down, tok_ref, root_ref, stat_ref, *refs):
    out_ref = refs[-1]
    half = own0.shape[0]
    stat = stat_ref[...] + read_stat(up, 2 * half) + read_stat(down, 2 * half)
    stat = jnp.broadcast_to(stat, (HS, stat.shape[1])).T[:, 0:1]
    root = root_ref[...]
    parts = (
        (own0[...], up[:half, :], down[half : 2 * half, :]),
        (own1[...], up[half : 2 * half, :], down[:half, :]),
    )
    for i, part in enumerate(parts):
        span = slice(i * half, (i + 1) * half)
        total = sum(p.astype(F32) for p in part)
        unit = tok_ref[:, span].astype(F32) / root
        out_ref[:, span] = ((total.T - unit * stat) / root).astype(BF)


def finish(ids, parts, tokens, root, stat, after=()):
    half, rows = parts[0].shape
    share = 2 * half
    tile = HS
    some = lambda a: pl.BlockSpec((a.shape[0], tile), lambda i, at: (0, i))
    return pl.pallas_call(
        finish_kernel,
        grid_spec=pltpu.PrefetchScalarGridSpec(
            num_scalar_prefetch=1,
            grid=(rows // tile,),
            in_specs=[some(p) for p in parts]
            + [pl.BlockSpec((tile, share), lambda i, at: (i, at[T]))]
            + [pl.BlockSpec((tile, 1), lambda i, at: (i, 0)), some(stat)]
            + [pl.BlockSpec(memory_space=pl.ANY)] * len(after),
            out_specs=pl.BlockSpec((tile, share), lambda i, at: (i, 0)),
        ),
        out_shape=shape(rows, share),
        compiler_params=PARAMS,
        cost_estimate=cost(BUSY, 1),
    )(ids, *parts, tokens, root, stat, *after)


def outer_kernel(tile, spots, at_ref, *refs):
    out_ref, a_ref, g_ref, sems = refs[-4:]
    m = max(spot[0] for spot in spots) + 1
    arrays, (mine_ref, other_ref) = refs[:m], refs[m : m + 2]
    n, rows, _ = mine_ref.shape
    depth = a_ref.shape[0]
    copies = []
    for step in range(depth // tile):
        span = pl.ds(step * tile, tile)
        some = []
        for i, (which, at, _, _) in enumerate(spots):
            to = a_ref.at[span, pl.ds(i * rows, rows)]
            some.append(pltpu.make_async_copy(arrays[which].at[at, span], to, sems.at[step, i]))
            some[-1].start()
        copies.append(some)
    for i, (_, _, by, frame) in enumerate(spots):
        ref = other_ref if frame else mine_ref
        g_ref[i * rows : (i + 1) * rows, :] = ref[lax.rem(at_ref[X] + by, n)]
    for step, some in enumerate(copies):
        for copy in some:
            copy.wait()
        span = slice(step * tile, (step + 1) * tile)
        out_ref[span, :] = jnp.dot(
            a_ref[span, :], g_ref[...], preferred_element_type=F32
        ).astype(BF)


def outer(ids, arrays, spots, mine, other, after):
    _, depth, rows = arrays[0].shape
    cols = mine.shape[2]
    n = len(spots)
    tile = 512
    vmem = pl.BlockSpec(memory_space=pltpu.VMEM)
    return pl.pallas_call(
        functools.partial(outer_kernel, tile, spots),
        in_specs=[pl.BlockSpec(memory_space=pltpu.SMEM)]
        + [pl.BlockSpec(memory_space=pl.ANY)] * len(arrays)
        + [vmem, vmem]
        + [pl.BlockSpec(memory_space=pl.ANY)] * len(after),
        out_specs=vmem,
        out_shape=shape(depth, cols),
        scratch_shapes=[
            pltpu.VMEM((depth, n * rows), BF),
            pltpu.VMEM((n * rows, cols), BF),
            pltpu.SemaphoreType.DMA((depth // tile, n)),
        ],
        compiler_params=PARAMS,
        cost_estimate=cost(1, 1),
    )(ids, *arrays, mine, other, *after)


def split_kernel(at_ref, part_ref, *refs):
    keep_ref, give_ref = refs[-2:]
    n, _, rows, _ = part_ref.shape
    for ref, which in ((keep_ref, at_ref[Z]), (give_ref, 1 - at_ref[Z])):
        ref[...] = sum(part_ref[i, which].astype(F32) for i in range(n)).astype(ref.dtype)


def split(ids, part, after=()):
    _, _, rows, cols = part.shape
    vmem = pl.BlockSpec(memory_space=pltpu.VMEM)
    return pl.pallas_call(
        split_kernel,
        in_specs=[pl.BlockSpec(memory_space=pltpu.SMEM), vmem]
        + [pl.BlockSpec(memory_space=pl.ANY)] * len(after),
        out_specs=(vmem, vmem),
        out_shape=(shape(rows, cols, dtype=F32), shape(rows, cols)),
        compiler_params=PARAMS,
        cost_estimate=cost(1, 1),
    )(ids, part, *after)


def merge_kernel(keep_ref, came_ref, att_ref, *refs):
    out_ref = refs[-1]
    total = (keep_ref[...] + came_ref[...].astype(F32)).astype(BF)
    cols = total.shape[1]
    for i in range(out_ref.shape[0]):
        out_ref[i, :, :cols] = total
        out_ref[i, :, cols:] = att_ref[i]


def merge(keep, came, att, after=()):
    rows, cols = keep.shape
    n, _, more = att.shape
    vmem = pl.BlockSpec(memory_space=pltpu.VMEM)
    return pl.pallas_call(
        merge_kernel,
        out_shape=shape(n, rows, cols + more),
        in_specs=[vmem] * 3 + [pl.BlockSpec(memory_space=pl.ANY)] * len(after),
        out_specs=vmem,
        compiler_params=PARAMS,
        cost_estimate=cost(1, 1),
    )(keep, came, att, *after)


def unpack_kernel(in_ref, w_ref, att_ref):
    for h in range(in_ref.shape[0]):
        span = slice(h * HS, (h + 1) * HS)
        for j in range(3):
            w_ref[j, :, span] = in_ref[h, :, j * HS : (j + 1) * HS].astype(F32)
        att_ref[:, span] = in_ref[h, :, 3 * HS :]


def unpack(last):
    heads, rows, more = last.shape
    tile = rows // 4
    return pl.pallas_call(
        unpack_kernel,
        grid=(rows // tile,),
        in_specs=[pl.BlockSpec((heads, tile, more), lambda i: (0, i, 0))],
        out_specs=(
            pl.BlockSpec((3, tile, heads * HS), lambda i: (0, i, 0)),
            pl.BlockSpec((tile, heads * HS), lambda i: (i, 0)),
        ),
        out_shape=(shape(3, rows, heads * HS, dtype=F32), shape(rows, heads * HS)),
        compiler_params=SMALL,
        cost_estimate=cost(1, 1),
    )(last)


def gate(arrays, after=(), pieces=()):
    n, m = len(arrays), len(arrays) + len(after)
    free = pl.BlockSpec(memory_space=pl.ANY)

    def kernel(*refs):
        outs, sems = refs[m + n : -1], refs[-1]
        copies = [
            pltpu.make_async_copy(refs[which].at[pl.ds(at, 1)], out, sems.at[i])
            for i, ((which, at), out) in enumerate(zip(pieces, outs))
        ]
        for copy in copies:
            copy.start()
        for copy in copies:
            copy.wait()

    return pl.pallas_call(
        kernel,
        in_specs=[free] * m,
        out_specs=(free,) * n + (pl.BlockSpec(memory_space=pltpu.VMEM),) * len(pieces),
        out_shape=tuple(shape(*a.shape) for a in arrays)
        + tuple(shape(1, *arrays[which].shape[1:]) for which, _ in pieces),
        scratch_shapes=[pltpu.SemaphoreType.DMA((max(len(pieces), 1),))],
        input_output_aliases={i: i for i in range(n)},
        compiler_params=PARAMS,
        cost_estimate=cost(1, 1),
    )(*arrays, *after)


def shift(x, axis, by):
    n = lax.axis_size(axis)
    return lax.ppermute(x, axis, [(i, (i + by) % n) for i in range(n)])


def per_device(tokens, weights, cotangent):
    _, rows, width = tokens.shape
    w_rows, _, cols = weights.shape
    heads = cols // HS
    n_x, n_y = (lax.axis_size(a) for a in ("x", "y"))
    ids = jnp.stack([lax.axis_index(a) for a in ("core", "x", "zh", "y", "zl")])
    tokens = tokens.reshape(rows, width)
    half = width // lax.axis_size("zh") // 2

    swap = lambda a: shift(a, "core", 1)
    own = weights.transpose(1, 0, 2)
    left, right, other = shift(own, "y", 1), shift(own, "y", -1), shift(own, "zl", 1)
    root, mine_t = unit_rows(ids, tokens, w_rows, ("root", "turned"))
    theirs, theirs_t = unit_rows(ids, swap(tokens), w_rows, ("mine", "turned"), (root,))
    mine, given = unit_rows(ids, tokens, w_rows, ("mine", "given"), (theirs,))
    left, right, other = gate((left, right, other), (mine,))

    left_0, right_0 = shift(mine_t, "x", 1), shift(mine_t, "x", -1)
    left_1, right_1 = shift(theirs_t, "x", 1), shift(theirs_t, "x", -1)

    near = ((0, 0), (3, 0), (1, 0), (0, 1))
    *sums, stack_0 = project(ids, mine, theirs, (own, left, right, other), near, after=(left_0, right_0))
    far, other_left, other_right, *pieces = gate(
        (shift(left, "y", 1), shift(left, "zl", 1), shift(other, "y", -1)),
        sums,
        ((0, 0), (1, 1), (2, 2)),
    )
    then = ((2, 0), (3, 1), (1, 1))
    keep, give, stack_1 = project(
        ids, mine, theirs, (far, other_left, other_right), then, sums, BF
    )
    *pieces, give = gate(
        (shift(pieces[0], "zl", 1), shift(pieces[1], "y", 1), shift(pieces[2], "y", -1), give)
    )
    pieces = (*pieces, *(swap(p) for p in pieces))
    proj, stack_0, stack_1 = project_last(
        ids, mine, given, keep, swap(give), cotangent.reshape(rows, cols), pieces, (2, 1), heads,
        (stack_0, stack_1), (left_1, right_1),
    )

    far_0, far_1 = shift(left_0, "x", 1), shift(right_1, "x", -1)
    blocks = (mine_t, theirs_t, left_0, left_1, right_0, right_1, far_0, far_1)
    spots = tuple((i, 0, by, i % 2) for i, by in enumerate((0, 0, 3, 3, 1, 1, 2, 2)))
    qkv = lax.all_to_all(proj, "x", 0, 0, tiled=True).reshape(n_x * rows, 4 * HS)
    att, head_grads = attention(qkv, (far_0, far_1))

    shards = (*pieces, stack_0, swap(stack_0), stack_1, swap(stack_1))
    places = {(2, 1): [[(3 * core + j, (0,)) for j in range(3)] for core in range(2)]}
    for first, keys in ((6, near), (8, then)):
        for i, key in enumerate(keys):
            places[key] = [[(first + core, (i, j)) for j in range(3)] for core in range(2)]
    places = [places[(by, z)] for by in range(n_y) for z in range(2)]

    head_grads = head_grads.reshape(n_x, rows, 3 * HS)
    grads = lax.all_to_all(head_grads, "x", 0, 0, tiled=True)
    part = outer(ids, blocks, spots, head_grads, swap(head_grads), (shards[7], shards[9]))

    up, down, stat = norm_halves(
        ids, grads, proj, shards, places,
        ((2, 0), (2, 1)),
        ((0, 0), (1, 0)),
        (half + 16, half),
        width,
    )
    up, down = shift(up, "zh", 1), shift(down, "zh", -1)
    up_part, down_part, up_direct, down_direct, _ = norm_halves(
        ids, grads, proj, shards, places,
        ((1, 0), (3, 1), (1, 1), (3, 0)),
        tuple((i, 0) for i in range(4)),
        (half,) * 4,
        width,
        (stat,),
    )
    part = lax.all_to_all(part, "y", 0, 0, tiled=True).reshape(n_y, 2, w_rows, 3 * HS)
    keep, give = split(ids, part, (up_part,))
    came = shift(give, "zl", 1)
    up_2, down_2 = add_messages(up_part, up, up_direct, down_part, down, down_direct, stat, came)
    own0, own1, _ = norm_halves(
        ids, grads, proj, shards, places, ((0, 0), (0, 1)), ((0, 0), (1, 0)), (half, half), width,
        (up_2,),
    )
    last = merge(keep, came, att.reshape(n_x, rows, HS), (own0,))
    up_2, down_2 = shift(up_2, "zh", 1), shift(down_2, "zh", -1)
    last = lax.all_to_all(last, "x", 0, 0, tiled=True)
    token_grad = finish(ids, (own0, own1, up_2, down_2), tokens, root, stat)
    weight_grad, attended = unpack(last)
    return attended[None], token_grad[None], weight_grad.transpose(1, 0, 2)


def solution(mesh):
    fine = Mesh(mesh.devices.reshape(4, 2, 2, 4, 4), ("y", "zl", "core", "x", "zh"))
    dp = ("y", "zl", "core")
    return jax.shard_map(
        per_device,
        mesh=fine,
        in_specs=(P(dp, "x", None), P(dp, None, "zh"), P(dp, "x", "zh")),
        out_specs=(P(dp, "x", "zh"), P(dp, "x", "zh"), P(dp, None, "zh")),
        check_vma=False,
    )
```

```python
import functools
import math

import jax
import jax.numpy as jnp
from jax import lax
from jax.experimental import pallas as pl
from jax.experimental.pallas import tpu as pltpu
from jax.sharding import Mesh
from jax.sharding import PartitionSpec as P

HS = 128
CORE, X, T, Y, Z = range(5)
BF = jnp.bfloat16
BUSY = 2 * 10**10
F32 = jnp.float32
PARAMS = pltpu.CompilerParams(vmem_limit_bytes=60 * 1024 * 1024)
SMALL = pltpu.CompilerParams(vmem_limit_bytes=24 * 1024 * 1024)


def dot(a, b, ca, cb):
    return lax.dot_general(a, b, (((ca,), (cb,)), ((), ())), preferred_element_type=F32)


def cost(flops, nbytes, exps=0):
    return pl.CostEstimate(flops=flops, bytes_accessed=nbytes, transcendentals=exps)


def shape(*dims, dtype=BF):
    return jax.ShapeDtypeStruct(dims, dtype)


def unit_kernel(at_ref, tok_ref, root_ref, *refs, band):
    tok = tok_ref[...].astype(F32)
    root = jnp.sqrt(jnp.mean(tok * tok, -1, keepdims=True) + 1e-05)
    root_ref[...] = root
    core = at_ref[CORE]
    mine_ref, mine_t_ref = refs[:2]
    for i in range(mine_ref.shape[1] // band):
        span = slice(i * band, (i + 1) * band)
        for ref, which in zip((mine_ref, *refs[2:]), (core, 1 - core)):
            at = pl.multiple_of((2 * i + which) * band, band)
            unit = (tok_ref[:, pl.ds(at, band)].astype(F32) / root).astype(BF)
            ref[:, span] = unit
            if ref is mine_ref:
                mine_t_ref[0, span, :] = unit.T


def unit_rows(ids, tokens, band, both):
    rows, width = tokens.shape
    tile = 128
    half = width // 2
    row = pl.BlockSpec((tile, half), lambda i, at: (i, 0))
    return pl.pallas_call(
        functools.partial(unit_kernel, band=band),
        grid_spec=pltpu.PrefetchScalarGridSpec(
            num_scalar_prefetch=1,
            grid=(rows // tile,),
            in_specs=[pl.BlockSpec((tile, width), lambda i, at: (i, 0))],
            out_specs=(pl.BlockSpec((tile, 1), lambda i, at: (i, 0)), row)
            + (pl.BlockSpec((1, half, tile), lambda i, at: (0, 0, i)),)
            + (row,) * both,
        ),
        out_shape=(shape(rows, 1, dtype=F32), shape(rows, half), shape(1, half, rows))
        + (shape(rows, half),) * both,
        compiler_params=PARAMS,
        cost_estimate=cost(BUSY, 1),
    )(ids, tokens)


def project_kernel(offsets, n_sums, at_ref, mine_ref, theirs_ref, *refs):
    keep_ref, give_ref, stack_ref, sems = refs[-4:]
    n = len(offsets)
    shards, sums = refs[:n], refs[n : n + n_sums]
    copies = [pltpu.make_async_copy(w, stack_ref.at[i], sems.at[i]) for i, w in enumerate(shards)]
    for copy in copies:
        copy.start()
    kinds, depth, cols = shards[0].shape
    bands = [
        pl.ds(pl.multiple_of(place_of(at_ref, *offset) * depth, depth), depth) for offset in offsets
    ]
    for i, (rows, out) in enumerate(((mine_ref, keep_ref), (theirs_ref, give_ref))):
        for j in range(kinds):
            span = slice(j * cols, (j + 1) * cols)
            total = sums[i][:, span] if n_sums else None
            for band, shard in zip(bands, shards):
                part = jnp.dot(rows[:, band], shard[j], preferred_element_type=F32)
                total = part if total is None else total + part
            out[:, span] = total.astype(out.dtype)
    for copy in copies:
        copy.wait()


def place_of(at_ref, y, z):
    return lax.rem(at_ref[Y] + y, 4) * 2 + lax.rem(at_ref[Z] + z, 2)


def project(ids, mine, theirs, shards, offsets, sums=(), give=F32, after=()):
    rows, _ = mine.shape
    n = len(shards)
    vmem = pl.BlockSpec(memory_space=pltpu.VMEM)
    cols = 3 * shards[0].shape[-1]
    return pl.pallas_call(
        functools.partial(project_kernel, offsets, len(sums)),
        in_specs=[pl.BlockSpec(memory_space=pltpu.SMEM)]
        + [vmem] * (2 + n + len(sums))
        + [pl.BlockSpec(memory_space=pl.ANY)] * len(after),
        out_specs=(vmem, vmem, pl.BlockSpec(memory_space=pl.ANY)),
        out_shape=(
            shape(rows, cols, dtype=F32),
            shape(rows, cols, dtype=give),
            shape(n, *shards[0].shape),
        ),
        scratch_shapes=[pltpu.SemaphoreType.DMA((n,))],
        compiler_params=PARAMS,
        cost_estimate=cost(1, 1),
    )(ids, mine, theirs, *shards, *sums, *after)


def project_last_kernel(offset, carried, at_ref, mine_ref, given_ref, keep_ref, came_ref, cot_ref, *refs):
    shards, heads_ref = refs[:6], refs[-1 - carried]
    depth, cols = shards[0].shape[-2:]
    band = pl.ds(pl.multiple_of(place_of(at_ref, *offset) * depth, depth), depth)
    heads = range(heads_ref.shape[0])
    for j in range(3):
        span = slice(j * cols, (j + 1) * cols)
        total = keep_ref[:, span] + came_ref[:, span].astype(F32)
        total += jnp.dot(mine_ref[:, band], shards[j][0], preferred_element_type=F32)
        total += jnp.dot(given_ref[:, band], shards[3 + j][0], preferred_element_type=F32)
        for h in heads:
            heads_ref[h, :, j * HS : (j + 1) * HS] = total[:, h * HS : (h + 1) * HS].astype(BF)
    for h in heads:
        heads_ref[h, :, 3 * HS :] = cot_ref[:, h * HS : (h + 1) * HS]


def project_last(ids, mine, given, keep, came, cotangent, pieces, offset, heads, carry, after):
    rows, cols = keep.shape
    n = len(carry)
    vmem = pl.BlockSpec(memory_space=pltpu.VMEM)
    free = pl.BlockSpec(memory_space=pl.ANY)
    return pl.pallas_call(
        functools.partial(project_last_kernel, offset, n),
        in_specs=[pl.BlockSpec(memory_space=pltpu.SMEM)]
        + [vmem] * (5 + len(pieces))
        + [free] * (n + len(after)),
        out_specs=(vmem,) + (free,) * n,
        out_shape=(shape(heads, rows, cols // heads + HS),) + tuple(shape(*c.shape) for c in carry),
        input_output_aliases={6 + len(pieces) + i: 1 + i for i in range(n)},
        compiler_params=PARAMS,
        cost_estimate=cost(1, 1),
    )(ids, mine, given, keep, came, cotangent, *pieces, *carry, *after)


def attention_kernel(q_rows, qkv_ref, *refs):
    att_ref, grad_ref, dk_ref, dv_ref = refs[-4:]
    scale = 1.0 / math.sqrt(HS)
    key = qkv_ref[:, HS : 2 * HS]
    value = qkv_ref[:, 2 * HS : 3 * HS]
    key_t = key.T
    value_t = value.T
    for i in range(qkv_ref.shape[0] // q_rows):
        rows = pl.ds(i * q_rows, q_rows)
        query = qkv_ref[rows, 0:HS]
        dout = qkv_ref[rows, 3 * HS :]
        scores = dot(key, query, 1, 1)
        to_log2 = scale * math.log2(math.e)
        top = jnp.max(scores, axis=0, keepdims=True) * to_log2
        expo = jnp.exp2(scores * to_log2 - top)
        prob = expo * (1.0 / jnp.sum(expo, axis=0, keepdims=True))
        prob_bf = prob.astype(BF)
        att = dot(value_t, prob_bf, 1, 0).T.astype(BF)
        att_ref[rows, :] = att
        row_dot = jnp.sum((dout.astype(F32) * att.astype(F32)).T, axis=0, keepdims=True)
        dprob = dot(value, dout, 1, 1)
        dscore = (prob * (dprob - row_dot)).astype(BF)
        grad_ref[rows, 0:HS] = (dot(key_t, dscore, 1, 0) * scale).T.astype(BF)
        dv = dot(prob_bf, dout, 1, 0)
        dk = dot(dscore, query, 1, 0)
        if i == 0:
            dv_ref[...] = dv
            dk_ref[...] = dk
        else:
            dv_ref[...] += dv
            dk_ref[...] += dk
    grad_ref[:, HS : 2 * HS] = (dk_ref[...] * scale).astype(BF)
    grad_ref[:, 2 * HS : 3 * HS] = dv_ref[...].astype(BF)


def attention(qkv, after):
    n = qkv.shape[0]
    vmem = pl.BlockSpec(memory_space=pltpu.VMEM)
    return pl.pallas_call(
        functools.partial(attention_kernel, n),
        out_shape=(shape(n, HS), shape(n, 3 * HS)),
        in_specs=[vmem] + [pl.BlockSpec(memory_space=pl.ANY)] * len(after),
        out_specs=(vmem,) * 2,
        scratch_shapes=[pltpu.VMEM((n, HS), F32), pltpu.VMEM((n, HS), F32)],
        compiler_params=PARAMS,
        cost_estimate=cost(BUSY, 1),
    )(qkv, *after)


def write_stat(ref, at, stat):
    ref[at:, :] = jnp.zeros((ref.shape[0] - at, ref.shape[1]), BF)
    rest = stat
    for i in range(3):
        top = rest.astype(BF)
        ref[at + i : at + i + 1, :] = top
        rest = rest - top.astype(F32)


def read_stat(ref, at):
    return sum(ref[at + i : at + i + 1, :].astype(F32) for i in range(3))


def norm_kernel(width, halves, spots, places, n_in, at_ref, g_ref, p_ref, *refs):
    shards = refs[:n_in]
    n_out = max(spot[0] for spot in spots) + 1
    outs, stat_ref = refs[-4 - n_out : -4], refs[-4]
    w_ref, flat_ref, sems = refs[-3:]
    _, kinds, depth, cols = w_ref.shape
    band = depth // 2
    quarters = len(places) // 2

    def copy(step, core, j, source):
        to = lax.rem(at_ref[CORE] + core, 2)
        at = pl.ds(pl.multiple_of(to * band, band), band)
        return pltpu.make_async_copy(source, w_ref.at[step, j, at], sems.at[step, core, j])

    for step, (by, half) in enumerate(halves):
        y_off = lax.rem(at_ref[T] + (by + quarters) - at_ref[Y], quarters)
        where = y_off * 2 + lax.rem(at_ref[Z] + half, 2)
        for place, cores in enumerate(places):

            @pl.when(where == place)
            def _(step=step, cores=cores):
                for core, pieces in enumerate(cores):
                    for j, (which, at) in enumerate(pieces):
                        copy(step, core, j, shards[which].at[*at]).start()

    heads, _, _ = g_ref.shape
    for h in range(heads):
        for j in range(kinds):
            at = (j * heads + h) * HS
            flat_ref[at : at + HS, :] = g_ref[h, :, j * HS : (j + 1) * HS].T
    total = sum(
        g_ref[h, :, j * HS : (j + 1) * HS].astype(F32)
        * p_ref[h, :, j * HS : (j + 1) * HS].astype(F32)
        for h in range(heads)
        for j in range(kinds)
    )
    stat = jnp.sum(total.T, axis=0, keepdims=True) * (1.0 / width)
    stat_ref[...] = stat
    for ref in outs:
        if ref.shape[0] % 128:
            write_stat(ref, ref.shape[0] - 16, stat)

    for step, (which, at) in enumerate(spots):
        for core in range(2):
            for j in range(kinds):
                copy(step, core, j, shards[0].at[0]).wait()
        total = sum(
            dot(w_ref[step, j], flat_ref[j * cols : (j + 1) * cols, :], 1, 0)
            for j in range(kinds)
        )
        outs[which][at : at + depth, :] = total.astype(BF)


def norm_halves(ids, grads, proj, shards, places, halves, spots, sizes, width, after=()):
    heads, rows, _ = grads.shape
    kinds = 3
    band, cols = shards[0].shape[-2:]
    n = len(spots)
    sizes = (*sizes, 1)
    vmem = pl.BlockSpec(memory_space=pltpu.VMEM)
    free = pl.BlockSpec(memory_space=pl.ANY)
    return pl.pallas_call(
        functools.partial(norm_kernel, width, halves, spots, places, len(shards)),
        in_specs=[pl.BlockSpec(memory_space=pltpu.SMEM), vmem, vmem]
        + [free] * (len(shards) + len(after)),
        out_specs=(vmem,) * len(sizes),
        out_shape=tuple(shape(s, rows) for s in sizes[:-1]) + (shape(1, rows, dtype=F32),),
        scratch_shapes=[
            pltpu.VMEM((n, kinds, 2 * band, cols), BF),
            pltpu.VMEM((kinds * cols, rows), BF),
            pltpu.SemaphoreType.DMA((n, 2, kinds)),
        ],
        compiler_params=PARAMS,
        cost_estimate=cost(1, 1),
    )(ids, grads, proj, *shards, *after)


def add_kernel(up_part, up_in, stat_in, up_direct, down_part, down_in, down_direct, stat_ref, *refs):
    up_out, down_out = refs[-2:]
    half = up_part.shape[0]
    for part, came, direct, out in (
        (up_part, up_in, up_direct, up_out),
        (down_part, down_in, down_direct, down_out),
    ):
        out[:half, :] = (part[...].astype(F32) + came[...].astype(F32)).astype(BF)
        out[half : 2 * half, :] = direct[...]
    write_stat(up_out, 2 * half, stat_ref[...] + read_stat(stat_in, 0))
    write_stat(down_out, 2 * half, stat_ref[...])


def add_messages(up_part, up_in, up_direct, down_part, down_in, down_direct, stat, after):
    half, rows = up_part.shape
    block = pl.BlockSpec((half, rows), lambda i: (0, 0))
    out = pl.BlockSpec((2 * half + 16, rows), lambda i: (0, 0))
    end = pl.BlockSpec((16, rows), lambda i: (half // 16, 0))
    return pl.pallas_call(
        add_kernel,
        grid=(1,),
        out_shape=(shape(2 * half + 16, rows),) * 2,
        in_specs=[block, block, end]
        + [block] * 4
        + [pl.BlockSpec((1, rows), lambda i: (0, 0)), pl.BlockSpec(memory_space=pl.ANY)],
        out_specs=(out, out),
        compiler_params=PARAMS,
        cost_estimate=cost(1, 1),
    )(up_part, up_in, up_in, up_direct, down_part, down_in, down_direct, stat, after)


def finish_kernel(at_ref, own0, own1, up, down, tok_ref, root_ref, stat_ref, *refs):
    out_ref = refs[-1]
    half = own0.shape[0]
    stat = stat_ref[...] + read_stat(up, 2 * half) + read_stat(down, 2 * half)
    stat = jnp.broadcast_to(stat, (HS, stat.shape[1])).T[:, 0:1]
    root = root_ref[...]
    parts = (
        (own0[...], up[:half, :], down[half : 2 * half, :]),
        (own1[...], up[half : 2 * half, :], down[:half, :]),
    )
    for i, part in enumerate(parts):
        span = slice(i * half, (i + 1) * half)
        total = sum(p.astype(F32) for p in part)
        unit = tok_ref[:, span].astype(F32) / root
        out_ref[:, span] = ((total.T - unit * stat) / root).astype(BF)


def finish(ids, parts, tokens, root, stat, after=()):
    half, rows = parts[0].shape
    share = 2 * half
    tile = HS
    some = lambda a: pl.BlockSpec((a.shape[0], tile), lambda i, at: (0, i))
    return pl.pallas_call(
        finish_kernel,
        grid_spec=pltpu.PrefetchScalarGridSpec(
            num_scalar_prefetch=1,
            grid=(rows // tile,),
            in_specs=[some(p) for p in parts]
            + [pl.BlockSpec((tile, share), lambda i, at: (i, at[T]))]
            + [pl.BlockSpec((tile, 1), lambda i, at: (i, 0)), some(stat)]
            + [pl.BlockSpec(memory_space=pl.ANY)] * len(after),
            out_specs=pl.BlockSpec((tile, share), lambda i, at: (i, 0)),
        ),
        out_shape=shape(rows, share),
        compiler_params=PARAMS,
        cost_estimate=cost(BUSY, 1),
    )(ids, *parts, tokens, root, stat, *after)


def outer_kernel(tile, spots, at_ref, *refs):
    out_ref, a_ref, g_ref, sems = refs[-4:]
    m = max(spot[0] for spot in spots) + 1
    arrays, (mine_ref, other_ref) = refs[:m], refs[m : m + 2]
    n, rows, _ = mine_ref.shape
    depth = a_ref.shape[0]
    copies = []
    for step in range(depth // tile):
        span = pl.ds(step * tile, tile)
        some = []
        for i, (which, at, _, _) in enumerate(spots):
            to = a_ref.at[span, pl.ds(i * rows, rows)]
            some.append(pltpu.make_async_copy(arrays[which].at[at, span], to, sems.at[step, i]))
            some[-1].start()
        copies.append(some)
    for i, (_, _, by, frame) in enumerate(spots):
        ref = other_ref if frame else mine_ref
        g_ref[i * rows : (i + 1) * rows, :] = ref[lax.rem(at_ref[X] + by, n)]
    for step, some in enumerate(copies):
        for copy in some:
            copy.wait()
        span = slice(step * tile, (step + 1) * tile)
        out_ref[span, :] = jnp.dot(
            a_ref[span, :], g_ref[...], preferred_element_type=F32
        ).astype(BF)


def outer(ids, arrays, spots, mine, other, after):
    _, depth, rows = arrays[0].shape
    cols = mine.shape[2]
    n = len(spots)
    tile = 512
    vmem = pl.BlockSpec(memory_space=pltpu.VMEM)
    return pl.pallas_call(
        functools.partial(outer_kernel, tile, spots),
        in_specs=[pl.BlockSpec(memory_space=pltpu.SMEM)]
        + [pl.BlockSpec(memory_space=pl.ANY)] * len(arrays)
        + [vmem, vmem]
        + [pl.BlockSpec(memory_space=pl.ANY)] * len(after),
        out_specs=vmem,
        out_shape=shape(depth, cols),
        scratch_shapes=[
            pltpu.VMEM((depth, n * rows), BF),
            pltpu.VMEM((n * rows, cols), BF),
            pltpu.SemaphoreType.DMA((depth // tile, n)),
        ],
        compiler_params=PARAMS,
        cost_estimate=cost(1, 1),
    )(ids, *arrays, mine, other, *after)


def split_kernel(at_ref, part_ref, *refs):
    keep_ref, give_ref = refs[-2:]
    n, _, rows, _ = part_ref.shape
    for ref, which in ((keep_ref, at_ref[Z]), (give_ref, 1 - at_ref[Z])):
        ref[...] = sum(part_ref[i, which].astype(F32) for i in range(n)).astype(ref.dtype)


def split(ids, part, after=()):
    _, _, rows, cols = part.shape
    vmem = pl.BlockSpec(memory_space=pltpu.VMEM)
    return pl.pallas_call(
        split_kernel,
        in_specs=[pl.BlockSpec(memory_space=pltpu.SMEM), vmem]
        + [pl.BlockSpec(memory_space=pl.ANY)] * len(after),
        out_specs=(vmem, vmem),
        out_shape=(shape(rows, cols, dtype=F32), shape(rows, cols)),
        compiler_params=PARAMS,
        cost_estimate=cost(1, 1),
    )(ids, part, *after)


def merge_kernel(keep_ref, came_ref, att_ref, *refs):
    out_ref = refs[-1]
    total = (keep_ref[...] + came_ref[...].astype(F32)).astype(BF)
    cols = total.shape[1]
    for i in range(out_ref.shape[0]):
        out_ref[i, :, :cols] = total
        out_ref[i, :, cols:] = att_ref[i]


def merge(keep, came, att, after=()):
    rows, cols = keep.shape
    n, _, more = att.shape
    vmem = pl.BlockSpec(memory_space=pltpu.VMEM)
    return pl.pallas_call(
        merge_kernel,
        out_shape=shape(n, rows, cols + more),
        in_specs=[vmem] * 3 + [pl.BlockSpec(memory_space=pl.ANY)] * len(after),
        out_specs=vmem,
        compiler_params=PARAMS,
        cost_estimate=cost(1, 1),
    )(keep, came, att, *after)


def unpack_kernel(in_ref, w_ref, att_ref):
    for h in range(in_ref.shape[0]):
        span = slice(h * HS, (h + 1) * HS)
        for j in range(3):
            w_ref[j, :, span] = in_ref[h, :, j * HS : (j + 1) * HS].astype(F32)
        att_ref[:, span] = in_ref[h, :, 3 * HS :]


def unpack(last):
    heads, rows, more = last.shape
    tile = rows // 4
    return pl.pallas_call(
        unpack_kernel,
        grid=(rows // tile,),
        in_specs=[pl.BlockSpec((heads, tile, more), lambda i: (0, i, 0))],
        out_specs=(
            pl.BlockSpec((3, tile, heads * HS), lambda i: (0, i, 0)),
            pl.BlockSpec((tile, heads * HS), lambda i: (i, 0)),
        ),
        out_shape=(shape(3, rows, heads * HS, dtype=F32), shape(rows, heads * HS)),
        compiler_params=SMALL,
        cost_estimate=cost(1, 1),
    )(last)


def gate(arrays, after=(), pieces=()):
    n, m = len(arrays), len(arrays) + len(after)
    free = pl.BlockSpec(memory_space=pl.ANY)

    def kernel(*refs):
        outs, sems = refs[m + n : -1], refs[-1]
        copies = [
            pltpu.make_async_copy(refs[which].at[pl.ds(at, 1)], out, sems.at[i])
            for i, ((which, at), out) in enumerate(zip(pieces, outs))
        ]
        for copy in copies:
            copy.start()
        for copy in copies:
            copy.wait()

    return pl.pallas_call(
        kernel,
        in_specs=[free] * m,
        out_specs=(free,) * n + (pl.BlockSpec(memory_space=pltpu.VMEM),) * len(pieces),
        out_shape=tuple(shape(*a.shape) for a in arrays)
        + tuple(shape(1, *arrays[which].shape[1:]) for which, _ in pieces),
        scratch_shapes=[pltpu.SemaphoreType.DMA((max(len(pieces), 1),))],
        input_output_aliases={i: i for i in range(n)},
        compiler_params=PARAMS,
        cost_estimate=cost(1, 1),
    )(*arrays, *after)


def shift(x, axis, by):
    n = lax.axis_size(axis)
    return lax.ppermute(x, axis, [(i, (i + by) % n) for i in range(n)])


def per_device(tokens, weights, cotangent):
    _, rows, width = tokens.shape
    w_rows, _, cols = weights.shape
    heads = cols // HS
    n_x, n_y = (lax.axis_size(a) for a in ("x", "y"))
    ids = jnp.stack([lax.axis_index(a) for a in ("core", "x", "zh", "y", "zl")])
    tokens = tokens.reshape(rows, width)
    half = width // lax.axis_size("zh") // 2

    swap = lambda a: shift(a, "core", 1)
    own = weights.transpose(1, 0, 2)
    left, right, other = shift(own, "y", 1), shift(own, "y", -1), shift(own, "zl", 1)
    root, mine, mine_t, given = unit_rows(ids, tokens, w_rows, True)
    _, theirs, theirs_t = unit_rows(ids, swap(tokens), w_rows, False)
    left, right, other = gate((left, right, other), (theirs,))

    left_0, right_0 = shift(mine_t, "x", 1), shift(mine_t, "x", -1)
    left_1, right_1 = shift(theirs_t, "x", 1), shift(theirs_t, "x", -1)

    near = ((0, 0), (3, 0), (1, 0), (0, 1))
    *sums, stack_0 = project(ids, mine, theirs, (own, left, right, other), near, after=(left_0, right_0))
    far, other_left, other_right, *pieces = gate(
        (shift(left, "y", 1), shift(left, "zl", 1), shift(other, "y", -1)),
        sums,
        ((0, 0), (1, 1), (2, 2)),
    )
    then = ((2, 0), (3, 1), (1, 1))
    keep, give, stack_1 = project(
        ids, mine, theirs, (far, other_left, other_right), then, sums, BF
    )
    *pieces, give = gate(
        (shift(pieces[0], "zl", 1), shift(pieces[1], "y", 1), shift(pieces[2], "y", -1), give)
    )
    pieces = (*pieces, *(swap(p) for p in pieces))
    proj, stack_0, stack_1 = project_last(
        ids, mine, given, keep, swap(give), cotangent.reshape(rows, cols), pieces, (2, 1), heads,
        (stack_0, stack_1), (left_1, right_1),
    )

    far_0, far_1 = shift(left_0, "x", 1), shift(right_1, "x", -1)
    blocks = (mine_t, theirs_t, left_0, left_1, right_0, right_1, far_0, far_1)
    spots = tuple((i, 0, by, i % 2) for i, by in enumerate((0, 0, 3, 3, 1, 1, 2, 2)))
    qkv = lax.all_to_all(proj, "x", 0, 0, tiled=True).reshape(n_x * rows, 4 * HS)
    att, head_grads = attention(qkv, (far_0, far_1))

    shards = (*pieces, stack_0, swap(stack_0), stack_1, swap(stack_1))
    places = {(2, 1): [[(3 * core + j, (0,)) for j in range(3)] for core in range(2)]}
    for first, keys in ((6, near), (8, then)):
        for i, key in enumerate(keys):
            places[key] = [[(first + core, (i, j)) for j in range(3)] for core in range(2)]
    places = [places[(by, z)] for by in range(n_y) for z in range(2)]

    head_grads = head_grads.reshape(n_x, rows, 3 * HS)
    grads = lax.all_to_all(head_grads, "x", 0, 0, tiled=True)
    part = outer(ids, blocks, spots, head_grads, swap(head_grads), (shards[7], shards[9]))

    up, down, stat = norm_halves(
        ids, grads, proj, shards, places,
        ((2, 0), (2, 1)),
        ((0, 0), (1, 0)),
        (half + 16, half),
        width,
    )
    up, down = shift(up, "zh", 1), shift(down, "zh", -1)
    up_part, down_part, up_direct, down_direct, _ = norm_halves(
        ids, grads, proj, shards, places,
        ((1, 0), (3, 1), (1, 1), (3, 0)),
        tuple((i, 0) for i in range(4)),
        (half,) * 4,
        width,
        (stat,),
    )
    part = lax.all_to_all(part, "y", 0, 0, tiled=True).reshape(n_y, 2, w_rows, 3 * HS)
    keep, give = split(ids, part, (up_part,))
    came = shift(give, "zl", 1)
    up_2, down_2 = add_messages(up_part, up, up_direct, down_part, down, down_direct, stat, came)
    own0, own1, _ = norm_halves(
        ids, grads, proj, shards, places, ((0, 0), (0, 1)), ((0, 0), (1, 0)), (half, half), width,
        (up_2,),
    )
    last = merge(keep, came, att.reshape(n_x, rows, HS), (own0,))
    up_2, down_2 = shift(up_2, "zh", 1), shift(down_2, "zh", -1)
    last = lax.all_to_all(last, "x", 0, 0, tiled=True)
    token_grad = finish(ids, (own0, own1, up_2, down_2), tokens, root, stat)
    weight_grad, attended = unpack(last)
    return attended[None], token_grad[None], weight_grad.transpose(1, 0, 2)


def solution(mesh):
    fine = Mesh(mesh.devices.reshape(4, 2, 2, 4, 4), ("y", "zl", "core", "x", "zh"))
    dp = ("y", "zl", "core")
    return jax.shard_map(
        per_device,
        mesh=fine,
        in_specs=(P(dp, "x", None), P(dp, None, "zh"), P(dp, "x", "zh")),
        out_specs=(P(dp, "x", "zh"), P(dp, "x", "zh"), P(dp, None, "zh")),
        check_vma=False,
    )
```
